32 devices in a mesh: row: 8 (over z, y), col: 4 (over x, core).
Axes of the slice: x: 2, y: 2, z: 4, core: 2. Of those that a mesh axis runs over, the one named last changes fastest.
Arguments:
- adjoint_source: float32 [96, 64, 2, 128], P('row', 'col'), may hold values from -6 to 6
- saved_currents: float32 [96, 64, 2, 128], P('row', 'col'), may hold values from -6 to 6
- lag_blocks: float32 [7, 7, 2, 128, 128], replicated, may hold values from -0.01875 to 0.01875
- element_inverse: float32 [2, 128, 128], replicated, may hold values from -0.088388348 to 1.0883883
Outputs:
- adjoint: float32 [96, 64, 2, 128], P('row', 'col')
- lag_grad: float32 [7, 7, 2, 128, 128], P(None, None, None, 'row')
The draws below stay inside these ranges and needn't reach their ends.
All inputs are finite; a program needn't handle non-finite values.
Results may differ from the reference program's by a relative error of at most 0.0001.
Values sent between devices are 32-bit elements; how exact they have to be, the bound alone decides.
No kernel may reach another device: no remote copies, remote signals or barrier semaphores. Data moves between devices by JAX's collectives and lax.ppermute only.
A program may use at most 128 MiB of HBM per device.

```python
import math
import jax
import jax.numpy as jnp
from jax import lax

M = 128
REACH = 3
SPAN = 7
SWEEPS = 2
NR = 96
NC = 64


def draw_element_inverse(key, part):
    noise_key = jax.random.fold_in(key, 17)
    noise = jnp.clip(jax.random.normal(noise_key, (2, M, M), jnp.float32), -5.0, 5.0)
    noise = noise * (0.2 / math.sqrt(M))
    identity = jnp.eye(M, dtype=jnp.float32)
    return noise + jnp.stack((identity, jnp.zeros_like(identity)))


def steps_of(own_key, extent, split, smallest, high):
    def one(axis_at, parts):
        draws = jax.random.uniform(jax.random.fold_in(jax.random.fold_in(own_key, 6), axis_at), (parts,), jnp.float32, smallest / len(split), high / len(split))
        return jnp.repeat(jnp.exp(draws), extent[axis_at] // parts).reshape((-1,) + (1,) * (len(extent) - axis_at - 1))

    gain = one(*split[0])
    for cut in split[1:]:
        gain = gain * one(*cut)
    return gain


def gaussian(rng, shape, width, most, split=(), kind=jnp.bfloat16):
    entries = width * jax.random.normal(rng, shape, jnp.float32)
    if split:
        entries = entries * steps_of(rng, shape, split, -0.22, 0.18)
    return jnp.clip(entries, -most, most).astype(kind)


def setup_inputs(seed: int = 0) -> dict:
    arg_keys = jax.random.split(jax.random.key(seed), 5)
    adjoint_source = gaussian(arg_keys[0], (NR, NC, 2, M), 1.0, 6.0, ((0, 8), (1, 4)), jnp.float32)
    saved_currents = gaussian(arg_keys[1], (NR, NC, 2, M), 1.0, 6.0, ((0, 8), (1, 4)), jnp.float32)
    lag_blocks = gaussian(arg_keys[2], (SPAN, SPAN, 2, M, M), (0.35 * (98 * M) ** -0.5), 0.01875, (), jnp.float32)
    element_inverse = draw_element_inverse(jax.random.fold_in(arg_keys[4], 71), 0)
    return {"adjoint_source": adjoint_source, "saved_currents": saved_currents, "lag_blocks": lag_blocks, "element_inverse": element_inverse}


precise = lax.Precision.HIGHEST

def combine_parts(product):
    real = product[..., 0, 0, :] + product[..., 1, 1, :]
    imag = product[..., 1, 0, :] - product[..., 0, 1, :]
    return jnp.stack((real, imag), axis=-2)

def conj_apply(field, blocks):
    product = jnp.einsum('ijkm,cmq->ijkcq', field, blocks, precision=precise)
    return combine_parts(product)

def lag_apply(padded, lag_blocks, rows, cols):
    span = lag_blocks.shape[0]
    accum = None
    for offset_row in range(span):
        stacked = jnp.stack([padded[offset_row:offset_row + rows, offset_col:offset_col + cols] for offset_col in range(span)])
        product = jnp.einsum('bijkm,bcmq->ijkcq', stacked, lag_blocks[offset_row], precision=precise)
        accum = product if accum is None else accum + product
    return combine_parts(accum)

def correlate(adjoint, current_pad, span, rows, cols):
    layers = []
    for offset_row in range(span):
        first = span - 1 - offset_row
        stacked = jnp.stack([current_pad[first:first + rows, span - 1 - offset_col:span - 1 - offset_col + cols] for offset_col in range(span)])
        product = jnp.einsum('ijkm,bijhq->bkmhq', adjoint, stacked, precision=precise)
        real = product[:, 0, :, 0] + product[:, 1, :, 1]
        imag = product[:, 1, :, 0] - product[:, 0, :, 1]
        layers.append(jnp.stack((real, imag), axis=1))
    return jnp.stack(layers)

def reference(adjoint_source, saved_currents, lag_blocks, element_inverse):
    widths = ((REACH, REACH), (REACH, REACH), (0, 0), (0, 0))
    adjoint = conj_apply(adjoint_source, element_inverse)
    for sweep in range(SWEEPS):
        padded = jnp.pad(adjoint, widths)
        image = adjoint + lag_apply(padded, lag_blocks, NR, NC)
        adjoint = adjoint + conj_apply(adjoint_source - image, element_inverse)
    current_pad = jnp.pad(saved_currents, widths)
    factor = -1.0 / math.sqrt(NR * NC)
    lag_grad = correlate(adjoint, current_pad, SPAN, NR, NC) * factor
    return (adjoint, lag_grad)
```

```python
import math

import jax
import jax.numpy as jnp
from jax import lax
from jax.sharding import PartitionSpec as P

SWEEPS = 2

precise = lax.Precision.HIGH


def pairing(peers, first):
    pairs = []
    for low in range(first, peers - 1, 2):
        pairs += [(low, low + 1), (low + 1, low)]
    return pairs


def swap(value, axis, first):
    pairs = pairing(lax.axis_size(axis), first)
    if not pairs:
        return jnp.zeros_like(value)
    return lax.ppermute(value, axis, pairs)


def edges(value, axis, dim, width):
    length = value.shape[dim]
    even = lax.axis_index(axis) % 2 == 0
    last = lax.slice_in_dim(value, length - width, length, axis=dim)
    initial = lax.slice_in_dim(value, 0, width, axis=dim)
    inner = swap(jnp.where(even, last, initial), axis, 0)
    outer = swap(jnp.where(even, initial, last), axis, 1)
    return jnp.where(even, outer, inner), jnp.where(even, inner, outer)


def extended(value, sides, width):
    for axis, dim in sides:
        before, after = edges(value, axis, dim, width)
        value = jnp.concatenate([before, value, after], axis=dim)
    return value


def combine_parts(product):
    real = product[..., 0, 0, :] + product[..., 1, 1, :]
    imag = product[..., 1, 0, :] - product[..., 0, 1, :]
    return jnp.stack((real, imag), axis=-2)


def conj_apply(field, blocks):
    product = jnp.einsum("ijkm,cmq->ijkcq", field, blocks, precision=precise)
    return combine_parts(product)


def lag_apply(padded, lag_blocks, rows, cols):
    span = lag_blocks.shape[0]
    accum = None
    for offset_row in range(span):
        stacked = jnp.stack(
            [
                padded[offset_row : offset_row + rows, offset_col : offset_col + cols]
                for offset_col in range(span)
            ]
        )
        product = jnp.einsum(
            "bijkm,bcmq->ijkcq", stacked, lag_blocks[offset_row], precision=precise
        )
        accum = product if accum is None else accum + product
    return combine_parts(accum)


def inside(rows, cols, margin, tile_rows, tile_cols):
    def one(axis, count, tile):
        at = lax.axis_index(axis) * tile - margin + jnp.arange(count)
        return (at >= 0) & (at < tile * lax.axis_size(axis))

    mask = one("row", rows, tile_rows)[:, None] & one("col", cols, tile_cols)[None, :]
    return mask[:, :, None, None]


def trim(value, margin):
    if margin == 0:
        return value
    return value[margin:-margin, margin:-margin]


def exchange_shares(field):
    peers = lax.axis_size("row")
    me = lax.axis_index("row")
    rows, cols, parts, width = field.shape
    share = width // peers
    pieces = jnp.moveaxis(field.reshape(rows, cols, parts, peers, share), 3, 0)
    out = jnp.zeros((peers, rows, cols, parts, share), field.dtype)
    for k in range(peers):
        piece = lax.dynamic_index_in_dim(pieces, (me + k) % peers, 0, keepdims=False)
        if k:
            piece = lax.ppermute(piece, "row", [(i, (i + k) % peers) for i in range(peers)])
        out = lax.dynamic_update_index_in_dim(out, piece, (me - k) % peers, 0)
    return out.reshape(peers * rows, cols, parts, share)


def core_join(value, dim):
    other = swap(value, "col", 0)
    even = lax.axis_index("col") % 2 == 0
    return jnp.concatenate(
        [jnp.where(even, value, other), jnp.where(even, other, value)], axis=dim
    )


def gather_currents(currents, reach):
    rows, cols, parts, width = currents.shape
    half = width // 2
    even = lax.axis_index("col") % 2 == 0
    last = currents[:, cols - reach :]
    initial = currents[:, :reach]
    outer = swap(jnp.where(even, initial, last), "col", 1)
    widened = jnp.where(
        even,
        jnp.concatenate([outer, currents], axis=1),
        jnp.concatenate([currents, outer], axis=1),
    )
    low, high = widened[..., :half], widened[..., half:]
    mine = jnp.where(even, low, high)
    other = swap(jnp.where(even, high, low), "col", 0)
    strip = jnp.concatenate(
        [jnp.where(even, mine, other), jnp.where(even, other, mine)], axis=1
    )
    peers = lax.axis_size("row")
    me = lax.axis_index("row")
    out = jnp.zeros((peers,) + strip.shape, strip.dtype)
    for k in range(peers // 2):
        shift = 2 * k
        piece = strip
        if k:
            piece = lax.ppermute(strip, "row", [(i, (i + shift) % peers) for i in range(peers)])
        twin = swap(piece, "row", 0)
        place = (me - shift) % peers
        out = lax.dynamic_update_index_in_dim(out, piece, place, 0)
        out = lax.dynamic_update_index_in_dim(out, twin, place ^ 1, 0)
    return out.reshape((peers * rows,) + strip.shape[1:])


def correlate(adjoint, currents, span):
    reach = span // 2
    rows, cols = adjoint.shape[:2]
    padded = jnp.pad(adjoint, ((reach, reach), (0, 0), (0, 0), (0, 0)))
    left = jnp.stack([padded[a : a + rows] for a in range(span)], axis=2)
    right = jnp.stack(
        [currents[:, span - 1 - b : span - 1 - b + cols] for b in range(span)], axis=2
    )
    product = jnp.einsum("ijakm,ijbhq->abkhmq", left, right, precision=precise)
    real = product[:, :, 0, 0] + product[:, :, 1, 1]
    imag = product[:, :, 1, 0] - product[:, :, 0, 1]
    return jnp.stack((real, imag), axis=2)


def on_device(adjoint_source, saved_currents, lag_blocks, element_inverse):
    rows, cols = adjoint_source.shape[:2]
    span = lag_blocks.shape[0]
    reach = span // 2
    source = extended(adjoint_source, (("row", 0), ("col", 1)), reach * SWEEPS)
    currents = gather_currents(saved_currents, reach)
    adjoint = conj_apply(source, element_inverse)
    for sweep in range(SWEEPS):
        margin = reach * (SWEEPS - 1 - sweep)
        source = trim(source, reach)
        tall, wide = source.shape[:2]
        centre = trim(adjoint, reach)
        image = centre + lag_apply(adjoint, lag_blocks, tall, wide)
        adjoint = centre + conj_apply(source - image, element_inverse)
        if margin:
            adjoint = jnp.where(inside(tall, wide, margin, rows, cols), adjoint, 0.0)
    elements = rows * lax.axis_size("row") * cols * lax.axis_size("col")
    factor = -1.0 / math.sqrt(elements)
    shares = core_join(exchange_shares(adjoint), 1)
    partial_terms = correlate(shares, currents, span) * factor
    groups = lax.axis_size("col") // 2
    total = partial_terms
    for k in range(1, groups):
        peers = lax.axis_size("col")
        total = total + lax.ppermute(
            partial_terms, "col", [(i, (i + 2 * k) % peers) for i in range(peers)]
        )
    lag_grad = core_join(total, 4)
    return (adjoint, lag_grad)


def solution(mesh):
    return jax.shard_map(
        on_device,
        mesh=mesh,
        in_specs=(P("row", "col", None, None), P("row", "col", None, None), P(), P()),
        out_specs=(P("row", "col", None, None), P(None, None, None, "row", None)),
        check_vma=False,
    )
```

```python
import functools
import math

import jax
import jax.numpy as jnp
from jax import lax
from jax.experimental import pallas as pl
from jax.experimental.pallas import tpu as pltpu
from jax.sharding import PartitionSpec as P

SWEEPS = 2
VMEM_LIMIT = 56 * 1024 * 1024

f32 = jnp.float32
bf16 = jnp.bfloat16


def split(value):
    high = value.astype(bf16)
    return high, (value - high.astype(f32)).astype(bf16)


def dot(left, right):
    return jnp.dot(left, right, preferred_element_type=f32)


def dot3(left, right):
    (left_high, left_low), (right_high, right_low) = left, right
    return dot(left_high, right_high) + dot(left_low, right_high) + dot(left_high, right_low)


def round_up(count, unit):
    return (count + unit - 1) // unit * unit


def store_block(ref, index, real, imag):
    width = real.shape[0]
    low, high = slice(0, width), slice(width, 2 * width)
    ref[index + (low, low)] = real
    ref[index + (low, high)] = -imag
    ref[index + (high, low)] = imag
    ref[index + (high, high)] = real


def weights_kernel(blocks_ref, high_ref, low_ref):
    span, _, width, _ = blocks_ref.shape[1:]
    for b in range(span):
        real_high, real_low = split(blocks_ref[0, b, 0])
        imag_high, imag_low = split(blocks_ref[0, b, 1])
        store_block(high_ref, (0, b), real_high, imag_high)
        store_block(low_ref, (0, b), real_low, imag_low)


def prepare_weights(lag_blocks):
    span, _, parts, width, _ = lag_blocks.shape
    shape = jax.ShapeDtypeStruct((span, span, parts * width, parts * width), bf16)
    spec = pl.BlockSpec((1,) + shape.shape[1:], lambda a: (a, 0, 0, 0))
    size = lag_blocks.size * 4
    return pl.pallas_call(
        weights_kernel,
        grid=(span,),
        in_specs=[pl.BlockSpec((1,) + lag_blocks.shape[1:], lambda a: (a, 0, 0, 0, 0))],
        out_specs=[spec, spec],
        out_shape=[shape, shape],
        cost_estimate=pl.CostEstimate(flops=0, bytes_accessed=3 * size, transcendentals=0),
        compiler_params=pltpu.CompilerParams(vmem_limit_bytes=VMEM_LIMIT),
        name="weights",
    )(lag_blocks)


def inside(rows, cols, pitch, margin, tile_rows, tile_cols):
    at = lax.broadcasted_iota(jnp.int32, (rows * pitch, 1), 0)
    i = at // pitch
    j = at - i * pitch
    row = i + (lax.axis_index("row") * tile_rows - margin)
    col = j + (lax.axis_index("col") * tile_cols - margin)
    row_ok = (row >= 0) & (row < tile_rows * lax.axis_size("row"))
    col_ok = (col >= 0) & (col < tile_cols * lax.axis_size("col"))
    return row_ok & col_ok & (j < cols)


def sweeps_kernel(
    sizes,
    source_ref,
    inverse_ref,
    high_hbm,
    low_hbm,
    adjoint_ref,
    *rest,
):
    rows, cols, span, peers, pitch, wide = sizes
    sends = rest[:peers]
    (first, second, x1_high, x1_low, x2_high, x2_low, acc, turned, w_high, w_low, e_high, e_low, sems) = rest[peers:]
    reach = span // 2
    mid_rows, mid_cols = rows + 2 * reach, cols + 2 * reach
    full_rows = rows + 4 * reach
    lanes = source_ref.shape[-1]
    width = lanes // 2

    def weight_copies(a):
        return (
            pltpu.make_async_copy(high_hbm.at[a], w_high.at[a], sems.at[0, a]),
            pltpu.make_async_copy(low_hbm.at[a], w_low.at[a], sems.at[1, a]),
        )

    for a in range(span):
        for copy in weight_copies(a):
            copy.start()

    real_high, real_low = split(inverse_ref[0])
    imag_high, imag_low = split(inverse_ref[1])
    store_block(e_high, (), real_high, imag_high)
    store_block(e_low, (), real_low, imag_low)

    def invert(value):
        return dot3(split(value), (e_high[...], e_low[...]))

    step_rows = 4

    @pl.loop(0, full_rows // step_rows)
    def _(s):
        at = pl.ds(s * step_rows, step_rows)
        piece = source_ref[at].reshape(step_rows * wide, lanes)
        first[at] = invert(piece).reshape(step_rows, wide, lanes)

    first[full_rows] = jnp.zeros((wide, lanes), f32)

    @pl.loop(0, full_rows // 2)
    def _(s):
        for odd in range(2):
            for b in range(span):
                value = first[pl.ds(2 * s + odd, 2), pl.ds(b, pitch), :]
                high, low = split(value.reshape(2 * pitch, lanes))
                to = pl.ds(pl.multiple_of(s * 2 * pitch, 2 * pitch), 2 * pitch)
                x1_high[odd, to, b * lanes : (b + 1) * lanes] = high
                x1_low[odd, to, b * lanes : (b + 1) * lanes] = low

    acc[...] = jnp.zeros_like(acc)

    @pl.loop(0, span)
    def _(a):
        for copy in weight_copies(a):
            copy.wait()
        odd = a % 2
        at = pl.ds(pl.multiple_of((a // 2) * 2 * pitch, 2 * pitch), mid_rows * pitch)
        high = x1_high[odd, at, :]
        low = x1_low[odd, at, :]
        weight_high = w_high[a].reshape(span * lanes, lanes)
        weight_low = w_low[a].reshape(span * lanes, lanes)
        acc[...] += dot(high, weight_high) + dot(low, weight_high) + dot(high, weight_low)

    step_rows = 3

    mask = inside(mid_rows, mid_cols, pitch, reach, rows, cols)
    for s in range(mid_rows // step_rows):
        at = pl.ds(s * step_rows + reach, step_rows)
        flat = slice(s * step_rows * pitch, (s + 1) * step_rows * pitch)
        centre = first[at, pl.ds(reach, pitch), :].reshape(step_rows * pitch, lanes)
        source = source_ref[at, pl.ds(reach, pitch), :].reshape(step_rows * pitch, lanes)
        value = centre + invert(source - centre - acc[flat, :])
        value = jnp.where(mask[flat], value, 0.0)
        second[s * step_rows : (s + 1) * step_rows] = value.reshape(step_rows, pitch, lanes)

    @pl.loop(0, mid_rows)
    def _(i):
        for b in range(span):
            high, low = split(second[i, pl.ds(b, cols), :])
            to = pl.ds(pl.multiple_of(i * cols, cols), cols)
            x2_high[to, b * lanes : (b + 1) * lanes] = high
            x2_low[to, b * lanes : (b + 1) * lanes] = low

    own = rows * cols
    acc[:own] = jnp.zeros((own, lanes), f32)

    @pl.loop(0, span)
    def _(a):
        at = pl.ds(pl.multiple_of(a * cols, cols), own)
        high = x2_high[at, :]
        low = x2_low[at, :]
        weight_high = w_high[a].reshape(span * lanes, lanes)
        weight_low = w_low[a].reshape(span * lanes, lanes)
        acc[:own] += dot(high, weight_high) + dot(low, weight_high) + dot(high, weight_low)

    centre = second[reach : reach + rows, pl.ds(reach, cols), :].reshape(own, lanes)
    source = source_ref[2 * reach : 2 * reach + rows, pl.ds(2 * reach, cols), :].reshape(own, lanes)
    value = centre + invert(source - centre - acc[:own])
    adjoint_ref[...] = value.reshape(adjoint_ref.shape)
    turned[...] = value.T

    share = width // peers
    me = lax.axis_index("row")
    for k in range(peers):
        peer = lax.rem(me + k, peers)
        for part in range(2):
            at = pl.multiple_of(part * width + peer * share, share)
            sends[k][part * share : (part + 1) * share, :] = turned[pl.ds(at, share), :]


def run_sweeps(source, inverse, high, low, rows, cols, peers):
    span = high.shape[0]
    reach = span // 2
    lanes = source.shape[-1]
    wide = source.shape[1]
    pitch = round_up(cols + 2 * reach, 8)
    full_rows, mid_rows = rows + 4 * reach, rows + 2 * reach
    share = lanes // 2 // peers
    sizes = (rows, cols, span, peers, pitch, wide)
    vmem = pl.BlockSpec(memory_space=pltpu.VMEM)
    hbm = pl.BlockSpec(memory_space=pl.ANY)
    send = jax.ShapeDtypeStruct((2 * share, rows * cols), f32)
    flops = 6 * span * span * lanes * lanes * (mid_rows * pitch + rows * cols)
    out = pl.pallas_call(
        functools.partial(sweeps_kernel, sizes),
        in_specs=[vmem, vmem, hbm, hbm],
        out_specs=[vmem] * (1 + peers),
        out_shape=[jax.ShapeDtypeStruct((rows, cols, lanes), f32)] + [send] * peers,
        scratch_shapes=[
            pltpu.VMEM((full_rows + 1, wide, lanes), f32),
            pltpu.VMEM((mid_rows, pitch, lanes), f32),
            pltpu.VMEM((2, full_rows * pitch, span * lanes), bf16),
            pltpu.VMEM((2, full_rows * pitch, span * lanes), bf16),
            pltpu.VMEM((mid_rows * cols, span * lanes), bf16),
            pltpu.VMEM((mid_rows * cols, span * lanes), bf16),
            pltpu.VMEM((mid_rows * pitch, lanes), f32),
            pltpu.VMEM((lanes, rows * cols), f32),
            pltpu.VMEM(high.shape, bf16),
            pltpu.VMEM(high.shape, bf16),
            pltpu.VMEM((lanes, lanes), bf16),
            pltpu.VMEM((lanes, lanes), bf16),
            pltpu.SemaphoreType.DMA((2, span)),
        ],
        cost_estimate=pl.CostEstimate(
            flops=flops, bytes_accessed=4 * high.size, transcendentals=0
        ),
        compiler_params=pltpu.CompilerParams(vmem_limit_bytes=VMEM_LIMIT),
        name="sweeps",
    )(source, inverse, high, low)
    return out[0], out[1:]


def correlate_kernel(sizes, factor, *refs):
    rows, cols, span, peers = sizes
    shares = refs[:peers]
    currents = refs[peers : 2 * peers]
    mine_ref, other_ref = refs[2 * peers : 2 * peers + 2]
    placed, flat, l_high, l_low, s_high, s_low = refs[2 * peers + 2 :]
    reach = span // 2
    own = rows * cols
    double = shares[0].shape[0]
    share = double // 2
    width = currents[0].shape[-1]
    lanes = 2 * width
    side = round_up(reach * cols, 128)
    me = lax.axis_index("row")

    twin = me + 1 - 2 * lax.rem(me, 2)
    for k in range(peers):
        placed[lax.rem(me - k + peers, peers)] = shares[k][...]
        tile = lax.rem((twin if k % 2 else me) - k + k % 2 + peers, peers)

        @pl.loop(0, rows)
        def _(i):
            to = pl.ds(pl.multiple_of(tile * own + i * cols, cols), cols)
            for b in range(span):
                for h in range(2):
                    value = currents[k][h, i, pl.ds(span - 1 - b, cols), :]
                    high, low = split(value)
                    at = b * lanes + h * width
                    s_high[to, at : at + width] = high
                    s_low[to, at : at + width] = low

    total = peers * own
    flat[:, :side] = jnp.zeros((double, side), f32)
    flat[:, side + total :] = jnp.zeros((double, side), f32)
    for tile in range(peers):
        flat[:, side + tile * own : side + (tile + 1) * own] = placed[tile]
    for a in range(span):
        start = side + (a - reach) * cols
        high, low = split(flat[:, start : start + total])
        l_high[a * double : (a + 1) * double, :] = high
        l_low[a * double : (a + 1) * double, :] = low

    half = share // 2
    upper = lax.axis_index("col") % 2 == 1
    for b in range(span):
        at = slice(b * lanes, (b + 1) * lanes)
        product = dot3((l_high[...], l_low[...]), (s_high[:, at], s_low[:, at])) * factor
        for a in range(span):
            top = product[a * double : a * double + share]
            bottom = product[a * double + share : (a + 1) * double]
            real = top[:, :width] + bottom[:, width:]
            imag = bottom[:, :width] - top[:, width:]
            for c, value in enumerate((real, imag)):
                mine_ref[a, b, c] = jnp.where(upper, value[half:], value[:half])
                other_ref[a, b, c] = jnp.where(upper, value[:half], value[half:])


def correlate(shares, currents, rows, cols, span, factor):
    peers = len(shares)
    reach = span // 2
    double, own = shares[0].shape
    share = double // 2
    width = currents[0].shape[-1]
    total = peers * own
    side = round_up(reach * cols, 128)
    vmem = pl.BlockSpec(memory_space=pltpu.VMEM)
    out = jax.ShapeDtypeStruct((span, span, 2, share // 2, width), f32)
    return pl.pallas_call(
        functools.partial(correlate_kernel, (rows, cols, span, peers), factor),
        in_specs=[vmem] * (2 * peers),
        out_specs=[vmem, vmem],
        out_shape=[out, out],
        scratch_shapes=[
            pltpu.VMEM((peers, double, own), f32),
            pltpu.VMEM((double, total + 2 * side), f32),
            pltpu.VMEM((span * double, total), bf16),
            pltpu.VMEM((span * double, total), bf16),
            pltpu.VMEM((total, span * 2 * width), bf16),
            pltpu.VMEM((total, span * 2 * width), bf16),
        ],
        cost_estimate=pl.CostEstimate(
            flops=6 * span * double * total * span * 2 * width,
            bytes_accessed=4 * (2 * out.size + peers * currents[0].size),
            transcendentals=0,
        ),
        compiler_params=pltpu.CompilerParams(vmem_limit_bytes=VMEM_LIMIT),
        name="correlate",
    )(*shares, *currents)


def swap(value, axis, first):
    pairs = []
    for low in range(first, lax.axis_size(axis) - 1, 2):
        pairs += [(low, low + 1), (low + 1, low)]
    if not pairs:
        return jnp.zeros_like(value)
    return lax.ppermute(value, axis, pairs)


def shifted(value, axis, shift):
    peers = lax.axis_size(axis)
    if shift % peers == 0:
        return value
    return lax.ppermute(value, axis, [(i, (i + shift) % peers) for i in range(peers)])


def edges(initial, last, axis):
    even = lax.axis_index(axis) % 2 == 0
    inner = swap(jnp.where(even, last, initial), axis, 0)
    outer = swap(jnp.where(even, initial, last), axis, 1)
    return jnp.where(even, outer, inner), jnp.where(even, inner, outer)


def on_device(adjoint_source, saved_currents, lag_blocks, element_inverse):
    rows, cols, parts, width = adjoint_source.shape
    span = lag_blocks.shape[0]
    reach = span // 2
    halo = SWEEPS * reach
    lanes = parts * width
    peers = lax.axis_size("row")
    source = adjoint_source.reshape(rows, cols, lanes)
    saved = saved_currents.reshape(rows, cols, lanes)

    high, low = prepare_weights(lag_blocks)

    initial = jnp.concatenate([source[:, :halo], saved[:, :reach]], axis=1)
    last = jnp.concatenate([source[:, cols - halo :], saved[:, cols - reach :]], axis=1)
    before, after = edges(initial, last, "col")
    wide = round_up(cols + 2 * halo, 8)
    filler = jnp.zeros((rows, wide - cols - 2 * halo, lanes), f32)
    source = jnp.concatenate([before[:, :halo], source, after[:, :halo], filler], axis=1)
    saved = jnp.concatenate([before[:, halo:], saved, after[:, halo:]], axis=1)
    before, after = edges(source[:halo], source[rows - halo :], "row")
    source = jnp.concatenate([before, source, after], axis=0)

    saved = jnp.pad(saved, ((0, 0), (0, round_up(cols + 2 * reach, 8) - cols - 2 * reach), (0, 0)))
    saved = saved.reshape(rows, -1, parts, width).transpose(2, 0, 1, 3)
    currents = [None] * peers
    for k in range(0, peers, 2):
        piece = shifted(saved, "row", k)
        twin = swap(piece, "row", 0)
        currents[k] = piece
        currents[k + 1] = twin

    adjoint, sends = run_sweeps(source, element_inverse, high, low, rows, cols, peers)
    shares = [shifted(send, "row", k) for k, send in enumerate(sends)]

    elements = rows * peers * cols * lax.axis_size("col")
    factor = -1.0 / math.sqrt(elements)
    mine, other = correlate(shares, currents, rows, cols, span, factor)
    mine = mine + swap(other, "col", 0)
    total = mine
    for k in range(2, lax.axis_size("col"), 2):
        total = total + shifted(mine, "col", k)
    twin = swap(total, "col", 0)
    even = lax.axis_index("col") % 2 == 0
    lag_grad = jnp.concatenate(
        [jnp.where(even, total, twin), jnp.where(even, twin, total)], axis=3
    )
    return (adjoint.reshape(adjoint_source.shape), lag_grad)


def solution(mesh):
    return jax.shard_map(
        on_device,
        mesh=mesh,
        in_specs=(P("row", "col", None, None), P("row", "col", None, None), P(), P()),
        out_specs=(P("row", "col", None, None), P(None, None, None, "row", None)),
        check_vma=False,
    )
```

```python
import functools
import math

import jax
import jax.numpy as jnp
from jax import lax
from jax.experimental import pallas as pl
from jax.experimental.pallas import tpu as pltpu
from jax.sharding import PartitionSpec as P

SWEEPS = 2
VMEM_LIMIT = 56 * 1024 * 1024

f32 = jnp.float32
bf16 = jnp.bfloat16


def split(value):
    high = value.astype(bf16)
    return high, (value - high.astype(f32)).astype(bf16)


def dot(left, right):
    return jnp.dot(left, right, preferred_element_type=f32)


def dot3(left, right):
    (left_high, left_low), (right_high, right_low) = left, right
    return dot(left_high, right_high) + dot(left_low, right_high) + dot(left_high, right_low)


def round_up(count, unit):
    return (count + unit - 1) // unit * unit


def store_block(ref, index, real, imag):
    width = real.shape[0]
    low, high = slice(0, width), slice(width, 2 * width)
    ref[index + (low, low)] = real
    ref[index + (low, high)] = -imag
    ref[index + (high, low)] = imag
    ref[index + (high, high)] = real


def inside(first_row, rows, cols, pitch, margin, tile_rows, tile_cols):
    at = lax.broadcasted_iota(jnp.int32, (rows * pitch, 1), 0)
    i = at // pitch
    j = at - i * pitch
    row = i + (first_row + lax.axis_index("row") * tile_rows - margin)
    col = j + (lax.axis_index("col") * tile_cols - margin)
    row_ok = (row >= 0) & (row < tile_rows * lax.axis_size("row"))
    col_ok = (col >= 0) & (col < tile_cols * lax.axis_size("col"))
    return row_ok & col_ok & (j < cols)


def sweeps_kernel(
    sizes,
    source_ref,
    inverse_ref,
    blocks_hbm,
    adjoint_ref,
    *rest,
):
    rows, cols, span, peers, pitch, wide = sizes
    sends = rest[:peers]
    (first, second, x1_high, x1_low, x2_high, x2_low, acc, turned, raw, w_high, w_low, e_high, e_low, sems) = rest[peers:]
    reach = span // 2
    mid_rows, mid_cols = rows + 2 * reach, cols + 2 * reach
    full_rows = rows + 4 * reach
    lanes = source_ref.shape[-1]
    width = lanes // 2

    def block_copy(a):
        return pltpu.make_async_copy(blocks_hbm.at[a], raw.at[a], sems.at[a])

    for a in range(span):
        block_copy(a).start()

    def prepare(a):
        @pl.loop(0, span)
        def _(b):
            real_high, real_low = split(raw[a, b, 0])
            imag_high, imag_low = split(raw[a, b, 1])
            store_block(w_high, (a, b), real_high, imag_high)
            store_block(w_low, (a, b), real_low, imag_low)

    def products(a, high, low):
        weight_high = w_high[a].reshape(span * lanes, lanes)
        weight_low = w_low[a].reshape(span * lanes, lanes)
        return dot(high, weight_high) + dot(low, weight_high) + dot(high, weight_low)

    real_high, real_low = split(inverse_ref[0])
    imag_high, imag_low = split(inverse_ref[1])
    store_block(e_high, (), real_high, imag_high)
    store_block(e_low, (), real_low, imag_low)

    def invert(value):
        return dot3(split(value), (e_high[...], e_low[...]))

    step_rows = 4

    @pl.loop(0, full_rows // step_rows)
    def _(s):
        at = pl.ds(s * step_rows, step_rows)
        piece = source_ref[at].reshape(step_rows * wide, lanes)
        first[at] = invert(piece).reshape(step_rows, wide, lanes)

    first[full_rows] = jnp.zeros((wide, lanes), f32)

    @pl.loop(0, full_rows // 2)
    def _(s):
        for odd in range(2):
            for b in range(span):
                value = first[pl.ds(2 * s + odd, 2), pl.ds(b, pitch), :]
                high, low = split(value.reshape(2 * pitch, lanes))
                to = pl.ds(pl.multiple_of(s * 2 * pitch, 2 * pitch), 2 * pitch)
                x1_high[odd, to, b * lanes : (b + 1) * lanes] = high
                x1_low[odd, to, b * lanes : (b + 1) * lanes] = low

    acc[...] = jnp.zeros_like(acc)

    @pl.loop(0, span)
    def _(a):
        block_copy(a).wait()
        prepare(a)
        at = pl.ds(pl.multiple_of((a // 2) * 2 * pitch, 2 * pitch), mid_rows * pitch)
        acc[...] += products(a, x1_high[a % 2, at, :], x1_low[a % 2, at, :])

    step_rows = 3

    @pl.loop(0, mid_rows // step_rows)
    def _(s):
        at = pl.ds(s * step_rows + reach, step_rows)
        count = step_rows * pitch
        flat = pl.ds(pl.multiple_of(s * count, 8), count)
        centre = first[at, pl.ds(reach, pitch), :].reshape(count, lanes)
        source = source_ref[at, pl.ds(reach, pitch), :].reshape(count, lanes)
        value = centre + invert(source - centre - acc[flat, :])
        mask = inside(s * step_rows, step_rows, mid_cols, pitch, reach, rows, cols)
        value = jnp.where(mask, value, 0.0)
        second[pl.ds(s * step_rows, step_rows)] = value.reshape(step_rows, pitch, lanes)

    @pl.loop(0, mid_rows)
    def _(i):
        for b in range(span):
            high, low = split(second[i, pl.ds(b, cols), :])
            to = pl.ds(pl.multiple_of(i * cols, cols), cols)
            x2_high[to, b * lanes : (b + 1) * lanes] = high
            x2_low[to, b * lanes : (b + 1) * lanes] = low

    own = rows * cols
    acc[:own] = jnp.zeros((own, lanes), f32)

    @pl.loop(0, span)
    def _(a):
        at = pl.ds(pl.multiple_of(a * cols, cols), own)
        acc[:own] += products(a, x2_high[at, :], x2_low[at, :])

    centre = second[reach : reach + rows, pl.ds(reach, cols), :].reshape(own, lanes)
    source = source_ref[2 * reach : 2 * reach + rows, pl.ds(2 * reach, cols), :].reshape(own, lanes)
    value = centre + invert(source - centre - acc[:own])
    adjoint_ref[...] = value.reshape(adjoint_ref.shape)
    turned[...] = value.T

    share = width // peers
    me = lax.axis_index("row")
    for k in range(peers):
        peer = lax.rem(me + k, peers)
        for part in range(2):
            at = pl.multiple_of(part * width + peer * share, share)
            sends[k][part * share : (part + 1) * share, :] = turned[pl.ds(at, share), :]


def run_sweeps(source, inverse, lag_blocks, rows, cols, peers):
    span = lag_blocks.shape[0]
    reach = span // 2
    lanes = source.shape[-1]
    wide = source.shape[1]
    pitch = round_up(cols + 2 * reach, 8)
    full_rows, mid_rows = rows + 4 * reach, rows + 2 * reach
    share = lanes // 2 // peers
    sizes = (rows, cols, span, peers, pitch, wide)
    vmem = pl.BlockSpec(memory_space=pltpu.VMEM)
    hbm = pl.BlockSpec(memory_space=pl.ANY)
    send = jax.ShapeDtypeStruct((2 * share, rows * cols), f32)
    flops = 6 * span * span * lanes * lanes * (mid_rows * pitch + rows * cols)
    out = pl.pallas_call(
        functools.partial(sweeps_kernel, sizes),
        in_specs=[vmem, vmem, hbm],
        out_specs=[vmem] * (1 + peers),
        out_shape=[jax.ShapeDtypeStruct((rows, cols, lanes), f32)] + [send] * peers,
        scratch_shapes=[
            pltpu.VMEM((full_rows + 1, wide, lanes), f32),
            pltpu.VMEM((mid_rows, pitch, lanes), f32),
            pltpu.VMEM((2, full_rows * pitch, span * lanes), bf16),
            pltpu.VMEM((2, full_rows * pitch, span * lanes), bf16),
            pltpu.VMEM((mid_rows * cols, span * lanes), bf16),
            pltpu.VMEM((mid_rows * cols, span * lanes), bf16),
            pltpu.VMEM((mid_rows * pitch, lanes), f32),
            pltpu.VMEM((lanes, rows * cols), f32),
            pltpu.VMEM(lag_blocks.shape, f32),
            pltpu.VMEM((span, span, lanes, lanes), bf16),
            pltpu.VMEM((span, span, lanes, lanes), bf16),
            pltpu.VMEM((lanes, lanes), bf16),
            pltpu.VMEM((lanes, lanes), bf16),
            pltpu.SemaphoreType.DMA((span,)),
        ],
        cost_estimate=pl.CostEstimate(
            flops=flops, bytes_accessed=4 * lag_blocks.size, transcendentals=0
        ),
        compiler_params=pltpu.CompilerParams(vmem_limit_bytes=VMEM_LIMIT),
        name="sweeps",
    )(source, inverse, lag_blocks)
    return out[0], out[1:]


def correlate_kernel(sizes, factor, *refs):
    rows, cols, span, peers = sizes
    shares = refs[:peers]
    piece_refs = refs[peers : peers + peers // 2]
    own_twin_ref, twins_ref = refs[peers + peers // 2 : peers + peers // 2 + 2]
    refs = refs[peers + peers // 2 + 2 :]
    mine_ref, other_ref = refs[:2]
    placed, flat, l_high, l_low, stage, s_high, s_low, sems = refs[2:]
    reach = span // 2
    own = rows * cols
    double = shares[0].shape[0]
    share = double // 2
    width = stage.shape[-1]
    me = lax.axis_index("row")
    even = me - lax.rem(me, 2)
    odd = 1 - lax.rem(me, 2)

    copies = []
    for k in range(peers // 2):
        base = lax.rem(even - 2 * k + peers, peers)
        twin = own_twin_ref if k == 0 else twins_ref.at[k - 1]
        copies.append(pltpu.make_async_copy(piece_refs[k], stage.at[base + 1 - odd], sems.at[0, k]))
        copies.append(pltpu.make_async_copy(twin, stage.at[base + odd], sems.at[1, k]))
    for copy in copies:
        copy.start()

    for k in range(peers):
        placed[lax.rem(me - k + peers, peers)] = shares[k][...]
    total = peers * own
    side = round_up(reach * cols, 128)
    flat[:, :side] = jnp.zeros((double, side), f32)
    flat[:, side + total :] = jnp.zeros((double, side), f32)
    for tile in range(peers):
        flat[:, side + tile * own : side + (tile + 1) * own] = placed[tile]

    @pl.loop(0, 2)
    def _(part):
        rows_at = pl.ds(pl.multiple_of(part * share, 8), share)
        for a in range(span):
            start = side + (a - reach) * cols
            high, low = split(flat[rows_at, start : start + total])
            l_high[a, part] = high
            l_low[a, part] = low

    for copy in copies:
        copy.wait()

    @pl.loop(0, peers)
    def _(tile):
        @pl.loop(0, rows)
        def _(i):
            to = pl.ds(pl.multiple_of(tile * own + i * cols, cols), cols)
            for b in range(span):
                for h in range(2):
                    high, low = split(stage[tile, h, i, pl.ds(span - 1 - b, cols), :])
                    s_high[b, to, h * width : (h + 1) * width] = high
                    s_low[b, to, h * width : (h + 1) * width] = low

    half = share // 2
    upper = lax.axis_index("col") % 2 == 1

    @pl.loop(0, span)
    def _(b):
        left = tuple(ref[...].reshape(span * double, total) for ref in (l_high, l_low))
        product = dot3(left, (s_high[b], s_low[b])) * factor
        for a in range(span):
            top = product[a * double : a * double + share]
            bottom = product[a * double + share : (a + 1) * double]
            real = top[:, :width] + bottom[:, width:]
            imag = bottom[:, :width] - top[:, width:]
            for c, value in enumerate((real, imag)):
                mine_ref[a, b, c] = jnp.where(upper, value[half:], value[:half])
                other_ref[a, b, c] = jnp.where(upper, value[:half], value[half:])


def correlate(shares, pieces, own_twin, twins, rows, cols, span, factor):
    peers = len(shares)
    reach = span // 2
    double, own = shares[0].shape
    share = double // 2
    width = own_twin.shape[-1]
    total = peers * own
    side = round_up(reach * cols, 128)
    vmem = pl.BlockSpec(memory_space=pltpu.VMEM)
    hbm = pl.BlockSpec(memory_space=pl.ANY)
    out = jax.ShapeDtypeStruct((span, span, 2, share // 2, width), f32)
    return pl.pallas_call(
        functools.partial(correlate_kernel, (rows, cols, span, peers), factor),
        in_specs=[vmem] * peers + [hbm] * (peers // 2 + 2),
        out_specs=[vmem, vmem],
        out_shape=[out, out],
        scratch_shapes=[
            pltpu.VMEM((peers, double, own), f32),
            pltpu.VMEM((double, total + 2 * side), f32),
            pltpu.VMEM((span, 2, share, total), bf16),
            pltpu.VMEM((span, 2, share, total), bf16),
            pltpu.VMEM((peers,) + own_twin.shape, f32),
            pltpu.VMEM((span, total, 2 * width), bf16),
            pltpu.VMEM((span, total, 2 * width), bf16),
            pltpu.SemaphoreType.DMA((2, peers // 2)),
        ],
        cost_estimate=pl.CostEstimate(
            flops=6 * span * double * total * span * 2 * width,
            bytes_accessed=4 * (2 * out.size + peers * own_twin.size),
            transcendentals=0,
        ),
        compiler_params=pltpu.CompilerParams(vmem_limit_bytes=VMEM_LIMIT),
        name="correlate",
    )(*shares, *pieces, own_twin, twins)


def swap(value, axis, first):
    pairs = []
    for low in range(first, lax.axis_size(axis) - 1, 2):
        pairs += [(low, low + 1), (low + 1, low)]
    if not pairs:
        return jnp.zeros_like(value)
    return lax.ppermute(value, axis, pairs)


def shifted(value, axis, shift):
    peers = lax.axis_size(axis)
    if shift % peers == 0:
        return value
    return lax.ppermute(value, axis, [(i, (i + shift) % peers) for i in range(peers)])


def edges(initial, last, axis):
    even = lax.axis_index(axis) % 2 == 0
    inner = swap(jnp.where(even, last, initial), axis, 0)
    outer = swap(jnp.where(even, initial, last), axis, 1)
    return jnp.where(even, outer, inner), jnp.where(even, inner, outer)


def on_device(adjoint_source, saved_currents, lag_blocks, element_inverse):
    rows, cols, parts, width = adjoint_source.shape
    span = lag_blocks.shape[0]
    reach = span // 2
    halo = SWEEPS * reach
    lanes = parts * width
    peers = lax.axis_size("row")
    source = adjoint_source.reshape(rows, cols, lanes)
    saved = saved_currents.reshape(rows, cols, lanes)

    initial = jnp.concatenate([source[:, :halo], saved[:, :reach]], axis=1)
    last = jnp.concatenate([source[:, cols - halo :], saved[:, cols - reach :]], axis=1)
    before, after = edges(initial, last, "col")
    wide = round_up(cols + 2 * halo, 8)
    filler = jnp.zeros((rows, wide - cols - 2 * halo, lanes), f32)
    source = jnp.concatenate([before[:, :halo], source, after[:, :halo], filler], axis=1)
    saved = jnp.concatenate([before[:, halo:], saved, after[:, halo:]], axis=1)
    before, after = edges(source[:halo], source[rows - halo :], "row")
    source = jnp.concatenate([before, source, after], axis=0)

    saved = jnp.pad(saved, ((0, 0), (0, round_up(cols + 2 * reach, 8) - cols - 2 * reach), (0, 0)))
    saved = saved.reshape(rows, -1, parts, width).transpose(2, 0, 1, 3)
    pieces = [shifted(saved, "row", k) for k in range(0, peers, 2)]
    own_twin = swap(saved, "row", 0)

    adjoint, sends = run_sweeps(source, element_inverse, lag_blocks, rows, cols, peers)
    twins, sends = lax.optimization_barrier((jnp.stack(pieces[1:]), sends))
    twins = swap(twins, "row", 0)
    shares = [shifted(send, "row", k) for k, send in enumerate(sends)]

    elements = rows * peers * cols * lax.axis_size("col")
    factor = -1.0 / math.sqrt(elements)
    mine, other = correlate(shares, pieces, own_twin, twins, rows, cols, span, factor)
    mine = mine + swap(other, "col", 0)
    total = mine
    for k in range(2, lax.axis_size("col"), 2):
        total = total + shifted(mine, "col", k)
    twin = swap(total, "col", 0)
    even = lax.axis_index("col") % 2 == 0
    lag_grad = jnp.concatenate(
        [jnp.where(even, total, twin), jnp.where(even, twin, total)], axis=3
    )
    return (adjoint.reshape(adjoint_source.shape), lag_grad)


def solution(mesh):
    return jax.shard_map(
        on_device,
        mesh=mesh,
        in_specs=(P("row", "col", None, None), P("row", "col", None, None), P(), P()),
        out_specs=(P("row", "col", None, None), P(None, None, None, "row", None)),
        check_vma=False,
    )
```

```python
import functools
import math

import jax
import jax.numpy as jnp
from jax import lax
from jax.experimental import pallas as pl
from jax.experimental.pallas import tpu as pltpu
from jax.sharding import PartitionSpec as P

SWEEPS = 2
VMEM_LIMIT = 56 * 1024 * 1024

f32 = jnp.float32
bf16 = jnp.bfloat16


def split(value):
    high = value.astype(bf16)
    return high, (value - high.astype(f32)).astype(bf16)


def dot(left, right):
    return jnp.dot(left, right, preferred_element_type=f32)


def dot3(left, right):
    (left_high, left_low), (right_high, right_low) = left, right
    return dot(left_high, right_high) + dot(left_low, right_high) + dot(left_high, right_low)


def round_up(count, unit):
    return (count + unit - 1) // unit * unit


def store_block(ref, index, real, imag):
    width = real.shape[0]
    low, high = slice(0, width), slice(width, 2 * width)
    ref[index + (low, low)] = real
    ref[index + (low, high)] = -imag
    ref[index + (high, low)] = imag
    ref[index + (high, high)] = real


def inside(first_row, rows, cols, pitch, margin, tile_rows, tile_cols):
    at = lax.broadcasted_iota(jnp.int32, (rows * pitch, 1), 0)
    i = at // pitch
    j = at - i * pitch
    row = i + (first_row + lax.axis_index("row") * tile_rows - margin)
    col = j + (lax.axis_index("col") * tile_cols - margin)
    row_ok = (row >= 0) & (row < tile_rows * lax.axis_size("row"))
    col_ok = (col >= 0) & (col < tile_cols * lax.axis_size("col"))
    return row_ok & col_ok & (j < cols)


def sweeps_kernel(
    sizes,
    source_ref,
    inverse_ref,
    blocks_hbm,
    adjoint_ref,
    *rest,
):
    rows, cols, span, peers, pitch, wide = sizes
    sends = rest[: peers // 2]
    (first, second, x1_high, x1_low, x2_high, x2_low, acc, turned, raw, w_high, w_low, e_high, e_low, sems) = rest[peers // 2 :]
    reach = span // 2
    mid_rows, mid_cols = rows + 2 * reach, cols + 2 * reach
    full_rows = rows + 4 * reach
    lanes = source_ref.shape[-1]
    width = lanes // 2

    def block_copy(a):
        return pltpu.make_async_copy(blocks_hbm.at[a], raw.at[a], sems.at[a])

    for a in range(span):
        block_copy(a).start()

    def prepare(a):
        @pl.loop(0, span)
        def _(b):
            real_high, real_low = split(raw[a, b, 0])
            imag_high, imag_low = split(raw[a, b, 1])
            store_block(w_high, (a, b), real_high, imag_high)
            store_block(w_low, (a, b), real_low, imag_low)

    def products(a, high, low):
        weight_high = w_high[a].reshape(span * lanes, lanes)
        weight_low = w_low[a].reshape(span * lanes, lanes)
        return dot(high, weight_high) + dot(low, weight_high) + dot(high, weight_low)

    real_high, real_low = split(inverse_ref[0])
    imag_high, imag_low = split(inverse_ref[1])
    store_block(e_high, (), real_high, imag_high)
    store_block(e_low, (), real_low, imag_low)

    def invert(value):
        return dot3(split(value), (e_high[...], e_low[...]))

    step_rows = 4

    @pl.loop(0, full_rows // step_rows)
    def _(s):
        at = pl.ds(s * step_rows, step_rows)
        piece = source_ref[at].reshape(step_rows * wide, lanes)
        first[at] = invert(piece).reshape(step_rows, wide, lanes)

    first[full_rows] = jnp.zeros((wide, lanes), f32)

    @pl.loop(0, full_rows // 2)
    def _(s):
        for odd in range(2):
            for b in range(span):
                value = first[pl.ds(2 * s + odd, 2), pl.ds(b, pitch), :]
                high, low = split(value.reshape(2 * pitch, lanes))
                to = pl.ds(pl.multiple_of(s * 2 * pitch, 2 * pitch), 2 * pitch)
                x1_high[odd, to, b * lanes : (b + 1) * lanes] = high
                x1_low[odd, to, b * lanes : (b + 1) * lanes] = low

    acc[...] = jnp.zeros_like(acc)

    @pl.loop(0, span)
    def _(a):
        block_copy(a).wait()
        prepare(a)
        at = pl.ds(pl.multiple_of((a // 2) * 2 * pitch, 2 * pitch), mid_rows * pitch)
        acc[...] += products(a, x1_high[a % 2, at, :], x1_low[a % 2, at, :])

    step_rows = 3

    @pl.loop(0, mid_rows // step_rows)
    def _(s):
        at = pl.ds(s * step_rows + reach, step_rows)
        count = step_rows * pitch
        flat = pl.ds(pl.multiple_of(s * count, 8), count)
        centre = first[at, pl.ds(reach, pitch), :].reshape(count, lanes)
        source = source_ref[at, pl.ds(reach, pitch), :].reshape(count, lanes)
        value = centre + invert(source - centre - acc[flat, :])
        mask = inside(s * step_rows, step_rows, mid_cols, pitch, reach, rows, cols)
        value = jnp.where(mask, value, 0.0)
        second[pl.ds(s * step_rows, step_rows)] = value.reshape(step_rows, pitch, lanes)

    @pl.loop(0, mid_rows)
    def _(i):
        for b in range(span):
            high, low = split(second[i, pl.ds(b, cols), :])
            to = pl.ds(pl.multiple_of(i * cols, cols), cols)
            x2_high[to, b * lanes : (b + 1) * lanes] = high
            x2_low[to, b * lanes : (b + 1) * lanes] = low

    own = rows * cols
    acc[:own] = jnp.zeros((own, lanes), f32)

    @pl.loop(0, span)
    def _(a):
        at = pl.ds(pl.multiple_of(a * cols, cols), own)
        acc[:own] += products(a, x2_high[at, :], x2_low[at, :])

    centre = second[reach : reach + rows, pl.ds(reach, cols), :].reshape(own, lanes)
    source = source_ref[2 * reach : 2 * reach + rows, pl.ds(2 * reach, cols), :].reshape(own, lanes)
    value = centre + invert(source - centre - acc[:own])
    adjoint_ref[...] = value.reshape(adjoint_ref.shape)
    turned[...] = value.T

    share = width // peers
    me = lax.axis_index("row")
    twin = me + 1 - 2 * lax.rem(me, 2)
    for k in range(peers // 2):
        for n, target in enumerate((me, twin)):
            peer = lax.rem(target + 2 * k, peers)
            for part in range(2):
                at = pl.multiple_of(part * width + peer * share, share)
                sends[k][n, part * share : (part + 1) * share, :] = turned[pl.ds(at, share), :]


def run_sweeps(source, inverse, lag_blocks, rows, cols, peers):
    span = lag_blocks.shape[0]
    reach = span // 2
    lanes = source.shape[-1]
    wide = source.shape[1]
    pitch = round_up(cols + 2 * reach, 8)
    full_rows, mid_rows = rows + 4 * reach, rows + 2 * reach
    share = lanes // 2 // peers
    sizes = (rows, cols, span, peers, pitch, wide)
    vmem = pl.BlockSpec(memory_space=pltpu.VMEM)
    hbm = pl.BlockSpec(memory_space=pl.ANY)
    send = jax.ShapeDtypeStruct((2, 2 * share, rows * cols), f32)
    flops = 6 * span * span * lanes * lanes * (mid_rows * pitch + rows * cols)
    out = pl.pallas_call(
        functools.partial(sweeps_kernel, sizes),
        in_specs=[vmem, vmem, hbm],
        out_specs=[vmem] * (1 + peers // 2),
        out_shape=[jax.ShapeDtypeStruct((rows, cols, lanes), f32)] + [send] * (peers // 2),
        scratch_shapes=[
            pltpu.VMEM((full_rows + 1, wide, lanes), f32),
            pltpu.VMEM((mid_rows, pitch, lanes), f32),
            pltpu.VMEM((2, full_rows * pitch, span * lanes), bf16),
            pltpu.VMEM((2, full_rows * pitch, span * lanes), bf16),
            pltpu.VMEM((mid_rows * cols, span * lanes), bf16),
            pltpu.VMEM((mid_rows * cols, span * lanes), bf16),
            pltpu.VMEM((mid_rows * pitch, lanes), f32),
            pltpu.VMEM((lanes, rows * cols), f32),
            pltpu.VMEM(lag_blocks.shape, f32),
            pltpu.VMEM((span, span, lanes, lanes), bf16),
            pltpu.VMEM((span, span, lanes, lanes), bf16),
            pltpu.VMEM((lanes, lanes), bf16),
            pltpu.VMEM((lanes, lanes), bf16),
            pltpu.SemaphoreType.DMA((span,)),
        ],
        cost_estimate=pl.CostEstimate(
            flops=flops, bytes_accessed=4 * lag_blocks.size, transcendentals=0
        ),
        compiler_params=pltpu.CompilerParams(vmem_limit_bytes=VMEM_LIMIT),
        name="sweeps",
    )(source, inverse, lag_blocks)
    return out[0], out[1:]


def correlate_kernel(sizes, factor, *refs):
    rows, cols, span, peers = sizes
    half_peers = peers // 2
    shares, piece_refs = refs[:half_peers], refs[half_peers:peers]
    twin_shares_ref, own_twin_ref, twins_ref, mine_ref, other_ref = refs[peers : peers + 5]
    placed, flat, l_high, l_low, stage, s_high, s_low, sems = refs[peers + 5 :]
    reach = span // 2
    own = rows * cols
    double = shares[0].shape[1]
    share = double // 2
    width = stage.shape[-1]
    me = lax.axis_index("row")
    even = me - lax.rem(me, 2)
    odd = 1 - lax.rem(me, 2)

    def tiles(k):
        base = lax.rem(even - 2 * k + peers, peers)
        return base + 1 - odd, base + odd

    for k in range(half_peers):
        twin = own_twin_ref if k == 0 else twins_ref.at[k - 1]
        for n, (source, tile) in enumerate(zip((piece_refs[k], twin), tiles(k))):
            pltpu.make_async_copy(source, stage.at[tile], sems.at[n, k]).start()
        first, second = tiles(k)
        placed[first] = shares[k][0]
        placed[second] = twin_shares_ref[k]

    total = peers * own
    side = round_up(reach * cols, 128)
    flat[:, :side] = jnp.zeros((double, side), f32)
    flat[:, side + total :] = jnp.zeros((double, side), f32)
    for tile in range(peers):
        flat[:, side + tile * own : side + (tile + 1) * own] = placed[tile]

    @pl.loop(0, 2)
    def _(part):
        rows_at = pl.ds(pl.multiple_of(part * share, 8), share)
        for a in range(span):
            start = side + (a - reach) * cols
            high, low = split(flat[rows_at, start : start + total])
            l_high[a, part] = high
            l_low[a, part] = low

    @pl.loop(0, peers)
    def _(at):
        n, k = lax.rem(at, 2), at // 2
        first, second = tiles(k)
        tile = jnp.where(n == 0, first, second)
        pltpu.make_async_copy(own_twin_ref, stage.at[tile], sems.at[n, k]).wait()

        @pl.loop(0, rows)
        def _(i):
            to = pl.ds(pl.multiple_of(tile * own + i * cols, cols), cols)
            for b in range(span):
                for h in range(2):
                    high, low = split(stage[tile, h, i, pl.ds(span - 1 - b, cols), :])
                    s_high[b, to, h * width : (h + 1) * width] = high
                    s_low[b, to, h * width : (h + 1) * width] = low

    half = share // 2
    upper = lax.axis_index("col") % 2 == 1

    @pl.loop(0, span)
    def _(b):
        left = tuple(ref[...].reshape(span * double, total) for ref in (l_high, l_low))
        product = dot3(left, (s_high[b], s_low[b])) * factor
        for a in range(span):
            top = product[a * double : a * double + share]
            bottom = product[a * double + share : (a + 1) * double]
            real = top[:, :width] + bottom[:, width:]
            imag = bottom[:, :width] - top[:, width:]
            for c, value in enumerate((real, imag)):
                mine_ref[a, b, c] = jnp.where(upper, value[half:], value[:half])
                other_ref[a, b, c] = jnp.where(upper, value[:half], value[half:])


def correlate(shares, twin_shares, pieces, own_twin, twins, rows, cols, span, factor):
    peers = 2 * len(shares)
    reach = span // 2
    double, own = twin_shares.shape[1:]
    share = double // 2
    width = own_twin.shape[-1]
    total = peers * own
    side = round_up(reach * cols, 128)
    vmem = pl.BlockSpec(memory_space=pltpu.VMEM)
    hbm = pl.BlockSpec(memory_space=pl.ANY)
    out = jax.ShapeDtypeStruct((span, span, 2, share // 2, width), f32)
    return pl.pallas_call(
        functools.partial(correlate_kernel, (rows, cols, span, peers), factor),
        in_specs=[vmem] * (peers // 2) + [hbm] * (peers // 2) + [vmem, hbm, hbm],
        out_specs=[vmem, vmem],
        out_shape=[out, out],
        scratch_shapes=[
            pltpu.VMEM((peers, double, own), f32),
            pltpu.VMEM((double, total + 2 * side), f32),
            pltpu.VMEM((span, 2, share, total), bf16),
            pltpu.VMEM((span, 2, share, total), bf16),
            pltpu.VMEM((peers,) + own_twin.shape, f32),
            pltpu.VMEM((span, total, 2 * width), bf16),
            pltpu.VMEM((span, total, 2 * width), bf16),
            pltpu.SemaphoreType.DMA((2, peers // 2)),
        ],
        cost_estimate=pl.CostEstimate(
            flops=6 * span * double * total * span * 2 * width,
            bytes_accessed=4 * (2 * out.size + peers * own_twin.size),
            transcendentals=0,
        ),
        compiler_params=pltpu.CompilerParams(vmem_limit_bytes=VMEM_LIMIT),
        name="correlate",
    )(*shares, *pieces, twin_shares, own_twin, twins)


def swap(value, axis, first):
    pairs = []
    for low in range(first, lax.axis_size(axis) - 1, 2):
        pairs += [(low, low + 1), (low + 1, low)]
    if not pairs:
        return jnp.zeros_like(value)
    return lax.ppermute(value, axis, pairs)


def shifted(value, axis, shift):
    peers = lax.axis_size(axis)
    if shift % peers == 0:
        return value
    return lax.ppermute(value, axis, [(i, (i + shift) % peers) for i in range(peers)])


def edges(initial, last, axis):
    even = lax.axis_index(axis) % 2 == 0
    inner = swap(jnp.where(even, last, initial), axis, 0)
    outer = swap(jnp.where(even, initial, last), axis, 1)
    return jnp.where(even, outer, inner), jnp.where(even, inner, outer)


def on_device(adjoint_source, saved_currents, lag_blocks, element_inverse):
    rows, cols, parts, width = adjoint_source.shape
    span = lag_blocks.shape[0]
    reach = span // 2
    halo = SWEEPS * reach
    lanes = parts * width
    peers = lax.axis_size("row")

    initial = jnp.concatenate([adjoint_source[:, :halo], saved_currents[:, :reach]], axis=1)
    last = jnp.concatenate(
        [adjoint_source[:, cols - halo :], saved_currents[:, cols - reach :]], axis=1
    )
    before, after = edges(initial, last, "col")
    source = jnp.concatenate([before[:, :halo], adjoint_source, after[:, :halo]], axis=1)
    source = source.reshape(rows, cols + 2 * halo, lanes)
    saved = jnp.concatenate([before[:, halo:], saved_currents, after[:, halo:]], axis=1)
    before, after = edges(source[:halo], source[rows - halo :], "row")
    source = jnp.concatenate([before, source, after], axis=0)
    wide = round_up(cols + 2 * halo, 8)
    source = jnp.pad(source, ((0, 0), (0, wide - cols - 2 * halo), (0, 0)))

    pitch = round_up(cols + 2 * reach, 8)
    saved = jnp.pad(saved.transpose(2, 0, 1, 3), ((0, 0), (0, 0), (0, pitch - cols - 2 * reach), (0, 0)))
    pieces = [shifted(saved, "row", k) for k in range(0, peers, 2)]
    own_twin = swap(saved, "row", 0)

    adjoint, sends = run_sweeps(source, element_inverse, lag_blocks, rows, cols, peers)
    twins, own_twin, sends = lax.optimization_barrier((jnp.stack(pieces[1:]), own_twin, sends))
    twins = swap(twins, "row", 0)
    shares = [shifted(send, "row", 2 * k) for k, send in enumerate(sends)]
    twin_shares = swap(jnp.stack([received[1] for received in shares]), "row", 0)

    elements = rows * peers * cols * lax.axis_size("col")
    factor = -1.0 / math.sqrt(elements)
    mine, other = correlate(shares, twin_shares, pieces, own_twin, twins, rows, cols, span, factor)
    mine = mine + swap(other, "col", 0)
    total = mine
    for k in range(2, lax.axis_size("col"), 2):
        total = total + shifted(mine, "col", k)
    twin = swap(total, "col", 0)
    even = lax.axis_index("col") % 2 == 0
    lag_grad = jnp.concatenate(
        [jnp.where(even, total, twin), jnp.where(even, twin, total)], axis=3
    )
    return (adjoint.reshape(adjoint_source.shape), lag_grad)


def solution(mesh):
    return jax.shard_map(
        on_device,
        mesh=mesh,
        in_specs=(P("row", "col", None, None), P("row", "col", None, None), P(), P()),
        out_specs=(P("row", "col", None, None), P(None, None, None, "row", None)),
        check_vma=False,
    )
```

```python
import functools
import math

import jax
import jax.numpy as jnp
from jax import lax
from jax.experimental import pallas as pl
from jax.experimental.pallas import tpu as pltpu
from jax.sharding import PartitionSpec as P

SWEEPS = 2

f32 = jnp.float32
bf16 = jnp.bfloat16


def split(value):
    high = value.astype(bf16)
    return high, (value - high.astype(f32)).astype(bf16)


def dot(left, right):
    return jnp.dot(left, right, preferred_element_type=f32)


def dot3(left, right):
    (left_high, left_low), (right_high, right_low) = left, right
    return dot(left_high, right_high) + dot(left_low, right_high) + dot(left_high, right_low)


def round_up(count, unit):
    return (count + unit - 1) // unit * unit


def store_block(ref, index, real, imag):
    width = real.shape[0]
    low, high = slice(0, width), slice(width, 2 * width)
    ref[index + (low, low)] = real
    ref[index + (low, high)] = -imag
    ref[index + (high, low)] = imag
    ref[index + (high, high)] = real


def inside(first_row, rows, cols, pitch, margin, tile_rows, tile_cols):
    at = lax.broadcasted_iota(jnp.int32, (rows * pitch, 1), 0)
    i = at // pitch
    j = at - i * pitch
    row = i + (first_row + lax.axis_index("row") * tile_rows - margin)
    col = j + (lax.axis_index("col") * tile_cols - margin)
    row_ok = (row >= 0) & (row < tile_rows * lax.axis_size("row"))
    col_ok = (col >= 0) & (col < tile_cols * lax.axis_size("col"))
    return row_ok & col_ok & (j < cols)


def store_inverse(inverse_ref, high_ref, low_ref):
    real_high, real_low = split(inverse_ref[0])
    imag_high, imag_low = split(inverse_ref[1])
    store_block(high_ref, (), real_high, imag_high)
    store_block(low_ref, (), real_low, imag_low)


def products(high, low, weight_high, weight_low):
    lanes = weight_high.shape[-1]
    weight_high = weight_high.reshape(-1, lanes)
    weight_low = weight_low.reshape(-1, lanes)
    return dot(high, weight_high) + dot(low, weight_high) + dot(high, weight_low)


def first_sweep_kernel(
    sizes,
    source_ref,
    inverse_ref,
    blocks_hbm,
    second_ref,
    own_source_ref,
    high_hbm,
    low_hbm,
    first,
    x_high,
    x_low,
    acc,
    raw,
    w_high,
    w_low,
    e_high,
    e_low,
    sems,
):
    rows, cols, span, pitch, wide = sizes
    reach = span // 2
    mid_rows, mid_cols = rows + 2 * reach, cols + 2 * reach
    full_rows = rows + 4 * reach
    lanes = source_ref.shape[-1]

    def block_copy(a):
        return pltpu.make_async_copy(blocks_hbm.at[a], raw.at[a], sems.at[0, a])

    def part_copies(a):
        return (
            pltpu.make_async_copy(w_high.at[a], high_hbm.at[a], sems.at[1, a]),
            pltpu.make_async_copy(w_low.at[a], low_hbm.at[a], sems.at[2, a]),
        )

    for a in range(span):
        block_copy(a).start()

    store_inverse(inverse_ref, e_high, e_low)

    def invert(value):
        return dot3(split(value), (e_high[...], e_low[...]))

    own_source_ref[...] = source_ref[2 * reach : 2 * reach + rows, pl.ds(2 * reach, cols), :]

    step_rows = 4

    @pl.loop(0, full_rows // step_rows)
    def _(s):
        at = pl.ds(s * step_rows, step_rows)
        piece = source_ref[at].reshape(step_rows * wide, lanes)
        first[at] = invert(piece).reshape(step_rows, wide, lanes)

    first[full_rows] = jnp.zeros((wide, lanes), f32)

    @pl.loop(0, full_rows // 2)
    def _(s):
        for odd in range(2):
            for b in range(span):
                value = first[pl.ds(2 * s + odd, 2), pl.ds(b, pitch), :]
                high, low = split(value.reshape(2 * pitch, lanes))
                to = pl.ds(pl.multiple_of(s * 2 * pitch, 2 * pitch), 2 * pitch)
                x_high[odd, to, b * lanes : (b + 1) * lanes] = high
                x_low[odd, to, b * lanes : (b + 1) * lanes] = low

    acc[...] = jnp.zeros_like(acc)

    @pl.loop(0, span)
    def _(a):
        block_copy(a).wait()

        @pl.loop(0, span)
        def _(b):
            real_high, real_low = split(raw[a, b, 0])
            imag_high, imag_low = split(raw[a, b, 1])
            store_block(w_high, (a, b), real_high, imag_high)
            store_block(w_low, (a, b), real_low, imag_low)

        for copy in part_copies(a):
            copy.start()
        at = pl.ds(pl.multiple_of((a // 2) * 2 * pitch, 2 * pitch), mid_rows * pitch)
        acc[...] += products(x_high[a % 2, at, :], x_low[a % 2, at, :], w_high[a], w_low[a])

    step_rows = 3

    @pl.loop(0, mid_rows // step_rows)
    def _(s):
        at = pl.ds(s * step_rows + reach, step_rows)
        count = step_rows * pitch
        flat = pl.ds(pl.multiple_of(s * count, 8), count)
        centre = first[at, pl.ds(reach, pitch), :].reshape(count, lanes)
        source = source_ref[at, pl.ds(reach, pitch), :].reshape(count, lanes)
        value = centre + invert(source - centre - acc[flat, :])
        mask = inside(s * step_rows, step_rows, mid_cols, pitch, reach, rows, cols)
        value = jnp.where(mask, value, 0.0)
        second_ref[pl.ds(s * step_rows, step_rows)] = value.reshape(step_rows, pitch, lanes)

    @pl.loop(0, span)
    def _(a):
        for copy in part_copies(a):
            copy.wait()


def first_sweep(source, inverse, lag_blocks, rows, cols):
    span = lag_blocks.shape[0]
    reach = span // 2
    lanes = source.shape[-1]
    wide = source.shape[1]
    pitch = round_up(cols + 2 * reach, 8)
    full_rows, mid_rows = rows + 4 * reach, rows + 2 * reach
    vmem = pl.BlockSpec(memory_space=pltpu.VMEM)
    hbm = pl.BlockSpec(memory_space=pltpu.HBM)
    weights = (span, span, lanes, lanes)
    return pl.pallas_call(
        functools.partial(first_sweep_kernel, (rows, cols, span, pitch, wide)),
        in_specs=[vmem, vmem, hbm],
        out_specs=[vmem, vmem, hbm, hbm],
        out_shape=[
            jax.ShapeDtypeStruct((mid_rows, pitch, lanes), f32),
            jax.ShapeDtypeStruct((rows, cols, lanes), f32),
            jax.ShapeDtypeStruct(weights, bf16),
            jax.ShapeDtypeStruct(weights, bf16),
        ],
        scratch_shapes=[
            pltpu.VMEM((full_rows + 1, wide, lanes), f32),
            pltpu.VMEM((2, full_rows * pitch, span * lanes), bf16),
            pltpu.VMEM((2, full_rows * pitch, span * lanes), bf16),
            pltpu.VMEM((mid_rows * pitch, lanes), f32),
            pltpu.VMEM(lag_blocks.shape, f32),
            pltpu.VMEM(weights, bf16),
            pltpu.VMEM(weights, bf16),
            pltpu.VMEM((lanes, lanes), bf16),
            pltpu.VMEM((lanes, lanes), bf16),
            pltpu.SemaphoreType.DMA((3, span)),
        ],
        cost_estimate=pl.CostEstimate(
            flops=6 * span * span * lanes * lanes * mid_rows * pitch,
            bytes_accessed=12 * lag_blocks.size,
            transcendentals=0,
        ),
        compiler_params=pltpu.CompilerParams(vmem_limit_bytes=40 * 1024 * 1024),
        name="first_sweep",
    )(source, inverse, lag_blocks)


def second_sweep_kernel(
    sizes,
    second_ref,
    source_ref,
    inverse_ref,
    high_hbm,
    low_hbm,
    adjoint_ref,
    *rest,
):
    rows, cols, span, peers = sizes
    sends = rest[: peers // 2]
    x_high, x_low, acc, turned, w_high, w_low, e_high, e_low, sems = rest[peers // 2 :]
    reach = span // 2
    mid_rows = rows + 2 * reach
    own = rows * cols
    lanes = source_ref.shape[-1]
    width = lanes // 2

    def part_copies(a):
        return (
            pltpu.make_async_copy(high_hbm.at[a], w_high.at[a], sems.at[0, a]),
            pltpu.make_async_copy(low_hbm.at[a], w_low.at[a], sems.at[1, a]),
        )

    for a in range(span):
        for copy in part_copies(a):
            copy.start()

    store_inverse(inverse_ref, e_high, e_low)

    @pl.loop(0, mid_rows)
    def _(i):
        for b in range(span):
            high, low = split(second_ref[i, pl.ds(b, cols), :])
            to = pl.ds(pl.multiple_of(i * cols, cols), cols)
            x_high[to, b * lanes : (b + 1) * lanes] = high
            x_low[to, b * lanes : (b + 1) * lanes] = low

    acc[...] = jnp.zeros_like(acc)

    @pl.loop(0, span)
    def _(a):
        for copy in part_copies(a):
            copy.wait()
        at = pl.ds(pl.multiple_of(a * cols, cols), own)
        acc[...] += products(x_high[at, :], x_low[at, :], w_high[a], w_low[a])

    centre = second_ref[reach : reach + rows, pl.ds(reach, cols), :].reshape(own, lanes)
    source = source_ref[...].reshape(own, lanes)
    value = centre + dot3(split(source - centre - acc[...]), (e_high[...], e_low[...]))
    adjoint_ref[...] = value.reshape(adjoint_ref.shape)
    turned[...] = value.T

    share = width // peers
    me = lax.axis_index("row")
    twin = me + 1 - 2 * lax.rem(me, 2)
    for k in range(peers // 2):
        for n, target in enumerate((me, twin)):
            peer = lax.rem(target + 2 * k, peers)
            for part in range(2):
                at = pl.multiple_of(part * width + peer * share, share)
                sends[k][n, part * share : (part + 1) * share, :] = turned[pl.ds(at, share), :]


def second_sweep(second, source, inverse, high, low, peers):
    span = high.shape[0]
    rows, cols, lanes = source.shape
    mid_rows = second.shape[0]
    share = lanes // 2 // peers
    vmem = pl.BlockSpec(memory_space=pltpu.VMEM)
    hbm = pl.BlockSpec(memory_space=pltpu.HBM)
    send = jax.ShapeDtypeStruct((2, 2 * share, rows * cols), f32)
    out = pl.pallas_call(
        functools.partial(second_sweep_kernel, (rows, cols, span, peers)),
        in_specs=[vmem, vmem, vmem, hbm, hbm],
        out_specs=[vmem] * (1 + peers // 2),
        out_shape=[jax.ShapeDtypeStruct((rows, cols, lanes), f32)] + [send] * (peers // 2),
        scratch_shapes=[
            pltpu.VMEM((mid_rows * cols, span * lanes), bf16),
            pltpu.VMEM((mid_rows * cols, span * lanes), bf16),
            pltpu.VMEM((rows * cols, lanes), f32),
            pltpu.VMEM((lanes, rows * cols), f32),
            pltpu.VMEM(high.shape, bf16),
            pltpu.VMEM(high.shape, bf16),
            pltpu.VMEM((lanes, lanes), bf16),
            pltpu.VMEM((lanes, lanes), bf16),
            pltpu.SemaphoreType.DMA((2, span)),
        ],
        cost_estimate=pl.CostEstimate(
            flops=6 * span * span * lanes * lanes * rows * cols,
            bytes_accessed=4 * high.size,
            transcendentals=0,
        ),
        compiler_params=pltpu.CompilerParams(vmem_limit_bytes=28 * 1024 * 1024),
        name="second_sweep",
    )(second, source, inverse, high, low)
    return out[0], out[1:]


def correlate_kernel(sizes, factor, *refs):
    rows, cols, span, peers = sizes
    half_peers = peers // 2
    shares, piece_refs = refs[:half_peers], refs[half_peers:peers]
    twin_shares_ref, own_twin_ref, early_ref, late_ref = refs[peers : peers + 4]
    mine_ref, other_ref = refs[peers + 4 : peers + 6]
    placed, flat, l_high, l_low, stage, s_high, s_low, sems = refs[peers + 6 :]
    reach = span // 2
    own = rows * cols
    double = shares[0].shape[1]
    share = double // 2
    width = stage.shape[-1]
    me = lax.axis_index("row")
    even = me - lax.rem(me, 2)
    odd = 1 - lax.rem(me, 2)

    def tiles(k):
        base = lax.rem(even - 2 * k + peers, peers)
        return base + 1 - odd, base + odd

    for k in range(half_peers):
        if k == 0:
            twin = own_twin_ref
        else:
            twin = late_ref if k == half_peers - 1 else early_ref.at[k - 1]
        for n, (source, tile) in enumerate(zip((piece_refs[k], twin), tiles(k))):
            pltpu.make_async_copy(source, stage.at[tile], sems.at[n, k]).start()
        first, second = tiles(k)
        placed[first] = shares[k][0]
        placed[second] = twin_shares_ref[k]

    total = peers * own
    side = round_up(reach * cols, 128)
    flat[:, :side] = jnp.zeros((double, side), f32)
    flat[:, side + total :] = jnp.zeros((double, side), f32)
    for tile in range(peers):
        flat[:, side + tile * own : side + (tile + 1) * own] = placed[tile]

    @pl.loop(0, 2)
    def _(part):
        rows_at = pl.ds(pl.multiple_of(part * share, 8), share)
        for a in range(span):
            start = side + (a - reach) * cols
            high, low = split(flat[rows_at, start : start + total])
            l_high[a, part] = high
            l_low[a, part] = low

    @pl.loop(0, peers)
    def _(at):
        n, k = lax.rem(at, 2), at // 2
        first, second = tiles(k)
        tile = jnp.where(n == 0, first, second)
        pltpu.make_async_copy(own_twin_ref, stage.at[tile], sems.at[n, k]).wait()

        @pl.loop(0, rows)
        def _(i):
            to = pl.ds(pl.multiple_of(tile * own + i * cols, cols), cols)
            for b in range(span):
                for h in range(2):
                    high, low = split(stage[tile, h, i, pl.ds(span - 1 - b, cols), :])
                    s_high[b, to, h * width : (h + 1) * width] = high
                    s_low[b, to, h * width : (h + 1) * width] = low

    half = share // 2
    upper = lax.axis_index("col") % 2 == 1

    @pl.loop(0, span)
    def _(b):
        left = tuple(ref[...].reshape(span * double, total) for ref in (l_high, l_low))
        product = dot3(left, (s_high[b], s_low[b])) * factor
        for a in range(span):
            top = product[a * double : a * double + share]
            bottom = product[a * double + share : (a + 1) * double]
            real = top[:, :width] + bottom[:, width:]
            imag = bottom[:, :width] - top[:, width:]
            for c, value in enumerate((real, imag)):
                mine_ref[a, b, c] = jnp.where(upper, value[half:], value[:half])
                other_ref[a, b, c] = jnp.where(upper, value[:half], value[half:])


def correlate(shares, twin_shares, pieces, twins, rows, cols, span, factor):
    peers = 2 * len(shares)
    reach = span // 2
    double, own = twin_shares.shape[1:]
    share = double // 2
    own_twin = twins[0]
    width = own_twin.shape[-1]
    total = peers * own
    side = round_up(reach * cols, 128)
    vmem = pl.BlockSpec(memory_space=pltpu.VMEM)
    hbm = pl.BlockSpec(memory_space=pltpu.HBM)
    out = jax.ShapeDtypeStruct((span, span, 2, share // 2, width), f32)
    return pl.pallas_call(
        functools.partial(correlate_kernel, (rows, cols, span, peers), factor),
        in_specs=[vmem] * (peers // 2) + [hbm] * (peers // 2) + [vmem, hbm, hbm, hbm],
        out_specs=[vmem, vmem],
        out_shape=[out, out],
        scratch_shapes=[
            pltpu.VMEM((peers, double, own), f32),
            pltpu.VMEM((double, total + 2 * side), f32),
            pltpu.VMEM((span, 2, share, total), bf16),
            pltpu.VMEM((span, 2, share, total), bf16),
            pltpu.VMEM((peers,) + own_twin.shape, f32),
            pltpu.VMEM((span, total, 2 * width), bf16),
            pltpu.VMEM((span, total, 2 * width), bf16),
            pltpu.SemaphoreType.DMA((2, peers // 2)),
        ],
        cost_estimate=pl.CostEstimate(
            flops=6 * span * double * total * span * 2 * width,
            bytes_accessed=4 * (2 * out.size + peers * own_twin.size),
            transcendentals=0,
        ),
        compiler_params=pltpu.CompilerParams(vmem_limit_bytes=28 * 1024 * 1024),
        name="correlate",
    )(*shares, *pieces, twin_shares, *twins)


def swap(value, axis, first):
    pairs = []
    for low in range(first, lax.axis_size(axis) - 1, 2):
        pairs += [(low, low + 1), (low + 1, low)]
    if not pairs:
        return jnp.zeros_like(value)
    return lax.ppermute(value, axis, pairs)


def shifted(value, axis, shift):
    peers = lax.axis_size(axis)
    if shift % peers == 0:
        return value
    return lax.ppermute(value, axis, [(i, (i + shift) % peers) for i in range(peers)])


def edges(initial, last, axis):
    even = lax.axis_index(axis) % 2 == 0
    inner = swap(jnp.where(even, last, initial), axis, 0)
    outer = swap(jnp.where(even, initial, last), axis, 1)
    return jnp.where(even, outer, inner), jnp.where(even, inner, outer)


def on_device(adjoint_source, saved_currents, lag_blocks, element_inverse):
    rows, cols, parts, width = adjoint_source.shape
    span = lag_blocks.shape[0]
    reach = span // 2
    halo = SWEEPS * reach
    lanes = parts * width
    peers = lax.axis_size("row")

    initial = jnp.concatenate([adjoint_source[:, :halo], saved_currents[:, :reach]], axis=1)
    last = jnp.concatenate(
        [adjoint_source[:, cols - halo :], saved_currents[:, cols - reach :]], axis=1
    )
    before, after = edges(initial, last, "col")
    source = jnp.concatenate([before[:, :halo], adjoint_source, after[:, :halo]], axis=1)
    source = source.reshape(rows, cols + 2 * halo, lanes)
    saved = jnp.concatenate([before[:, halo:], saved_currents, after[:, halo:]], axis=1)
    before, after = edges(source[:halo], source[rows - halo :], "row")
    source = jnp.concatenate([before, source, after], axis=0)
    wide = round_up(cols + 2 * halo, 8)
    source = jnp.pad(source, ((0, 0), (0, wide - cols - 2 * halo), (0, 0)))

    pitch = round_up(cols + 2 * reach, 8)
    saved = jnp.pad(saved.transpose(2, 0, 1, 3), ((0, 0), (0, 0), (0, pitch - cols - 2 * reach), (0, 0)))
    pieces = [shifted(saved, "row", k) for k in range(0, peers, 2)]
    own_twin = swap(saved, "row", 0)

    second, own_source, high, low = first_sweep(source, element_inverse, lag_blocks, rows, cols)
    second, own_twin, early = lax.optimization_barrier((second, own_twin, jnp.stack(pieces[1:-1])))
    early_twins = swap(early, "row", 0)
    adjoint, sends = second_sweep(second, own_source, element_inverse, high, low, peers)
    late, sends = lax.optimization_barrier((pieces[-1], sends))
    late_twin = swap(late, "row", 0)
    shares = [shifted(send, "row", 2 * k) for k, send in enumerate(sends)]
    twin_shares = swap(jnp.stack([received[1] for received in shares]), "row", 0)

    elements = rows * peers * cols * lax.axis_size("col")
    factor = -1.0 / math.sqrt(elements)
    mine, other = correlate(
        shares, twin_shares, pieces, (own_twin, early_twins, late_twin), rows, cols, span, factor
    )
    mine = mine + swap(other, "col", 0)
    total = mine
    for k in range(2, lax.axis_size("col"), 2):
        total = total + shifted(mine, "col", k)
    twin = swap(total, "col", 0)
    even = lax.axis_index("col") % 2 == 0
    lag_grad = jnp.concatenate(
        [jnp.where(even, total, twin), jnp.where(even, twin, total)], axis=3
    )
    return (adjoint.reshape(adjoint_source.shape), lag_grad)


def solution(mesh):
    return jax.shard_map(
        on_device,
        mesh=mesh,
        in_specs=(P("row", "col", None, None), P("row", "col", None, None), P(), P()),
        out_specs=(P("row", "col", None, None), P(None, None, None, "row", None)),
        check_vma=False,
    )
```

```python
import functools
import math

import jax
import jax.numpy as jnp
from jax import lax
from jax.experimental import pallas as pl
from jax.experimental.pallas import tpu as pltpu
from jax.sharding import PartitionSpec as P

SWEEPS = 2

f32 = jnp.float32
bf16 = jnp.bfloat16


def split(value):
    high = value.astype(bf16)
    return high, (value - high.astype(f32)).astype(bf16)


def dot(left, right):
    return jnp.dot(left, right, preferred_element_type=f32)


def dot3(left, right):
    (left_high, left_low), (right_high, right_low) = left, right
    return dot(left_high, right_high) + dot(left_low, right_high) + dot(left_high, right_low)


def round_up(count, unit):
    return (count + unit - 1) // unit * unit


def store_block(ref, index, real, imag):
    width = real.shape[0]
    low, high = slice(0, width), slice(width, 2 * width)
    ref[index + (low, low)] = real
    ref[index + (low, high)] = -imag
    ref[index + (high, low)] = imag
    ref[index + (high, high)] = real


def inside(first_row, rows, cols, pitch, margin, tile_rows, tile_cols):
    at = lax.broadcasted_iota(jnp.int32, (rows * pitch, 1), 0)
    i = at // pitch
    j = at - i * pitch
    row = i + (first_row + lax.axis_index("row") * tile_rows - margin)
    col = j + (lax.axis_index("col") * tile_cols - margin)
    row_ok = (row >= 0) & (row < tile_rows * lax.axis_size("row"))
    col_ok = (col >= 0) & (col < tile_cols * lax.axis_size("col"))
    return row_ok & col_ok & (j < cols)


def store_inverse(inverse_ref, high_ref, low_ref):
    real_high, real_low = split(inverse_ref[0])
    imag_high, imag_low = split(inverse_ref[1])
    store_block(high_ref, (), real_high, imag_high)
    store_block(low_ref, (), real_low, imag_low)


def products(high, low, weight_high, weight_low):
    lanes = weight_high.shape[-1]
    weight_high = weight_high.reshape(-1, lanes)
    weight_low = weight_low.reshape(-1, lanes)
    return dot(high, weight_high) + dot(low, weight_high) + dot(high, weight_low)


def first_sweep_kernel(
    sizes,
    source_ref,
    inverse_ref,
    blocks_hbm,
    second_ref,
    own_source_ref,
    w_high,
    w_low,
    first,
    x_high,
    x_low,
    acc,
    raw,
    e_high,
    e_low,
    sems,
):
    rows, cols, span, pitch, wide = sizes
    reach = span // 2
    mid_rows, mid_cols = rows + 2 * reach, cols + 2 * reach
    full_rows = rows + 4 * reach
    lanes = 2 * source_ref.shape[-1]

    def source_at(i, j):
        return jnp.concatenate([source_ref[0, i, j, :], source_ref[1, i, j, :]], axis=-1)

    def block_copy(a):
        return pltpu.make_async_copy(blocks_hbm.at[a], raw.at[a], sems.at[a])

    for a in range(span):
        block_copy(a).start()

    store_inverse(inverse_ref, e_high, e_low)

    def invert(value):
        return dot3(split(value), (e_high[...], e_low[...]))

    own_source_ref[...] = source_at(pl.ds(2 * reach, rows), pl.ds(2 * reach, cols))

    step_rows = 4

    @pl.loop(0, full_rows // step_rows)
    def _(s):
        at = pl.ds(s * step_rows, step_rows)
        piece = source_at(at, pl.ds(0, wide)).reshape(step_rows * wide, lanes)
        first[at] = invert(piece).reshape(step_rows, wide, lanes)

    first[full_rows] = jnp.zeros((wide, lanes), f32)

    @pl.loop(0, full_rows // 2)
    def _(s):
        for odd in range(2):
            for b in range(span):
                value = first[pl.ds(2 * s + odd, 2), pl.ds(b, pitch), :]
                high, low = split(value.reshape(2 * pitch, lanes))
                to = pl.ds(pl.multiple_of(s * 2 * pitch, 2 * pitch), 2 * pitch)
                x_high[odd, to, b * lanes : (b + 1) * lanes] = high
                x_low[odd, to, b * lanes : (b + 1) * lanes] = low

    acc[...] = jnp.zeros_like(acc)

    @pl.loop(0, span)
    def _(a):
        block_copy(a).wait()

        @pl.loop(0, span)
        def _(b):
            real_high, real_low = split(raw[a, b, 0])
            imag_high, imag_low = split(raw[a, b, 1])
            store_block(w_high, (a, b), real_high, imag_high)
            store_block(w_low, (a, b), real_low, imag_low)

        at = pl.ds(pl.multiple_of((a // 2) * 2 * pitch, 2 * pitch), mid_rows * pitch)
        acc[...] += products(x_high[a % 2, at, :], x_low[a % 2, at, :], w_high[a], w_low[a])

    step_rows = 3

    @pl.loop(0, mid_rows // step_rows)
    def _(s):
        at = pl.ds(s * step_rows + reach, step_rows)
        count = step_rows * pitch
        flat = pl.ds(pl.multiple_of(s * count, 8), count)
        centre = first[at, pl.ds(reach, pitch), :].reshape(count, lanes)
        source = source_at(at, pl.ds(reach, pitch)).reshape(count, lanes)
        value = centre + invert(source - centre - acc[flat, :])
        mask = inside(s * step_rows, step_rows, mid_cols, pitch, reach, rows, cols)
        value = jnp.where(mask, value, 0.0)
        second_ref[pl.ds(s * step_rows, step_rows)] = value.reshape(step_rows, pitch, lanes)


def first_sweep(source, inverse, lag_blocks, rows, cols):
    span = lag_blocks.shape[0]
    reach = span // 2
    lanes = 2 * source.shape[-1]
    wide = source.shape[2]
    pitch = round_up(cols + 2 * reach, 8)
    full_rows, mid_rows = rows + 4 * reach, rows + 2 * reach
    vmem = pl.BlockSpec(memory_space=pltpu.VMEM)
    hbm = pl.BlockSpec(memory_space=pltpu.HBM)
    weights = (span, span, lanes, lanes)
    return pl.pallas_call(
        functools.partial(first_sweep_kernel, (rows, cols, span, pitch, wide)),
        in_specs=[vmem, vmem, hbm],
        out_specs=[vmem] * 4,
        out_shape=[
            jax.ShapeDtypeStruct((mid_rows, pitch, lanes), f32),
            jax.ShapeDtypeStruct((rows, cols, lanes), f32),
            jax.ShapeDtypeStruct(weights, bf16),
            jax.ShapeDtypeStruct(weights, bf16),
        ],
        scratch_shapes=[
            pltpu.VMEM((full_rows + 1, wide, lanes), f32),
            pltpu.VMEM((2, full_rows * pitch, span * lanes), bf16),
            pltpu.VMEM((2, full_rows * pitch, span * lanes), bf16),
            pltpu.VMEM((mid_rows * pitch, lanes), f32),
            pltpu.VMEM(lag_blocks.shape, f32),
            pltpu.VMEM((lanes, lanes), bf16),
            pltpu.VMEM((lanes, lanes), bf16),
            pltpu.SemaphoreType.DMA((span,)),
        ],
        cost_estimate=pl.CostEstimate(
            flops=6 * span * span * lanes * lanes * mid_rows * pitch,
            bytes_accessed=12 * lag_blocks.size,
            transcendentals=0,
        ),
        compiler_params=pltpu.CompilerParams(vmem_limit_bytes=40 * 1024 * 1024),
        name="first_sweep",
    )(source, inverse, lag_blocks)


def second_sweep_kernel(
    sizes,
    second_ref,
    source_ref,
    inverse_ref,
    w_high,
    w_low,
    adjoint_ref,
    *rest,
):
    rows, cols, span, peers = sizes
    sends = rest[: peers // 2]
    x_high, x_low, acc, turned, e_high, e_low = rest[peers // 2 :]
    reach = span // 2
    mid_rows = rows + 2 * reach
    own = rows * cols
    lanes = source_ref.shape[-1]
    width = lanes // 2

    store_inverse(inverse_ref, e_high, e_low)

    @pl.loop(0, mid_rows)
    def _(i):
        for b in range(span):
            high, low = split(second_ref[i, pl.ds(b, cols), :])
            to = pl.ds(pl.multiple_of(i * cols, cols), cols)
            x_high[to, b * lanes : (b + 1) * lanes] = high
            x_low[to, b * lanes : (b + 1) * lanes] = low

    acc[...] = jnp.zeros_like(acc)

    @pl.loop(0, span)
    def _(a):
        at = pl.ds(pl.multiple_of(a * cols, cols), own)
        acc[...] += products(x_high[at, :], x_low[at, :], w_high[a], w_low[a])

    centre = second_ref[reach : reach + rows, pl.ds(reach, cols), :].reshape(own, lanes)
    source = source_ref[...].reshape(own, lanes)
    value = centre + dot3(split(source - centre - acc[...]), (e_high[...], e_low[...]))
    adjoint_ref[...] = value.reshape(adjoint_ref.shape)
    turned[...] = value.T

    share = width // peers
    me = lax.axis_index("row")
    twin = me + 1 - 2 * lax.rem(me, 2)
    for k in range(peers // 2):
        for n, target in enumerate((me, twin)):
            peer = lax.rem(target + 2 * k, peers)
            for part in range(2):
                at = pl.multiple_of(part * width + peer * share, share)
                sends[k][n, part * share : (part + 1) * share, :] = turned[pl.ds(at, share), :]


def second_sweep(second, source, inverse, high, low, peers):
    span = high.shape[0]
    rows, cols, lanes = source.shape
    mid_rows = second.shape[0]
    share = lanes // 2 // peers
    vmem = pl.BlockSpec(memory_space=pltpu.VMEM)
    send = jax.ShapeDtypeStruct((2, 2 * share, rows * cols), f32)
    out = pl.pallas_call(
        functools.partial(second_sweep_kernel, (rows, cols, span, peers)),
        in_specs=[vmem] * 5,
        out_specs=[vmem] * (1 + peers // 2),
        out_shape=[jax.ShapeDtypeStruct((rows, cols, lanes), f32)] + [send] * (peers // 2),
        scratch_shapes=[
            pltpu.VMEM((mid_rows * cols, span * lanes), bf16),
            pltpu.VMEM((mid_rows * cols, span * lanes), bf16),
            pltpu.VMEM((rows * cols, lanes), f32),
            pltpu.VMEM((lanes, rows * cols), f32),
            pltpu.VMEM((lanes, lanes), bf16),
            pltpu.VMEM((lanes, lanes), bf16),
        ],
        cost_estimate=pl.CostEstimate(
            flops=6 * span * span * lanes * lanes * rows * cols,
            bytes_accessed=4 * high.size,
            transcendentals=0,
        ),
        compiler_params=pltpu.CompilerParams(vmem_limit_bytes=28 * 1024 * 1024),
        name="second_sweep",
    )(second, source, inverse, high, low)
    return out[0], out[1:]


def correlate_kernel(sizes, factor, *refs):
    rows, cols, span, peers = sizes
    half_peers = peers // 2
    shares, piece_refs = refs[:half_peers], refs[half_peers:peers]
    twin_shares_ref, own_twin_ref, early_ref, late_ref = refs[peers : peers + 4]
    mine_ref, other_ref = refs[peers + 4 : peers + 6]
    placed, flat, l_high, l_low, stage, s_high, s_low, sems = refs[peers + 6 :]
    reach = span // 2
    own = rows * cols
    double = shares[0].shape[1]
    share = double // 2
    width = stage.shape[-1]
    me = lax.axis_index("row")
    even = me - lax.rem(me, 2)
    odd = 1 - lax.rem(me, 2)

    def tiles(k):
        base = lax.rem(even - 2 * k + peers, peers)
        return base + 1 - odd, base + odd

    for k in range(half_peers):
        if k == 0:
            twin = own_twin_ref
        else:
            twin = late_ref if k == half_peers - 1 else early_ref.at[k - 1]
        for n, (source, tile) in enumerate(zip((piece_refs[k], twin), tiles(k))):
            pltpu.make_async_copy(source, stage.at[tile], sems.at[n, k]).start()
        first, second = tiles(k)
        placed[first] = shares[k][0]
        placed[second] = twin_shares_ref[k]

    total = peers * own
    side = round_up(reach * cols, 128)
    flat[:, :side] = jnp.zeros((double, side), f32)
    flat[:, side + total :] = jnp.zeros((double, side), f32)
    for tile in range(peers):
        flat[:, side + tile * own : side + (tile + 1) * own] = placed[tile]

    @pl.loop(0, 2)
    def _(part):
        rows_at = pl.ds(pl.multiple_of(part * share, 8), share)
        for a in range(span):
            start = side + (a - reach) * cols
            high, low = split(flat[rows_at, start : start + total])
            l_high[a, part] = high
            l_low[a, part] = low

    @pl.loop(0, peers)
    def _(at):
        n, k = lax.rem(at, 2), at // 2
        first, second = tiles(k)
        tile = jnp.where(n == 0, first, second)
        pltpu.make_async_copy(own_twin_ref, stage.at[tile], sems.at[n, k]).wait()

        @pl.loop(0, rows)
        def _(i):
            to = pl.ds(pl.multiple_of(tile * own + i * cols, cols), cols)
            for b in range(span):
                for h in range(2):
                    high, low = split(stage[tile, h, i, pl.ds(span - 1 - b, cols), :])
                    s_high[b, to, h * width : (h + 1) * width] = high
                    s_low[b, to, h * width : (h + 1) * width] = low

    half = share // 2
    upper = lax.axis_index("col") % 2 == 1

    @pl.loop(0, span)
    def _(b):
        left = tuple(ref[...].reshape(span * double, total) for ref in (l_high, l_low))
        product = dot3(left, (s_high[b], s_low[b])) * factor
        for a in range(span):
            top = product[a * double : a * double + share]
            bottom = product[a * double + share : (a + 1) * double]
            real = top[:, :width] + bottom[:, width:]
            imag = bottom[:, :width] - top[:, width:]
            for c, value in enumerate((real, imag)):
                mine_ref[a, b, c] = jnp.where(upper, value[half:], value[:half])
                other_ref[a, b, c] = jnp.where(upper, value[:half], value[half:])


def correlate(shares, twin_shares, pieces, twins, rows, cols, span, factor):
    peers = 2 * len(shares)
    reach = span // 2
    double, own = twin_shares.shape[1:]
    share = double // 2
    own_twin = twins[0]
    width = own_twin.shape[-1]
    total = peers * own
    side = round_up(reach * cols, 128)
    vmem = pl.BlockSpec(memory_space=pltpu.VMEM)
    hbm = pl.BlockSpec(memory_space=pltpu.HBM)
    out = jax.ShapeDtypeStruct((span, span, 2, share // 2, width), f32)
    return pl.pallas_call(
        functools.partial(correlate_kernel, (rows, cols, span, peers), factor),
        in_specs=[vmem] * (peers // 2) + [hbm] * (peers // 2) + [vmem, hbm, hbm, hbm],
        out_specs=[vmem, vmem],
        out_shape=[out, out],
        scratch_shapes=[
            pltpu.VMEM((peers, double, own), f32),
            pltpu.VMEM((double, total + 2 * side), f32),
            pltpu.VMEM((span, 2, share, total), bf16),
            pltpu.VMEM((span, 2, share, total), bf16),
            pltpu.VMEM((peers,) + own_twin.shape, f32),
            pltpu.VMEM((span, total, 2 * width), bf16),
            pltpu.VMEM((span, total, 2 * width), bf16),
            pltpu.SemaphoreType.DMA((2, peers // 2)),
        ],
        cost_estimate=pl.CostEstimate(
            flops=6 * span * double * total * span * 2 * width,
            bytes_accessed=4 * (2 * out.size + peers * own_twin.size),
            transcendentals=0,
        ),
        compiler_params=pltpu.CompilerParams(vmem_limit_bytes=28 * 1024 * 1024),
        name="correlate",
    )(*shares, *pieces, twin_shares, *twins)


def swap(value, axis, first):
    pairs = []
    for low in range(first, lax.axis_size(axis) - 1, 2):
        pairs += [(low, low + 1), (low + 1, low)]
    if not pairs:
        return jnp.zeros_like(value)
    return lax.ppermute(value, axis, pairs)


def shifted(value, axis, shift):
    peers = lax.axis_size(axis)
    if shift % peers == 0:
        return value
    return lax.ppermute(value, axis, [(i, (i + shift) % peers) for i in range(peers)])


def edges(initial, last, axis):
    even = lax.axis_index(axis) % 2 == 0
    shape = initial.shape
    initial, last = (value.reshape(shape[0], -1, shape[-1]) for value in (initial, last))
    inner = jnp.where(even, last, initial)
    outer = swap(jnp.where(even, initial, last), axis, 1)
    if axis == "col":
        inner, outer = lax.optimization_barrier((inner, outer))
    inner = swap(inner, axis, 0)
    inner, outer = inner.reshape(shape), outer.reshape(shape)
    return jnp.where(even, outer, inner), jnp.where(even, inner, outer)


def on_device(adjoint_source, saved_currents, lag_blocks, element_inverse):
    rows, cols, parts, width = adjoint_source.shape
    span = lag_blocks.shape[0]
    reach = span // 2
    halo = SWEEPS * reach
    peers = lax.axis_size("row")

    source = adjoint_source.transpose(2, 0, 1, 3)
    saved = saved_currents.transpose(2, 0, 1, 3)
    initial = jnp.concatenate([source[:, :, :halo], saved[:, :, :reach]], axis=2)
    last = jnp.concatenate([source[:, :, cols - halo :], saved[:, :, cols - reach :]], axis=2)
    before, after = edges(initial, last, "col")
    source = jnp.concatenate([before[:, :, :halo], source, after[:, :, :halo]], axis=2)
    saved = jnp.concatenate([before[:, :, halo:], saved, after[:, :, halo:]], axis=2)
    before, after = edges(source[:, :halo], source[:, rows - halo :], "row")
    source = jnp.concatenate([before, source, after], axis=1)
    wide = round_up(cols + 2 * halo, 8)
    source = jnp.pad(source, ((0, 0), (0, 0), (0, wide - cols - 2 * halo), (0, 0)))

    pitch = round_up(cols + 2 * reach, 8)
    saved = jnp.pad(saved, ((0, 0), (0, 0), (0, pitch - cols - 2 * reach), (0, 0)))
    pieces = [shifted(saved, "row", k) for k in range(0, peers, 2)]
    own_twin = swap(saved, "row", 0)

    second, own_source, high, low = first_sweep(source, element_inverse, lag_blocks, rows, cols)
    second, own_twin, early = lax.optimization_barrier((second, own_twin, jnp.stack(pieces[1:-1])))
    early_twins = swap(early, "row", 0)
    adjoint, sends = second_sweep(second, own_source, element_inverse, high, low, peers)
    late, sends = lax.optimization_barrier((pieces[-1], sends))
    late_twin = swap(late, "row", 0)
    shares = [shifted(send, "row", 2 * k) for k, send in enumerate(sends)]
    twin_shares = swap(jnp.stack([received[1] for received in shares]), "row", 0)

    elements = rows * peers * cols * lax.axis_size("col")
    factor = -1.0 / math.sqrt(elements)
    mine, other = correlate(
        shares, twin_shares, pieces, (own_twin, early_twins, late_twin), rows, cols, span, factor
    )
    mine = mine + swap(other, "col", 0)
    total = mine
    for k in range(2, lax.axis_size("col"), 2):
        total = total + shifted(mine, "col", k)
    twin = swap(total, "col", 0)
    even = lax.axis_index("col") % 2 == 0
    lag_grad = jnp.concatenate(
        [jnp.where(even, total, twin), jnp.where(even, twin, total)], axis=3
    )
    return (adjoint.reshape(adjoint_source.shape), lag_grad)


def solution(mesh):
    return jax.shard_map(
        on_device,
        mesh=mesh,
        in_specs=(P("row", "col", None, None), P("row", "col", None, None), P(), P()),
        out_specs=(P("row", "col", None, None), P(None, None, None, "row", None)),
        check_vma=False,
    )
```

```python
import functools
import math

import jax
import jax.numpy as jnp
from jax import lax
from jax.experimental import pallas as pl
from jax.experimental.pallas import tpu as pltpu
from jax.sharding import PartitionSpec as P

SWEEPS = 2

f32 = jnp.float32
bf16 = jnp.bfloat16


def split(value):
    high = value.astype(bf16)
    return high, (value - high.astype(f32)).astype(bf16)


def dot(left, right):
    return jnp.dot(left, right, preferred_element_type=f32)


def dot3(left, right):
    (left_high, left_low), (right_high, right_low) = left, right
    return dot(left_high, right_high) + dot(left_low, right_high) + dot(left_high, right_low)


def round_up(count, unit):
    return (count + unit - 1) // unit * unit


def store_block(ref, index, real, imag):
    width = real.shape[0]
    low, high = slice(0, width), slice(width, 2 * width)
    ref[index + (low, low)] = real
    ref[index + (low, high)] = -imag
    ref[index + (high, low)] = imag
    ref[index + (high, high)] = real


def inside(first_row, rows, cols, pitch, margin, tile_rows, tile_cols):
    at = lax.broadcasted_iota(jnp.int32, (rows * pitch, 1), 0)
    i = at // pitch
    j = at - i * pitch
    row = i + (first_row + lax.axis_index("row") * tile_rows - margin)
    col = j + (lax.axis_index("col") * tile_cols - margin)
    row_ok = (row >= 0) & (row < tile_rows * lax.axis_size("row"))
    col_ok = (col >= 0) & (col < tile_cols * lax.axis_size("col"))
    return row_ok & col_ok & (j < cols)


def store_inverse(inverse_ref, high_ref, low_ref):
    real_high, real_low = split(inverse_ref[0])
    imag_high, imag_low = split(inverse_ref[1])
    store_block(high_ref, (), real_high, imag_high)
    store_block(low_ref, (), real_low, imag_low)


def products(high, low, weight_high, weight_low):
    lanes = weight_high.shape[-1]
    weight_high = weight_high.reshape(-1, lanes)
    weight_low = weight_low.reshape(-1, lanes)
    return dot(high, weight_high) + dot(low, weight_high) + dot(high, weight_low)


def weights_kernel(blocks_hbm, w_high, w_low, raw, sems):
    span = blocks_hbm.shape[0]

    def block_copy(a):
        return pltpu.make_async_copy(blocks_hbm.at[a], raw.at[a], sems.at[a])

    for a in range(span):
        block_copy(a).start()

    @pl.loop(0, span)
    def _(a):
        block_copy(a).wait()

        @pl.loop(0, span)
        def _(b):
            real_high, real_low = split(raw[a, b, 0])
            imag_high, imag_low = split(raw[a, b, 1])
            store_block(w_high, (a, b), real_high, imag_high)
            store_block(w_low, (a, b), real_low, imag_low)


def prepare_weights(lag_blocks):
    span, _, parts, width, _ = lag_blocks.shape
    vmem = pl.BlockSpec(memory_space=pltpu.VMEM)
    out = jax.ShapeDtypeStruct((span, span, parts * width, parts * width), bf16)
    return pl.pallas_call(
        weights_kernel,
        in_specs=[pl.BlockSpec(memory_space=pltpu.HBM)],
        out_specs=[vmem, vmem],
        out_shape=[out, out],
        scratch_shapes=[
            pltpu.VMEM(lag_blocks.shape, f32),
            pltpu.SemaphoreType.DMA((span,)),
        ],
        cost_estimate=pl.CostEstimate(
            flops=0, bytes_accessed=4 * lag_blocks.size, transcendentals=0
        ),
        compiler_params=pltpu.CompilerParams(vmem_limit_bytes=28 * 1024 * 1024),
        name="weights",
    )(lag_blocks)


def first_sweep_kernel(
    sizes,
    source_ref,
    inverse_ref,
    w_high,
    w_low,
    second_ref,
    own_source_ref,
    first,
    x_high,
    x_low,
    acc,
    e_high,
    e_low,
):
    rows, cols, span, pitch, wide = sizes
    reach = span // 2
    mid_rows, mid_cols = rows + 2 * reach, cols + 2 * reach
    full_rows = rows + 4 * reach
    lanes = 2 * source_ref.shape[-1]

    def source_at(i, j):
        return jnp.concatenate([source_ref[0, i, j, :], source_ref[1, i, j, :]], axis=-1)

    store_inverse(inverse_ref, e_high, e_low)

    def invert(value):
        return dot3(split(value), (e_high[...], e_low[...]))

    own_source_ref[...] = source_at(pl.ds(2 * reach, rows), pl.ds(2 * reach, cols))

    step_rows = 4

    @pl.loop(0, full_rows // step_rows)
    def _(s):
        at = pl.ds(s * step_rows, step_rows)
        piece = source_at(at, pl.ds(0, wide)).reshape(step_rows * wide, lanes)
        first[at] = invert(piece).reshape(step_rows, wide, lanes)

    first[full_rows] = jnp.zeros((wide, lanes), f32)

    @pl.loop(0, full_rows // 2)
    def _(s):
        for odd in range(2):
            for b in range(span):
                value = first[pl.ds(2 * s + odd, 2), pl.ds(b, pitch), :]
                high, low = split(value.reshape(2 * pitch, lanes))
                to = pl.ds(pl.multiple_of(s * 2 * pitch, 2 * pitch), 2 * pitch)
                x_high[odd, to, b * lanes : (b + 1) * lanes] = high
                x_low[odd, to, b * lanes : (b + 1) * lanes] = low

    acc[...] = jnp.zeros_like(acc)

    @pl.loop(0, span)
    def _(a):
        at = pl.ds(pl.multiple_of((a // 2) * 2 * pitch, 2 * pitch), mid_rows * pitch)
        acc[...] += products(x_high[a % 2, at, :], x_low[a % 2, at, :], w_high[a], w_low[a])

    step_rows = 3

    @pl.loop(0, mid_rows // step_rows)
    def _(s):
        at = pl.ds(s * step_rows + reach, step_rows)
        count = step_rows * pitch
        flat = pl.ds(pl.multiple_of(s * count, 8), count)
        centre = first[at, pl.ds(reach, pitch), :].reshape(count, lanes)
        source = source_at(at, pl.ds(reach, pitch)).reshape(count, lanes)
        value = centre + invert(source - centre - acc[flat, :])
        mask = inside(s * step_rows, step_rows, mid_cols, pitch, reach, rows, cols)
        value = jnp.where(mask, value, 0.0)
        second_ref[pl.ds(s * step_rows, step_rows)] = value.reshape(step_rows, pitch, lanes)


def first_sweep(source, inverse, high, low, rows, cols):
    span = high.shape[0]
    reach = span // 2
    lanes = 2 * source.shape[-1]
    wide = source.shape[2]
    pitch = round_up(cols + 2 * reach, 8)
    full_rows, mid_rows = rows + 4 * reach, rows + 2 * reach
    vmem = pl.BlockSpec(memory_space=pltpu.VMEM)
    return pl.pallas_call(
        functools.partial(first_sweep_kernel, (rows, cols, span, pitch, wide)),
        in_specs=[vmem] * 4,
        out_specs=[vmem] * 2,
        out_shape=[
            jax.ShapeDtypeStruct((mid_rows, pitch, lanes), f32),
            jax.ShapeDtypeStruct((rows, cols, lanes), f32),
        ],
        scratch_shapes=[
            pltpu.VMEM((full_rows + 1, wide, lanes), f32),
            pltpu.VMEM((2, full_rows * pitch, span * lanes), bf16),
            pltpu.VMEM((2, full_rows * pitch, span * lanes), bf16),
            pltpu.VMEM((mid_rows * pitch, lanes), f32),
            pltpu.VMEM((lanes, lanes), bf16),
            pltpu.VMEM((lanes, lanes), bf16),
        ],
        cost_estimate=pl.CostEstimate(
            flops=6 * span * span * lanes * lanes * mid_rows * pitch,
            bytes_accessed=4 * high.size,
            transcendentals=0,
        ),
        compiler_params=pltpu.CompilerParams(vmem_limit_bytes=40 * 1024 * 1024),
        name="first_sweep",
    )(source, inverse, high, low)


def second_sweep_kernel(
    sizes,
    second_ref,
    source_ref,
    inverse_ref,
    w_high,
    w_low,
    adjoint_ref,
    *rest,
):
    rows, cols, span, peers = sizes
    sends = rest[: peers // 2]
    x_high, x_low, acc, turned, e_high, e_low = rest[peers // 2 :]
    reach = span // 2
    mid_rows = rows + 2 * reach
    own = rows * cols
    lanes = source_ref.shape[-1]
    width = lanes // 2

    store_inverse(inverse_ref, e_high, e_low)

    @pl.loop(0, mid_rows)
    def _(i):
        for b in range(span):
            high, low = split(second_ref[i, pl.ds(b, cols), :])
            to = pl.ds(pl.multiple_of(i * cols, cols), cols)
            x_high[to, b * lanes : (b + 1) * lanes] = high
            x_low[to, b * lanes : (b + 1) * lanes] = low

    acc[...] = jnp.zeros_like(acc)

    @pl.loop(0, span)
    def _(a):
        at = pl.ds(pl.multiple_of(a * cols, cols), own)
        acc[...] += products(x_high[at, :], x_low[at, :], w_high[a], w_low[a])

    centre = second_ref[reach : reach + rows, pl.ds(reach, cols), :].reshape(own, lanes)
    source = source_ref[...].reshape(own, lanes)
    value = centre + dot3(split(source - centre - acc[...]), (e_high[...], e_low[...]))
    adjoint_ref[...] = value.reshape(adjoint_ref.shape)
    turned[...] = value.T

    share = width // peers
    me = lax.axis_index("row")
    twin = me + 1 - 2 * lax.rem(me, 2)
    for k in range(peers // 2):
        for n, target in enumerate((me, twin)):
            peer = lax.rem(target + 2 * k, peers)
            for part in range(2):
                at = pl.multiple_of(part * width + peer * share, share)
                sends[k][n, part * share : (part + 1) * share, :] = turned[pl.ds(at, share), :]


def second_sweep(second, source, inverse, high, low, peers):
    span = high.shape[0]
    rows, cols, lanes = source.shape
    mid_rows = second.shape[0]
    share = lanes // 2 // peers
    vmem = pl.BlockSpec(memory_space=pltpu.VMEM)
    send = jax.ShapeDtypeStruct((2, 2 * share, rows * cols), f32)
    out = pl.pallas_call(
        functools.partial(second_sweep_kernel, (rows, cols, span, peers)),
        in_specs=[vmem] * 5,
        out_specs=[vmem] * (1 + peers // 2),
        out_shape=[jax.ShapeDtypeStruct((rows, cols, lanes), f32)] + [send] * (peers // 2),
        scratch_shapes=[
            pltpu.VMEM((mid_rows * cols, span * lanes), bf16),
            pltpu.VMEM((mid_rows * cols, span * lanes), bf16),
            pltpu.VMEM((rows * cols, lanes), f32),
            pltpu.VMEM((lanes, rows * cols), f32),
            pltpu.VMEM((lanes, lanes), bf16),
            pltpu.VMEM((lanes, lanes), bf16),
        ],
        cost_estimate=pl.CostEstimate(
            flops=6 * span * span * lanes * lanes * rows * cols,
            bytes_accessed=4 * high.size,
            transcendentals=0,
        ),
        compiler_params=pltpu.CompilerParams(vmem_limit_bytes=28 * 1024 * 1024),
        name="second_sweep",
    )(second, source, inverse, high, low)
    return out[0], out[1:]


def correlate_kernel(sizes, factor, *refs):
    rows, cols, span, peers = sizes
    half_peers = peers // 2
    shares, piece_refs = refs[:half_peers], refs[half_peers:peers]
    twin_shares_ref, own_twin_ref, early_ref, late_ref = refs[peers : peers + 4]
    mine_ref, other_ref = refs[peers + 4 : peers + 6]
    placed, flat, l_high, l_low, stage, s_high, s_low, sems = refs[peers + 6 :]
    reach = span // 2
    own = rows * cols
    double = shares[0].shape[1]
    share = double // 2
    width = stage.shape[-1]
    me = lax.axis_index("row")
    even = me - lax.rem(me, 2)
    odd = 1 - lax.rem(me, 2)

    def tiles(k):
        base = lax.rem(even - 2 * k + peers, peers)
        return base + 1 - odd, base + odd

    for k in range(half_peers):
        twin = (own_twin_ref, early_ref)[k] if k < 2 else late_ref.at[k - 2]
        for n, (source, tile) in enumerate(zip((piece_refs[k], twin), tiles(k))):
            pltpu.make_async_copy(source, stage.at[tile], sems.at[n, k]).start()
        first, second = tiles(k)
        placed[first] = shares[k][0]
        placed[second] = twin_shares_ref[k]

    total = peers * own
    side = round_up(reach * cols, 128)
    flat[:, :side] = jnp.zeros((double, side), f32)
    flat[:, side + total :] = jnp.zeros((double, side), f32)
    for tile in range(peers):
        flat[:, side + tile * own : side + (tile + 1) * own] = placed[tile]

    @pl.loop(0, 2)
    def _(part):
        rows_at = pl.ds(pl.multiple_of(part * share, 8), share)
        for a in range(span):
            start = side + (a - reach) * cols
            high, low = split(flat[rows_at, start : start + total])
            l_high[a, part] = high
            l_low[a, part] = low

    @pl.loop(0, peers)
    def _(at):
        n, k = lax.rem(at, 2), at // 2
        first, second = tiles(k)
        tile = jnp.where(n == 0, first, second)
        pltpu.make_async_copy(own_twin_ref, stage.at[tile], sems.at[n, k]).wait()

        @pl.loop(0, rows)
        def _(i):
            to = pl.ds(pl.multiple_of(tile * own + i * cols, cols), cols)
            for b in range(span):
                for h in range(2):
                    high, low = split(stage[tile, h, i, pl.ds(span - 1 - b, cols), :])
                    s_high[b, to, h * width : (h + 1) * width] = high
                    s_low[b, to, h * width : (h + 1) * width] = low

    half = share // 2
    upper = lax.axis_index("col") % 2 == 1

    @pl.loop(0, span)
    def _(b):
        left = tuple(ref[...].reshape(span * double, total) for ref in (l_high, l_low))
        product = dot3(left, (s_high[b], s_low[b])) * factor
        for a in range(span):
            top = product[a * double : a * double + share]
            bottom = product[a * double + share : (a + 1) * double]
            real = top[:, :width] + bottom[:, width:]
            imag = bottom[:, :width] - top[:, width:]
            for c, value in enumerate((real, imag)):
                mine_ref[a, b, c] = jnp.where(upper, value[half:], value[:half])
                other_ref[a, b, c] = jnp.where(upper, value[:half], value[half:])


def correlate(shares, twin_shares, pieces, twins, rows, cols, span, factor):
    peers = 2 * len(shares)
    reach = span // 2
    double, own = twin_shares.shape[1:]
    share = double // 2
    own_twin = twins[0]
    width = own_twin.shape[-1]
    total = peers * own
    side = round_up(reach * cols, 128)
    vmem = pl.BlockSpec(memory_space=pltpu.VMEM)
    hbm = pl.BlockSpec(memory_space=pltpu.HBM)
    out = jax.ShapeDtypeStruct((span, span, 2, share // 2, width), f32)
    return pl.pallas_call(
        functools.partial(correlate_kernel, (rows, cols, span, peers), factor),
        in_specs=[vmem] * (peers // 2) + [hbm] * (peers // 2) + [vmem, hbm, hbm, hbm],
        out_specs=[vmem, vmem],
        out_shape=[out, out],
        scratch_shapes=[
            pltpu.VMEM((peers, double, own), f32),
            pltpu.VMEM((double, total + 2 * side), f32),
            pltpu.VMEM((span, 2, share, total), bf16),
            pltpu.VMEM((span, 2, share, total), bf16),
            pltpu.VMEM((peers,) + own_twin.shape, f32),
            pltpu.VMEM((span, total, 2 * width), bf16),
            pltpu.VMEM((span, total, 2 * width), bf16),
            pltpu.SemaphoreType.DMA((2, peers // 2)),
        ],
        cost_estimate=pl.CostEstimate(
            flops=6 * span * double * total * span * 2 * width,
            bytes_accessed=4 * (2 * out.size + peers * own_twin.size),
            transcendentals=0,
        ),
        compiler_params=pltpu.CompilerParams(vmem_limit_bytes=28 * 1024 * 1024),
        name="correlate",
    )(*shares, *pieces, twin_shares, *twins)


def swap(value, axis, first):
    pairs = []
    for low in range(first, lax.axis_size(axis) - 1, 2):
        pairs += [(low, low + 1), (low + 1, low)]
    if not pairs:
        return jnp.zeros_like(value)
    return lax.ppermute(value, axis, pairs)


def shifted(value, axis, shift):
    peers = lax.axis_size(axis)
    if shift % peers == 0:
        return value
    return lax.ppermute(value, axis, [(i, (i + shift) % peers) for i in range(peers)])


def edges(initial, last, axis, beside=()):
    even = lax.axis_index(axis) % 2 == 0
    shape = initial.shape
    initial, last = (value.reshape(shape[0], -1, shape[-1]) for value in (initial, last))
    inner = jnp.where(even, last, initial)
    outer = swap(jnp.where(even, initial, last), axis, 1)
    if beside:
        inner, outer, beside = lax.optimization_barrier((inner, outer, beside))
    inner = swap(inner, axis, 0)
    inner, outer = inner.reshape(shape), outer.reshape(shape)
    return jnp.where(even, outer, inner), jnp.where(even, inner, outer), beside or inner


def on_device(adjoint_source, saved_currents, lag_blocks, element_inverse):
    rows, cols, parts, width = adjoint_source.shape
    span = lag_blocks.shape[0]
    reach = span // 2
    halo = SWEEPS * reach
    peers = lax.axis_size("row")

    source = adjoint_source.transpose(2, 0, 1, 3)
    saved = saved_currents.transpose(2, 0, 1, 3)
    initial = jnp.concatenate([source[:, :, :halo], saved[:, :, :reach]], axis=2)
    last = jnp.concatenate([source[:, :, cols - halo :], saved[:, :, cols - reach :]], axis=2)
    weights = prepare_weights(lag_blocks)
    before, after, (high, low) = edges(initial, last, "col", tuple(weights))
    source = jnp.concatenate([before[:, :, :halo], source, after[:, :, :halo]], axis=2)
    saved = jnp.concatenate([before[:, :, halo:], saved, after[:, :, halo:]], axis=2)
    before, after, arrived = edges(source[:, :halo], source[:, rows - halo :], "row")
    source = jnp.concatenate([before, source, after], axis=1)
    wide = round_up(cols + 2 * halo, 8)
    source = jnp.pad(source, ((0, 0), (0, 0), (0, wide - cols - 2 * halo), (0, 0)))

    pitch = round_up(cols + 2 * reach, 8)
    saved = jnp.pad(saved, ((0, 0), (0, 0), (0, pitch - cols - 2 * reach), (0, 0)))
    pieces = [shifted(saved, "row", k) for k in range(0, peers, 2)]
    own_twin = swap(lax.optimization_barrier((saved, arrived))[0], "row", 0)

    second, own_source = first_sweep(source, element_inverse, high, low, rows, cols)
    second, own_twin, early = lax.optimization_barrier((second, own_twin, pieces[1]))
    early_twin = swap(early, "row", 0)
    adjoint, sends = second_sweep(second, own_source, element_inverse, high, low, peers)
    *late, early_twin, sends = lax.optimization_barrier((*pieces[2:], early_twin, sends))
    late_twins = swap(jnp.stack(late), "row", 0)
    shares = [shifted(send, "row", 2 * k) for k, send in enumerate(sends)]
    twin_shares = swap(jnp.stack([received[1] for received in shares]), "row", 0)

    elements = rows * peers * cols * lax.axis_size("col")
    factor = -1.0 / math.sqrt(elements)
    mine, other = correlate(
        shares, twin_shares, pieces, (own_twin, early_twin, late_twins), rows, cols, span, factor
    )
    mine = mine + swap(other, "col", 0)
    total = mine
    for k in range(2, lax.axis_size("col"), 2):
        total = total + shifted(mine, "col", k)
    twin = swap(total, "col", 0)
    even = lax.axis_index("col") % 2 == 0
    lag_grad = jnp.concatenate(
        [jnp.where(even, total, twin), jnp.where(even, twin, total)], axis=3
    )
    return (adjoint.reshape(adjoint_source.shape), lag_grad)


def solution(mesh):
    return jax.shard_map(
        on_device,
        mesh=mesh,
        in_specs=(P("row", "col", None, None), P("row", "col", None, None), P(), P()),
        out_specs=(P("row", "col", None, None), P(None, None, None, "row", None)),
        check_vma=False,
    )
```

```python
import functools
import math

import jax
import jax.numpy as jnp
from jax import lax
from jax.experimental import pallas as pl
from jax.experimental.pallas import tpu as pltpu
from jax.sharding import PartitionSpec as P

SWEEPS = 2

f32 = jnp.float32
bf16 = jnp.bfloat16


def split(value):
    high = value.astype(bf16)
    return high, (value - high.astype(f32)).astype(bf16)


def dot(left, right):
    return jnp.dot(left, right, preferred_element_type=f32)


def dot3(left, right):
    (left_high, left_low), (right_high, right_low) = left, right
    return dot(left_high, right_high) + dot(left_low, right_high) + dot(left_high, right_low)


def round_up(count, unit):
    return (count + unit - 1) // unit * unit


def store_block(ref, index, real, imag):
    width = real.shape[0]
    low, high = slice(0, width), slice(width, 2 * width)
    ref[index + (low, low)] = real
    ref[index + (low, high)] = -imag
    ref[index + (high, low)] = imag
    ref[index + (high, high)] = real


def inside(first_row, rows, cols, pitch, margin, tile_rows, tile_cols):
    at = lax.broadcasted_iota(jnp.int32, (rows * pitch, 1), 0)
    i = at // pitch
    j = at - i * pitch
    row = i + (first_row + lax.axis_index("row") * tile_rows - margin)
    col = j + (lax.axis_index("col") * tile_cols - margin)
    row_ok = (row >= 0) & (row < tile_rows * lax.axis_size("row"))
    col_ok = (col >= 0) & (col < tile_cols * lax.axis_size("col"))
    return row_ok & col_ok & (j < cols)


def store_inverse(inverse_ref, high_ref, low_ref):
    real_high, real_low = split(inverse_ref[0])
    imag_high, imag_low = split(inverse_ref[1])
    store_block(high_ref, (), real_high, imag_high)
    store_block(low_ref, (), real_low, imag_low)


def products(high, low, weight_high, weight_low):
    lanes = weight_high.shape[-1]
    weight_high = weight_high.reshape(-1, lanes)
    weight_low = weight_low.reshape(-1, lanes)
    return dot(high, weight_high) + dot(low, weight_high) + dot(high, weight_low)


def first_sweep_kernel(
    sizes,
    source_ref,
    inverse_ref,
    blocks_hbm,
    second_ref,
    own_source_ref,
    w_high,
    w_low,
    first,
    x_high,
    x_low,
    acc,
    raw,
    e_high,
    e_low,
    sems,
):
    rows, cols, span, pitch, wide = sizes
    reach = span // 2
    mid_rows, mid_cols = rows + 2 * reach, cols + 2 * reach
    full_rows = rows + 4 * reach
    lanes = 2 * source_ref.shape[-1]

    def source_at(i, j):
        return jnp.concatenate([source_ref[0, i, j, :], source_ref[1, i, j, :]], axis=-1)

    def block_copy(a):
        return pltpu.make_async_copy(blocks_hbm.at[a], raw.at[a], sems.at[a])

    for a in range(span):
        block_copy(a).start()

    store_inverse(inverse_ref, e_high, e_low)

    def invert(value):
        return dot3(split(value), (e_high[...], e_low[...]))

    own_source_ref[...] = source_at(pl.ds(2 * reach, rows), pl.ds(2 * reach, cols))

    step_rows = 4

    @pl.loop(0, full_rows // step_rows)
    def _(s):
        at = pl.ds(s * step_rows, step_rows)
        piece = source_at(at, pl.ds(0, wide)).reshape(step_rows * wide, lanes)
        first[at] = invert(piece).reshape(step_rows, wide, lanes)

    first[full_rows] = jnp.zeros((wide, lanes), f32)

    @pl.loop(0, full_rows // 2)
    def _(s):
        for odd in range(2):
            for b in range(span):
                value = first[pl.ds(2 * s + odd, 2), pl.ds(b, pitch), :]
                high, low = split(value.reshape(2 * pitch, lanes))
                to = pl.ds(pl.multiple_of(s * 2 * pitch, 2 * pitch), 2 * pitch)
                x_high[odd, to, b * lanes : (b + 1) * lanes] = high
                x_low[odd, to, b * lanes : (b + 1) * lanes] = low

    acc[...] = jnp.zeros_like(acc)

    @pl.loop(0, span)
    def _(a):
        block_copy(a).wait()

        @pl.loop(0, span)
        def _(b):
            real_high, real_low = split(raw[a, b, 0])
            imag_high, imag_low = split(raw[a, b, 1])
            store_block(w_high, (a, b), real_high, imag_high)
            store_block(w_low, (a, b), real_low, imag_low)

        at = pl.ds(pl.multiple_of((a // 2) * 2 * pitch, 2 * pitch), mid_rows * pitch)
        acc[...] += products(x_high[a % 2, at, :], x_low[a % 2, at, :], w_high[a], w_low[a])

    step_rows = 3

    @pl.loop(0, mid_rows // step_rows)
    def _(s):
        at = pl.ds(s * step_rows + reach, step_rows)
        count = step_rows * pitch
        flat = pl.ds(pl.multiple_of(s * count, 8), count)
        centre = first[at, pl.ds(reach, pitch), :].reshape(count, lanes)
        source = source_at(at, pl.ds(reach, pitch)).reshape(count, lanes)
        value = centre + invert(source - centre - acc[flat, :])
        mask = inside(s * step_rows, step_rows, mid_cols, pitch, reach, rows, cols)
        value = jnp.where(mask, value, 0.0)
        second_ref[pl.ds(s * step_rows, step_rows)] = value.reshape(step_rows, pitch, lanes)


def first_sweep(source, inverse, lag_blocks, rows, cols):
    span = lag_blocks.shape[0]
    reach = span // 2
    lanes = 2 * source.shape[-1]
    wide = source.shape[2]
    pitch = round_up(cols + 2 * reach, 8)
    full_rows, mid_rows = rows + 4 * reach, rows + 2 * reach
    vmem = pl.BlockSpec(memory_space=pltpu.VMEM)
    hbm = pl.BlockSpec(memory_space=pltpu.HBM)
    weights = (span, span, lanes, lanes)
    return pl.pallas_call(
        functools.partial(first_sweep_kernel, (rows, cols, span, pitch, wide)),
        in_specs=[vmem, vmem, hbm],
        out_specs=[vmem] * 4,
        out_shape=[
            jax.ShapeDtypeStruct((mid_rows, pitch, lanes), f32),
            jax.ShapeDtypeStruct((rows, cols, lanes), f32),
            jax.ShapeDtypeStruct(weights, bf16),
            jax.ShapeDtypeStruct(weights, bf16),
        ],
        scratch_shapes=[
            pltpu.VMEM((full_rows + 1, wide, lanes), f32),
            pltpu.VMEM((2, full_rows * pitch, span * lanes), bf16),
            pltpu.VMEM((2, full_rows * pitch, span * lanes), bf16),
            pltpu.VMEM((mid_rows * pitch, lanes), f32),
            pltpu.VMEM(lag_blocks.shape, f32),
            pltpu.VMEM((lanes, lanes), bf16),
            pltpu.VMEM((lanes, lanes), bf16),
            pltpu.SemaphoreType.DMA((span,)),
        ],
        cost_estimate=pl.CostEstimate(
            flops=6 * span * span * lanes * lanes * mid_rows * pitch,
            bytes_accessed=12 * lag_blocks.size,
            transcendentals=0,
        ),
        compiler_params=pltpu.CompilerParams(vmem_limit_bytes=40 * 1024 * 1024),
        name="first_sweep",
    )(source, inverse, lag_blocks)


def second_sweep_kernel(
    sizes,
    second_ref,
    source_ref,
    inverse_ref,
    w_high,
    w_low,
    adjoint_ref,
    *rest,
):
    rows, cols, span, peers = sizes
    sends = rest[: peers // 2]
    x_high, x_low, acc, turned, e_high, e_low = rest[peers // 2 :]
    reach = span // 2
    mid_rows = rows + 2 * reach
    own = rows * cols
    lanes = source_ref.shape[-1]
    width = lanes // 2

    store_inverse(inverse_ref, e_high, e_low)

    @pl.loop(0, mid_rows)
    def _(i):
        for b in range(span):
            high, low = split(second_ref[i, pl.ds(b, cols), :])
            to = pl.ds(pl.multiple_of(i * cols, cols), cols)
            x_high[to, b * lanes : (b + 1) * lanes] = high
            x_low[to, b * lanes : (b + 1) * lanes] = low

    acc[...] = jnp.zeros_like(acc)

    @pl.loop(0, span)
    def _(a):
        at = pl.ds(pl.multiple_of(a * cols, cols), own)
        acc[...] += products(x_high[at, :], x_low[at, :], w_high[a], w_low[a])

    centre = second_ref[reach : reach + rows, pl.ds(reach, cols), :].reshape(own, lanes)
    source = source_ref[...].reshape(own, lanes)
    value = centre + dot3(split(source - centre - acc[...]), (e_high[...], e_low[...]))
    adjoint_ref[...] = value.reshape(adjoint_ref.shape)
    turned[...] = value.T

    share = width // peers
    me = lax.axis_index("row")
    twin = me + 1 - 2 * lax.rem(me, 2)
    for k in range(peers // 2):
        for n, target in enumerate((me, twin)):
            peer = lax.rem(target + 2 * k, peers)
            for part in range(2):
                at = pl.multiple_of(part * width + peer * share, share)
                sends[k][n, part * share : (part + 1) * share, :] = turned[pl.ds(at, share), :]


def second_sweep(second, source, inverse, high, low, peers):
    span = high.shape[0]
    rows, cols, lanes = source.shape
    mid_rows = second.shape[0]
    share = lanes // 2 // peers
    vmem = pl.BlockSpec(memory_space=pltpu.VMEM)
    send = jax.ShapeDtypeStruct((2, 2 * share, rows * cols), f32)
    out = pl.pallas_call(
        functools.partial(second_sweep_kernel, (rows, cols, span, peers)),
        in_specs=[vmem] * 5,
        out_specs=[vmem] * (1 + peers // 2),
        out_shape=[jax.ShapeDtypeStruct((rows, cols, lanes), f32)] + [send] * (peers // 2),
        scratch_shapes=[
            pltpu.VMEM((mid_rows * cols, span * lanes), bf16),
            pltpu.VMEM((mid_rows * cols, span * lanes), bf16),
            pltpu.VMEM((rows * cols, lanes), f32),
            pltpu.VMEM((lanes, rows * cols), f32),
            pltpu.VMEM((lanes, lanes), bf16),
            pltpu.VMEM((lanes, lanes), bf16),
        ],
        cost_estimate=pl.CostEstimate(
            flops=6 * span * span * lanes * lanes * rows * cols,
            bytes_accessed=4 * high.size,
            transcendentals=0,
        ),
        compiler_params=pltpu.CompilerParams(vmem_limit_bytes=28 * 1024 * 1024),
        name="second_sweep",
    )(second, source, inverse, high, low)
    return out[0], out[1:]


def correlate_kernel(sizes, factor, *refs):
    rows, cols, span, peers = sizes
    half_peers = peers // 2
    shares, piece_refs = refs[:half_peers], refs[half_peers:peers]
    twin_shares_ref, own_twin_ref, early_ref, late_ref = refs[peers : peers + 4]
    mine_ref, other_ref = refs[peers + 4 : peers + 6]
    placed, flat, l_high, l_low, stage, s_high, s_low, sems = refs[peers + 6 :]
    reach = span // 2
    own = rows * cols
    double = shares[0].shape[1]
    share = double // 2
    width = stage.shape[-1]
    me = lax.axis_index("row")
    even = me - lax.rem(me, 2)
    odd = 1 - lax.rem(me, 2)

    def tiles(k):
        base = lax.rem(even - 2 * k + peers, peers)
        return base + 1 - odd, base + odd

    for k in range(half_peers):
        twin = (own_twin_ref, early_ref)[k] if k < 2 else late_ref.at[k - 2]
        for n, (source, tile) in enumerate(zip((piece_refs[k], twin), tiles(k))):
            pltpu.make_async_copy(source, stage.at[tile], sems.at[n, k]).start()
        first, second = tiles(k)
        placed[first] = shares[k][0]
        placed[second] = twin_shares_ref[k]

    total = peers * own
    side = round_up(reach * cols, 128)
    flat[:, :side] = jnp.zeros((double, side), f32)
    flat[:, side + total :] = jnp.zeros((double, side), f32)
    for tile in range(peers):
        flat[:, side + tile * own : side + (tile + 1) * own] = placed[tile]

    @pl.loop(0, 2)
    def _(part):
        rows_at = pl.ds(pl.multiple_of(part * share, 8), share)
        for a in range(span):
            start = side + (a - reach) * cols
            high, low = split(flat[rows_at, start : start + total])
            l_high[a, part] = high
            l_low[a, part] = low

    @pl.loop(0, peers)
    def _(at):
        n, k = lax.rem(at, 2), at // 2
        first, second = tiles(k)
        tile = jnp.where(n == 0, first, second)
        pltpu.make_async_copy(own_twin_ref, stage.at[tile], sems.at[n, k]).wait()

        @pl.loop(0, rows)
        def _(i):
            to = pl.ds(pl.multiple_of(tile * own + i * cols, cols), cols)
            for b in range(span):
                for h in range(2):
                    high, low = split(stage[tile, h, i, pl.ds(span - 1 - b, cols), :])
                    s_high[b, to, h * width : (h + 1) * width] = high
                    s_low[b, to, h * width : (h + 1) * width] = low

    half = share // 2
    upper = lax.axis_index("col") % 2 == 1

    @pl.loop(0, span)
    def _(b):
        left = tuple(ref[...].reshape(span * double, total) for ref in (l_high, l_low))
        product = dot3(left, (s_high[b], s_low[b])) * factor
        for a in range(span):
            top = product[a * double : a * double + share]
            bottom = product[a * double + share : (a + 1) * double]
            real = top[:, :width] + bottom[:, width:]
            imag = bottom[:, :width] - top[:, width:]
            for c, value in enumerate((real, imag)):
                mine_ref[a, b, c] = jnp.where(upper, value[half:], value[:half])
                other_ref[a, b, c] = jnp.where(upper, value[:half], value[half:])


def correlate(shares, twin_shares, pieces, twins, rows, cols, span, factor):
    peers = 2 * len(shares)
    reach = span // 2
    double, own = twin_shares.shape[1:]
    share = double // 2
    own_twin = twins[0]
    width = own_twin.shape[-1]
    total = peers * own
    side = round_up(reach * cols, 128)
    vmem = pl.BlockSpec(memory_space=pltpu.VMEM)
    hbm = pl.BlockSpec(memory_space=pltpu.HBM)
    out = jax.ShapeDtypeStruct((span, span, 2, share // 2, width), f32)
    return pl.pallas_call(
        functools.partial(correlate_kernel, (rows, cols, span, peers), factor),
        in_specs=[vmem] * (peers // 2) + [hbm] * (peers // 2) + [vmem, hbm, hbm, hbm],
        out_specs=[vmem, vmem],
        out_shape=[out, out],
        scratch_shapes=[
            pltpu.VMEM((peers, double, own), f32),
            pltpu.VMEM((double, total + 2 * side), f32),
            pltpu.VMEM((span, 2, share, total), bf16),
            pltpu.VMEM((span, 2, share, total), bf16),
            pltpu.VMEM((peers,) + own_twin.shape, f32),
            pltpu.VMEM((span, total, 2 * width), bf16),
            pltpu.VMEM((span, total, 2 * width), bf16),
            pltpu.SemaphoreType.DMA((2, peers // 2)),
        ],
        cost_estimate=pl.CostEstimate(
            flops=6 * span * double * total * span * 2 * width,
            bytes_accessed=4 * (2 * out.size + peers * own_twin.size),
            transcendentals=0,
        ),
        compiler_params=pltpu.CompilerParams(vmem_limit_bytes=28 * 1024 * 1024),
        name="correlate",
    )(*shares, *pieces, twin_shares, *twins)


def swap(value, axis, first):
    pairs = []
    for low in range(first, lax.axis_size(axis) - 1, 2):
        pairs += [(low, low + 1), (low + 1, low)]
    if not pairs:
        return jnp.zeros_like(value)
    return lax.ppermute(value, axis, pairs)


def shifted(value, axis, shift):
    peers = lax.axis_size(axis)
    if shift % peers == 0:
        return value
    return lax.ppermute(value, axis, [(i, (i + shift) % peers) for i in range(peers)])


def edges(initial, last, axis):
    even = lax.axis_index(axis) % 2 == 0
    shape = initial.shape
    initial, last = (value.reshape(shape[0], -1, shape[-1]) for value in (initial, last))
    inner = jnp.where(even, last, initial)
    outer = swap(jnp.where(even, initial, last), axis, 1)
    if axis == "col":
        inner, outer = lax.optimization_barrier((inner, outer))
    inner = swap(inner, axis, 0)
    inner, outer = inner.reshape(shape), outer.reshape(shape)
    return jnp.where(even, outer, inner), jnp.where(even, inner, outer), inner


def on_device(adjoint_source, saved_currents, lag_blocks, element_inverse):
    rows, cols, parts, width = adjoint_source.shape
    span = lag_blocks.shape[0]
    reach = span // 2
    halo = SWEEPS * reach
    peers = lax.axis_size("row")

    source = adjoint_source.transpose(2, 0, 1, 3)
    saved = saved_currents.transpose(2, 0, 1, 3)
    initial = jnp.concatenate([source[:, :, :halo], saved[:, :, :reach]], axis=2)
    last = jnp.concatenate([source[:, :, cols - halo :], saved[:, :, cols - reach :]], axis=2)
    before, after, _ = edges(initial, last, "col")
    source = jnp.concatenate([before[:, :, :halo], source, after[:, :, :halo]], axis=2)
    saved = jnp.concatenate([before[:, :, halo:], saved, after[:, :, halo:]], axis=2)
    before, after, arrived = edges(source[:, :halo], source[:, rows - halo :], "row")
    source = jnp.concatenate([before, source, after], axis=1)
    wide = round_up(cols + 2 * halo, 8)
    source = jnp.pad(source, ((0, 0), (0, 0), (0, wide - cols - 2 * halo), (0, 0)))

    pitch = round_up(cols + 2 * reach, 8)
    saved = jnp.pad(saved, ((0, 0), (0, 0), (0, pitch - cols - 2 * reach), (0, 0)))
    pieces = [shifted(saved, "row", k) for k in range(0, peers, 2)]
    own_twin = swap(lax.optimization_barrier((saved, arrived))[0], "row", 0)

    second, own_source, high, low = first_sweep(source, element_inverse, lag_blocks, rows, cols)
    second, own_twin, early = lax.optimization_barrier((second, own_twin, pieces[1]))
    early_twin = swap(early, "row", 0)
    adjoint, sends = second_sweep(second, own_source, element_inverse, high, low, peers)
    *late, early_twin, sends = lax.optimization_barrier((*pieces[2:], early_twin, sends))
    late_twins = swap(jnp.stack(late), "row", 0)
    shares = [shifted(send, "row", 2 * k) for k, send in enumerate(sends)]
    twin_shares = swap(jnp.stack([received[1] for received in shares]), "row", 0)

    elements = rows * peers * cols * lax.axis_size("col")
    factor = -1.0 / math.sqrt(elements)
    mine, other = correlate(
        shares, twin_shares, pieces, (own_twin, early_twin, late_twins), rows, cols, span, factor
    )
    mine = mine + swap(other, "col", 0)
    total = mine
    for k in range(2, lax.axis_size("col"), 2):
        total = total + shifted(mine, "col", k)
    twin = swap(total, "col", 0)
    even = lax.axis_index("col") % 2 == 0
    lag_grad = jnp.concatenate(
        [jnp.where(even, total, twin), jnp.where(even, twin, total)], axis=3
    )
    return (adjoint.reshape(adjoint_source.shape), lag_grad)


def solution(mesh):
    return jax.shard_map(
        on_device,
        mesh=mesh,
        in_specs=(P("row", "col", None, None), P("row", "col", None, None), P(), P()),
        out_specs=(P("row", "col", None, None), P(None, None, None, "row", None)),
        check_vma=False,
    )
```

```python
import functools
import math

import jax
import jax.numpy as jnp
from jax import lax
from jax.experimental import pallas as pl
from jax.experimental.pallas import tpu as pltpu
from jax.sharding import PartitionSpec as P

SWEEPS = 2

f32 = jnp.float32
bf16 = jnp.bfloat16


def split(value):
    high = value.astype(bf16)
    return high, (value - high.astype(f32)).astype(bf16)


def dot(left, right):
    return jnp.dot(left, right, preferred_element_type=f32)


def dot3(left, right):
    (left_high, left_low), (right_high, right_low) = left, right
    return dot(left_high, right_high) + dot(left_low, right_high) + dot(left_high, right_low)


def round_up(count, unit):
    return (count + unit - 1) // unit * unit


def store_block(ref, index, real, imag):
    width = real.shape[0]
    low, high = slice(0, width), slice(width, 2 * width)
    ref[index + (low, low)] = real
    ref[index + (low, high)] = -imag
    ref[index + (high, low)] = imag
    ref[index + (high, high)] = real


def inside(first_row, rows, cols, pitch, margin, tile_rows, tile_cols):
    at = lax.broadcasted_iota(jnp.int32, (rows * pitch, 1), 0)
    i = at // pitch
    j = at - i * pitch
    row = i + (first_row + lax.axis_index("row") * tile_rows - margin)
    col = j + (lax.axis_index("col") * tile_cols - margin)
    row_ok = (row >= 0) & (row < tile_rows * lax.axis_size("row"))
    col_ok = (col >= 0) & (col < tile_cols * lax.axis_size("col"))
    return row_ok & col_ok & (j < cols)


def store_inverse(inverse_ref, high_ref, low_ref):
    real_high, real_low = split(inverse_ref[0])
    imag_high, imag_low = split(inverse_ref[1])
    store_block(high_ref, (), real_high, imag_high)
    store_block(low_ref, (), real_low, imag_low)


def products(high, low, weight_high, weight_low):
    lanes = weight_high.shape[-1]
    weight_high = weight_high.reshape(-1, lanes)
    weight_low = weight_low.reshape(-1, lanes)
    return dot(high, weight_high) + dot(low, weight_high) + dot(high, weight_low)


def first_sweep_kernel(
    sizes,
    source_ref,
    inverse_ref,
    blocks_hbm,
    second_ref,
    own_source_ref,
    w_high,
    w_low,
    first,
    x_high,
    x_low,
    acc,
    raw,
    e_high,
    e_low,
    sems,
):
    rows, cols, span, pitch, wide = sizes
    reach = span // 2
    mid_rows, mid_cols = rows + 2 * reach, cols + 2 * reach
    full_rows = rows + 4 * reach
    lanes = 2 * source_ref.shape[-1]

    def source_at(i, j):
        return jnp.concatenate([source_ref[0, i, j, :], source_ref[1, i, j, :]], axis=-1)

    def block_copy(a):
        return pltpu.make_async_copy(blocks_hbm.at[a], raw.at[a], sems.at[a])

    for a in range(span):
        block_copy(a).start()

    store_inverse(inverse_ref, e_high, e_low)

    def invert(value):
        return dot3(split(value), (e_high[...], e_low[...]))

    own_source_ref[...] = source_at(pl.ds(2 * reach, rows), pl.ds(2 * reach, cols))

    step_rows = 4

    @pl.loop(0, full_rows // step_rows)
    def _(s):
        at = pl.ds(s * step_rows, step_rows)
        piece = source_at(at, pl.ds(0, wide)).reshape(step_rows * wide, lanes)
        first[at] = invert(piece).reshape(step_rows, wide, lanes)

    first[full_rows] = jnp.zeros((wide, lanes), f32)

    @pl.loop(0, full_rows // 2)
    def _(s):
        for odd in range(2):
            for b in range(span):
                value = first[pl.ds(2 * s + odd, 2), pl.ds(b, pitch), :]
                high, low = split(value.reshape(2 * pitch, lanes))
                to = pl.ds(pl.multiple_of(s * 2 * pitch, 2 * pitch), 2 * pitch)
                x_high[odd, to, b * lanes : (b + 1) * lanes] = high
                x_low[odd, to, b * lanes : (b + 1) * lanes] = low

    acc[...] = jnp.zeros_like(acc)

    @pl.loop(0, span)
    def _(a):
        block_copy(a).wait()

        @pl.loop(0, span)
        def _(b):
            real_high, real_low = split(raw[a, b, 0])
            imag_high, imag_low = split(raw[a, b, 1])
            store_block(w_high, (a, b), real_high, imag_high)
            store_block(w_low, (a, b), real_low, imag_low)

        at = pl.ds(pl.multiple_of((a // 2) * 2 * pitch, 2 * pitch), mid_rows * pitch)
        acc[...] += products(x_high[a % 2, at, :], x_low[a % 2, at, :], w_high[a], w_low[a])

    step_rows = 3

    @pl.loop(0, mid_rows // step_rows)
    def _(s):
        at = pl.ds(s * step_rows + reach, step_rows)
        count = step_rows * pitch
        flat = pl.ds(pl.multiple_of(s * count, 8), count)
        centre = first[at, pl.ds(reach, pitch), :].reshape(count, lanes)
        source = source_at(at, pl.ds(reach, pitch)).reshape(count, lanes)
        value = centre + invert(source - centre - acc[flat, :])
        mask = inside(s * step_rows, step_rows, mid_cols, pitch, reach, rows, cols)
        value = jnp.where(mask, value, 0.0)
        second_ref[pl.ds(s * step_rows, step_rows)] = value.reshape(step_rows, pitch, lanes)


def first_sweep(source, inverse, lag_blocks, rows, cols):
    span = lag_blocks.shape[0]
    reach = span // 2
    lanes = 2 * source.shape[-1]
    wide = source.shape[2]
    pitch = round_up(cols + 2 * reach, 8)
    full_rows, mid_rows = rows + 4 * reach, rows + 2 * reach
    vmem = pl.BlockSpec(memory_space=pltpu.VMEM)
    hbm = pl.BlockSpec(memory_space=pltpu.HBM)
    weights = (span, span, lanes, lanes)
    return pl.pallas_call(
        functools.partial(first_sweep_kernel, (rows, cols, span, pitch, wide)),
        in_specs=[vmem, vmem, hbm],
        out_specs=[vmem] * 4,
        out_shape=[
            jax.ShapeDtypeStruct((mid_rows, pitch, lanes), f32),
            jax.ShapeDtypeStruct((rows, cols, lanes), f32),
            jax.ShapeDtypeStruct(weights, bf16),
            jax.ShapeDtypeStruct(weights, bf16),
        ],
        scratch_shapes=[
            pltpu.VMEM((full_rows + 1, wide, lanes), f32),
            pltpu.VMEM((2, full_rows * pitch, span * lanes), bf16),
            pltpu.VMEM((2, full_rows * pitch, span * lanes), bf16),
            pltpu.VMEM((mid_rows * pitch, lanes), f32),
            pltpu.VMEM(lag_blocks.shape, f32),
            pltpu.VMEM((lanes, lanes), bf16),
            pltpu.VMEM((lanes, lanes), bf16),
            pltpu.SemaphoreType.DMA((span,)),
        ],
        cost_estimate=pl.CostEstimate(
            flops=6 * span * span * lanes * lanes * mid_rows * pitch,
            bytes_accessed=12 * lag_blocks.size,
            transcendentals=0,
        ),
        compiler_params=pltpu.CompilerParams(vmem_limit_bytes=40 * 1024 * 1024),
        name="first_sweep",
    )(source, inverse, lag_blocks)


def second_sweep_kernel(
    sizes,
    second_ref,
    source_ref,
    inverse_ref,
    w_high,
    w_low,
    adjoint_ref,
    *rest,
):
    rows, cols, span, peers = sizes
    sends = rest[: peers // 2]
    x_high, x_low, acc, turned, e_high, e_low = rest[peers // 2 :]
    reach = span // 2
    mid_rows = rows + 2 * reach
    own = rows * cols
    lanes = source_ref.shape[-1]
    width = lanes // 2

    store_inverse(inverse_ref, e_high, e_low)

    @pl.loop(0, mid_rows)
    def _(i):
        for b in range(span):
            high, low = split(second_ref[i, pl.ds(b, cols), :])
            to = pl.ds(pl.multiple_of(i * cols, cols), cols)
            x_high[to, b * lanes : (b + 1) * lanes] = high
            x_low[to, b * lanes : (b + 1) * lanes] = low

    acc[...] = jnp.zeros_like(acc)

    @pl.loop(0, span)
    def _(a):
        at = pl.ds(pl.multiple_of(a * cols, cols), own)
        acc[...] += products(x_high[at, :], x_low[at, :], w_high[a], w_low[a])

    centre = second_ref[reach : reach + rows, pl.ds(reach, cols), :].reshape(own, lanes)
    source = source_ref[...].reshape(own, lanes)
    value = centre + dot3(split(source - centre - acc[...]), (e_high[...], e_low[...]))
    adjoint_ref[...] = value.reshape(adjoint_ref.shape)
    turned[...] = value.T

    share = width // peers
    me = lax.axis_index("row")
    twin = me + 1 - 2 * lax.rem(me, 2)
    for k in range(peers // 2):
        for n, target in enumerate((me, twin)):
            peer = lax.rem(target + 2 * k, peers)
            for part in range(2):
                at = pl.multiple_of(part * width + peer * share, share)
                sends[k][n, part * share : (part + 1) * share, :] = turned[pl.ds(at, share), :]


def second_sweep(second, source, inverse, high, low, peers):
    span = high.shape[0]
    rows, cols, lanes = source.shape
    mid_rows = second.shape[0]
    share = lanes // 2 // peers
    vmem = pl.BlockSpec(memory_space=pltpu.VMEM)
    send = jax.ShapeDtypeStruct((2, 2 * share, rows * cols), f32)
    out = pl.pallas_call(
        functools.partial(second_sweep_kernel, (rows, cols, span, peers)),
        in_specs=[vmem] * 5,
        out_specs=[vmem] * (1 + peers // 2),
        out_shape=[jax.ShapeDtypeStruct((rows, cols, lanes), f32)] + [send] * (peers // 2),
        scratch_shapes=[
            pltpu.VMEM((mid_rows * cols, span * lanes), bf16),
            pltpu.VMEM((mid_rows * cols, span * lanes), bf16),
            pltpu.VMEM((rows * cols, lanes), f32),
            pltpu.VMEM((lanes, rows * cols), f32),
            pltpu.VMEM((lanes, lanes), bf16),
            pltpu.VMEM((lanes, lanes), bf16),
        ],
        cost_estimate=pl.CostEstimate(
            flops=6 * span * span * lanes * lanes * rows * cols,
            bytes_accessed=4 * high.size,
            transcendentals=0,
        ),
        compiler_params=pltpu.CompilerParams(vmem_limit_bytes=28 * 1024 * 1024),
        name="second_sweep",
    )(second, source, inverse, high, low)
    return out[0], out[1:]


def correlate_kernel(sizes, factor, *refs):
    rows, cols, span, peers = sizes
    half_peers = peers // 2
    shares, piece_refs = refs[:half_peers], refs[half_peers:peers]
    twin_shares_ref, own_twin_ref, early_ref, late_ref = refs[peers : peers + 4]
    mine_ref, other_ref = refs[peers + 4 : peers + 6]
    placed, flat, l_high, l_low, stage, s_high, s_low, sems = refs[peers + 6 :]
    reach = span // 2
    own = rows * cols
    double = shares[0].shape[1]
    share = double // 2
    width = stage.shape[-1]
    me = lax.axis_index("row")
    even = me - lax.rem(me, 2)
    odd = 1 - lax.rem(me, 2)

    def tiles(k):
        base = lax.rem(even - 2 * k + peers, peers)
        return base + 1 - odd, base + odd

    for k in range(half_peers):
        if k == 0:
            twin = own_twin_ref
        elif k in (1, half_peers - 1):
            twin = early_ref.at[0 if k == 1 else 1]
        else:
            twin = late_ref.at[k - 2]
        for n, (source, tile) in enumerate(zip((piece_refs[k], twin), tiles(k))):
            pltpu.make_async_copy(source, stage.at[tile], sems.at[n, k]).start()
        first, second = tiles(k)
        placed[first] = shares[k][0]
        placed[second] = twin_shares_ref[k]

    total = peers * own
    side = round_up(reach * cols, 128)
    flat[:, :side] = jnp.zeros((double, side), f32)
    flat[:, side + total :] = jnp.zeros((double, side), f32)
    for tile in range(peers):
        flat[:, side + tile * own : side + (tile + 1) * own] = placed[tile]

    @pl.loop(0, 2)
    def _(part):
        rows_at = pl.ds(pl.multiple_of(part * share, 8), share)
        for a in range(span):
            start = side + (a - reach) * cols
            high, low = split(flat[rows_at, start : start + total])
            l_high[a, part] = high
            l_low[a, part] = low

    @pl.loop(0, peers)
    def _(at):
        n, k = lax.rem(at, 2), at // 2
        first, second = tiles(k)
        tile = jnp.where(n == 0, first, second)
        pltpu.make_async_copy(own_twin_ref, stage.at[tile], sems.at[n, k]).wait()

        @pl.loop(0, rows)
        def _(i):
            to = pl.ds(pl.multiple_of(tile * own + i * cols, cols), cols)
            for b in range(span):
                for h in range(2):
                    start = i * (cols + span - 1) + span - 1 - b
                    high, low = split(stage[tile, h, pl.ds(start, cols), :])
                    s_high[b, to, h * width : (h + 1) * width] = high
                    s_low[b, to, h * width : (h + 1) * width] = low

    half = share // 2
    upper = lax.axis_index("col") % 2 == 1

    @pl.loop(0, span)
    def _(b):
        left = tuple(ref[...].reshape(span * double, total) for ref in (l_high, l_low))
        product = dot3(left, (s_high[b], s_low[b])) * factor
        for a in range(span):
            top = product[a * double : a * double + share]
            bottom = product[a * double + share : (a + 1) * double]
            real = top[:, :width] + bottom[:, width:]
            imag = bottom[:, :width] - top[:, width:]
            for c, value in enumerate((real, imag)):
                mine_ref[a, b, c] = jnp.where(upper, value[half:], value[:half])
                other_ref[a, b, c] = jnp.where(upper, value[:half], value[half:])


def correlate(shares, twin_shares, pieces, twins, rows, cols, span, factor):
    peers = 2 * len(shares)
    reach = span // 2
    double, own = twin_shares.shape[1:]
    share = double // 2
    own_twin = twins[0]
    width = own_twin.shape[-1]
    total = peers * own
    side = round_up(reach * cols, 128)
    vmem = pl.BlockSpec(memory_space=pltpu.VMEM)
    hbm = pl.BlockSpec(memory_space=pltpu.HBM)
    out = jax.ShapeDtypeStruct((span, span, 2, share // 2, width), f32)
    return pl.pallas_call(
        functools.partial(correlate_kernel, (rows, cols, span, peers), factor),
        in_specs=[vmem] * (peers // 2) + [hbm] * (peers // 2) + [vmem, hbm, hbm, hbm],
        out_specs=[vmem, vmem],
        out_shape=[out, out],
        scratch_shapes=[
            pltpu.VMEM((peers, double, own), f32),
            pltpu.VMEM((double, total + 2 * side), f32),
            pltpu.VMEM((span, 2, share, total), bf16),
            pltpu.VMEM((span, 2, share, total), bf16),
            pltpu.VMEM((peers,) + own_twin.shape, f32),
            pltpu.VMEM((span, total, 2 * width), bf16),
            pltpu.VMEM((span, total, 2 * width), bf16),
            pltpu.SemaphoreType.DMA((2, peers // 2)),
        ],
        cost_estimate=pl.CostEstimate(
            flops=6 * span * double * total * span * 2 * width,
            bytes_accessed=4 * (2 * out.size + peers * own_twin.size),
            transcendentals=0,
        ),
        compiler_params=pltpu.CompilerParams(vmem_limit_bytes=28 * 1024 * 1024),
        name="correlate",
    )(*shares, *pieces, twin_shares, *twins)


def swap(value, axis, first):
    pairs = []
    for low in range(first, lax.axis_size(axis) - 1, 2):
        pairs += [(low, low + 1), (low + 1, low)]
    if not pairs:
        return jnp.zeros_like(value)
    return lax.ppermute(value, axis, pairs)


def shifted(value, axis, shift):
    peers = lax.axis_size(axis)
    if shift % peers == 0:
        return value
    return lax.ppermute(value, axis, [(i, (i + shift) % peers) for i in range(peers)])


def edges(initial, last, axis, rider=None, beside=None):
    even = lax.axis_index(axis) % 2 == 0
    shape = initial.shape
    initial, last = (value.reshape(shape[0], -1, shape[-1]) for value in (initial, last))
    inner = jnp.where(even, last, initial)
    outer = swap(jnp.where(even, initial, last), axis, 1)
    count = inner.shape[1]
    if beside is None:
        inner = swap(jnp.concatenate([inner, rider], axis=1), axis, 0)
        inner, rider = inner[:, :count], inner[:, count:]
    else:
        inner, outer, rider = lax.optimization_barrier((inner, outer, beside))
        inner = swap(inner, axis, 0)
    inner = inner.reshape(shape)
    outer = outer.reshape(shape)
    return jnp.where(even, outer, inner), jnp.where(even, inner, outer), rider


def on_device(adjoint_source, saved_currents, lag_blocks, element_inverse):
    rows, cols, parts, width = adjoint_source.shape
    span = lag_blocks.shape[0]
    reach = span // 2
    halo = SWEEPS * reach
    peers = lax.axis_size("row")

    source = adjoint_source.transpose(2, 0, 1, 3)
    saved = saved_currents.transpose(2, 0, 1, 3)
    twin_own = swap(saved, "row", 0)
    initial = jnp.concatenate([source[:, :, :halo], saved[:, :, :reach]], axis=2)
    last = jnp.concatenate([source[:, :, cols - halo :], saved[:, :, cols - reach :]], axis=2)
    before, after, twin_own = edges(initial, last, "col", beside=twin_own)
    source = jnp.concatenate([before[:, :, :halo], source, after[:, :, :halo]], axis=2)
    saved = jnp.concatenate([before[:, :, halo:], saved, after[:, :, halo:]], axis=2)
    sides = jnp.concatenate([saved[:, :, :reach], saved[:, :, cols + reach :]], axis=2)
    twin_sides = sides.reshape(parts, -1, width)
    before, after, arrived = edges(source[:, :halo], source[:, rows - halo :], "row", twin_sides)
    source = jnp.concatenate([before, source, after], axis=1)
    wide = round_up(cols + 2 * halo, 8)
    source = jnp.pad(source, ((0, 0), (0, 0), (0, wide - cols - 2 * halo), (0, 0)))
    twin_sides = arrived.reshape(sides.shape)
    own_twin = jnp.concatenate([twin_sides[:, :, :reach], twin_own, twin_sides[:, :, reach:]], axis=2)
    own_twin = own_twin.reshape(parts, -1, width)

    saved = saved.reshape(parts, -1, width)
    pieces = [saved] + [None] * (peers // 2 - 1)
    middle = lax.optimization_barrier((saved, arrived))[0]
    for k in range(1, peers // 2):
        near = k in (1, peers // 2 - 1)
        pieces[k] = shifted(saved if near else middle, "row", 2 * k)

    second, own_source, high, low = first_sweep(source, element_inverse, lag_blocks, rows, cols)
    second, own_twin, early = lax.optimization_barrier((second, own_twin, jnp.stack([pieces[1], pieces[-1]])))
    early_twins = swap(early, "row", 0)
    adjoint, sends = second_sweep(second, own_source, element_inverse, high, low, peers)
    *late, sends = lax.optimization_barrier((*pieces[2:-1], sends))
    late_twins = swap(jnp.stack(late), "row", 0)
    shares = [shifted(send, "row", 2 * k) for k, send in enumerate(sends)]
    twin_shares = swap(jnp.stack([received[1] for received in shares]), "row", 0)

    elements = rows * peers * cols * lax.axis_size("col")
    factor = -1.0 / math.sqrt(elements)
    mine, other = correlate(
        shares, twin_shares, pieces, (own_twin, early_twins, late_twins), rows, cols, span, factor
    )
    mine = mine + swap(other, "col", 0)
    total = mine
    for k in range(2, lax.axis_size("col"), 2):
        total = total + shifted(mine, "col", k)
    twin = swap(total, "col", 0)
    even = lax.axis_index("col") % 2 == 0
    lag_grad = jnp.concatenate(
        [jnp.where(even, total, twin), jnp.where(even, twin, total)], axis=3
    )
    return (adjoint.reshape(adjoint_source.shape), lag_grad)


def solution(mesh):
    return jax.shard_map(
        on_device,
        mesh=mesh,
        in_specs=(P("row", "col", None, None), P("row", "col", None, None), P(), P()),
        out_specs=(P("row", "col", None, None), P(None, None, None, "row", None)),
        check_vma=False,
    )
```

```python
import functools
import math

import jax
import jax.numpy as jnp
from jax import lax
from jax.experimental import pallas as pl
from jax.experimental.pallas import tpu as pltpu
from jax.sharding import PartitionSpec as P

SWEEPS = 2

f32 = jnp.float32
bf16 = jnp.bfloat16


def split(value):
    high = value.astype(bf16)
    return high, (value - high.astype(f32)).astype(bf16)


def dot(left, right):
    return jnp.dot(left, right, preferred_element_type=f32)


def dot3(left, right):
    (left_high, left_low), (right_high, right_low) = left, right
    return dot(left_high, right_high) + dot(left_low, right_high) + dot(left_high, right_low)


def round_up(count, unit):
    return (count + unit - 1) // unit * unit


def store_block(ref, index, real, imag):
    width = real.shape[0]
    low, high = slice(0, width), slice(width, 2 * width)
    ref[index + (low, low)] = real
    ref[index + (low, high)] = -imag
    ref[index + (high, low)] = imag
    ref[index + (high, high)] = real


def inside(first_row, rows, cols, pitch, margin, tile_rows, tile_cols):
    at = lax.broadcasted_iota(jnp.int32, (rows * pitch, 1), 0)
    i = at // pitch
    j = at - i * pitch
    row = i + (first_row + lax.axis_index("row") * tile_rows - margin)
    col = j + (lax.axis_index("col") * tile_cols - margin)
    row_ok = (row >= 0) & (row < tile_rows * lax.axis_size("row"))
    col_ok = (col >= 0) & (col < tile_cols * lax.axis_size("col"))
    return row_ok & col_ok & (j < cols)


def store_inverse(inverse_ref, high_ref, low_ref):
    real_high, real_low = split(inverse_ref[0])
    imag_high, imag_low = split(inverse_ref[1])
    store_block(high_ref, (), real_high, imag_high)
    store_block(low_ref, (), real_low, imag_low)


def products(high, low, weight_high, weight_low):
    lanes = weight_high.shape[-1]
    weight_high = weight_high.reshape(-1, lanes)
    weight_low = weight_low.reshape(-1, lanes)
    return dot(high, weight_high) + dot(low, weight_high) + dot(high, weight_low)


def first_sweep_kernel(
    sizes,
    source_ref,
    inverse_ref,
    blocks_hbm,
    second_ref,
    own_source_ref,
    w_high,
    w_low,
    first,
    x_high,
    x_low,
    acc,
    raw,
    e_high,
    e_low,
    sems,
):
    rows, cols, span, pitch, wide = sizes
    reach = span // 2
    mid_rows, mid_cols = rows + 2 * reach, cols + 2 * reach
    full_rows = rows + 4 * reach
    lanes = 2 * source_ref.shape[-1]

    def source_at(i, j):
        return jnp.concatenate([source_ref[0, i, j, :], source_ref[1, i, j, :]], axis=-1)

    def block_copy(a):
        return pltpu.make_async_copy(blocks_hbm.at[a], raw.at[a], sems.at[a])

    for a in range(span):
        block_copy(a).start()

    store_inverse(inverse_ref, e_high, e_low)

    def invert(value):
        return dot3(split(value), (e_high[...], e_low[...]))

    own_source_ref[...] = source_at(pl.ds(2 * reach, rows), pl.ds(2 * reach, cols))

    step_rows = 4

    @pl.loop(0, full_rows // step_rows)
    def _(s):
        at = pl.ds(s * step_rows, step_rows)
        piece = source_at(at, pl.ds(0, wide)).reshape(step_rows * wide, lanes)
        first[at] = invert(piece).reshape(step_rows, wide, lanes)

    first[full_rows] = jnp.zeros((wide, lanes), f32)

    @pl.loop(0, full_rows // 2)
    def _(s):
        for odd in range(2):
            for b in range(span):
                value = first[pl.ds(2 * s + odd, 2), pl.ds(b, pitch), :]
                high, low = split(value.reshape(2 * pitch, lanes))
                to = pl.ds(pl.multiple_of(s * 2 * pitch, 2 * pitch), 2 * pitch)
                x_high[odd, to, b * lanes : (b + 1) * lanes] = high
                x_low[odd, to, b * lanes : (b + 1) * lanes] = low

    acc[...] = jnp.zeros_like(acc)

    @pl.loop(0, span)
    def _(a):
        block_copy(a).wait()

        @pl.loop(0, span)
        def _(b):
            real_high, real_low = split(raw[a, b, 0])
            imag_high, imag_low = split(raw[a, b, 1])
            store_block(w_high, (a, b), real_high, imag_high)
            store_block(w_low, (a, b), real_low, imag_low)

        at = pl.ds(pl.multiple_of((a // 2) * 2 * pitch, 2 * pitch), mid_rows * pitch)
        acc[...] += products(x_high[a % 2, at, :], x_low[a % 2, at, :], w_high[a], w_low[a])

    step_rows = 3

    @pl.loop(0, mid_rows // step_rows)
    def _(s):
        at = pl.ds(s * step_rows + reach, step_rows)
        count = step_rows * pitch
        flat = pl.ds(pl.multiple_of(s * count, 8), count)
        centre = first[at, pl.ds(reach, pitch), :].reshape(count, lanes)
        source = source_at(at, pl.ds(reach, pitch)).reshape(count, lanes)
        value = centre + invert(source - centre - acc[flat, :])
        mask = inside(s * step_rows, step_rows, mid_cols, pitch, reach, rows, cols)
        value = jnp.where(mask, value, 0.0)
        second_ref[pl.ds(s * step_rows, step_rows)] = value.reshape(step_rows, pitch, lanes)


def first_sweep(source, inverse, lag_blocks, rows, cols):
    span = lag_blocks.shape[0]
    reach = span // 2
    lanes = 2 * source.shape[-1]
    wide = source.shape[2]
    pitch = round_up(cols + 2 * reach, 8)
    full_rows, mid_rows = rows + 4 * reach, rows + 2 * reach
    vmem = pl.BlockSpec(memory_space=pltpu.VMEM)
    hbm = pl.BlockSpec(memory_space=pltpu.HBM)
    weights = (span, span, lanes, lanes)
    return pl.pallas_call(
        functools.partial(first_sweep_kernel, (rows, cols, span, pitch, wide)),
        in_specs=[vmem, vmem, hbm],
        out_specs=[vmem] * 4,
        out_shape=[
            jax.ShapeDtypeStruct((mid_rows, pitch, lanes), f32),
            jax.ShapeDtypeStruct((rows, cols, lanes), f32),
            jax.ShapeDtypeStruct(weights, bf16),
            jax.ShapeDtypeStruct(weights, bf16),
        ],
        scratch_shapes=[
            pltpu.VMEM((full_rows + 1, wide, lanes), f32),
            pltpu.VMEM((2, full_rows * pitch, span * lanes), bf16),
            pltpu.VMEM((2, full_rows * pitch, span * lanes), bf16),
            pltpu.VMEM((mid_rows * pitch, lanes), f32),
            pltpu.VMEM(lag_blocks.shape, f32),
            pltpu.VMEM((lanes, lanes), bf16),
            pltpu.VMEM((lanes, lanes), bf16),
            pltpu.SemaphoreType.DMA((span,)),
        ],
        cost_estimate=pl.CostEstimate(
            flops=6 * span * span * lanes * lanes * mid_rows * pitch,
            bytes_accessed=12 * lag_blocks.size,
            transcendentals=0,
        ),
        compiler_params=pltpu.CompilerParams(vmem_limit_bytes=40 * 1024 * 1024),
        name="first_sweep",
    )(source, inverse, lag_blocks)


def second_sweep_kernel(
    sizes,
    second_ref,
    source_ref,
    inverse_ref,
    w_high,
    w_low,
    adjoint_ref,
    *rest,
):
    rows, cols, span, peers = sizes
    sends = rest[: peers // 2]
    x_high, x_low, acc, turned, e_high, e_low = rest[peers // 2 :]
    reach = span // 2
    mid_rows = rows + 2 * reach
    own = rows * cols
    lanes = source_ref.shape[-1]
    width = lanes // 2

    store_inverse(inverse_ref, e_high, e_low)

    @pl.loop(0, mid_rows)
    def _(i):
        for b in range(span):
            high, low = split(second_ref[i, pl.ds(b, cols), :])
            to = pl.ds(pl.multiple_of(i * cols, cols), cols)
            x_high[to, b * lanes : (b + 1) * lanes] = high
            x_low[to, b * lanes : (b + 1) * lanes] = low

    acc[...] = jnp.zeros_like(acc)

    @pl.loop(0, span)
    def _(a):
        at = pl.ds(pl.multiple_of(a * cols, cols), own)
        acc[...] += products(x_high[at, :], x_low[at, :], w_high[a], w_low[a])

    centre = second_ref[reach : reach + rows, pl.ds(reach, cols), :].reshape(own, lanes)
    source = source_ref[...].reshape(own, lanes)
    value = centre + dot3(split(source - centre - acc[...]), (e_high[...], e_low[...]))
    adjoint_ref[...] = value.reshape(adjoint_ref.shape)
    turned[...] = value.T

    share = width // peers
    me = lax.axis_index("row")
    twin = me + 1 - 2 * lax.rem(me, 2)
    for k in range(peers // 2):
        for n, target in enumerate((me, twin)):
            peer = lax.rem(target + 2 * k, peers)
            for part in range(2):
                at = pl.multiple_of(part * width + peer * share, share)
                sends[k][n, part * share : (part + 1) * share, :] = turned[pl.ds(at, share), :]


def second_sweep(second, source, inverse, high, low, peers):
    span = high.shape[0]
    rows, cols, lanes = source.shape
    mid_rows = second.shape[0]
    share = lanes // 2 // peers
    vmem = pl.BlockSpec(memory_space=pltpu.VMEM)
    send = jax.ShapeDtypeStruct((2, 2 * share, rows * cols), f32)
    out = pl.pallas_call(
        functools.partial(second_sweep_kernel, (rows, cols, span, peers)),
        in_specs=[vmem] * 5,
        out_specs=[vmem] * (1 + peers // 2),
        out_shape=[jax.ShapeDtypeStruct((rows, cols, lanes), f32)] + [send] * (peers // 2),
        scratch_shapes=[
            pltpu.VMEM((mid_rows * cols, span * lanes), bf16),
            pltpu.VMEM((mid_rows * cols, span * lanes), bf16),
            pltpu.VMEM((rows * cols, lanes), f32),
            pltpu.VMEM((lanes, rows * cols), f32),
            pltpu.VMEM((lanes, lanes), bf16),
            pltpu.VMEM((lanes, lanes), bf16),
        ],
        cost_estimate=pl.CostEstimate(
            flops=6 * span * span * lanes * lanes * rows * cols,
            bytes_accessed=4 * high.size,
            transcendentals=0,
        ),
        compiler_params=pltpu.CompilerParams(vmem_limit_bytes=28 * 1024 * 1024),
        name="second_sweep",
    )(second, source, inverse, high, low)
    return out[0], out[1:]


def correlate_kernel(sizes, factor, *refs):
    rows, cols, span, peers = sizes
    half_peers = peers // 2
    shares, piece_refs = refs[:half_peers], refs[half_peers:peers]
    twin_shares_ref, own_twin_ref, early_ref, late_ref = refs[peers : peers + 4]
    mine_ref, other_ref = refs[peers + 4 : peers + 6]
    placed, flat, l_high, l_low, stage, s_high, s_low, sems = refs[peers + 6 :]
    reach = span // 2
    own = rows * cols
    double = shares[0].shape[1]
    share = double // 2
    width = stage.shape[-1]
    me = lax.axis_index("row")
    even = me - lax.rem(me, 2)
    odd = 1 - lax.rem(me, 2)

    def tiles(k):
        base = lax.rem(even - 2 * k + peers, peers)
        return base + 1 - odd, base + odd

    for k in range(half_peers):
        if k == 0:
            twin = own_twin_ref
        elif k in (1, half_peers - 1):
            twin = early_ref.at[0 if k == 1 else 1]
        else:
            twin = late_ref.at[k - 2]
        for n, (source, tile) in enumerate(zip((piece_refs[k], twin), tiles(k))):
            pltpu.make_async_copy(source, stage.at[tile], sems.at[n, k]).start()
        first, second = tiles(k)
        placed[first] = shares[k][0]
        placed[second] = twin_shares_ref[k]

    total = peers * own
    side = round_up(reach * cols, 128)
    flat[:, :side] = jnp.zeros((double, side), f32)
    flat[:, side + total :] = jnp.zeros((double, side), f32)
    for tile in range(peers):
        flat[:, side + tile * own : side + (tile + 1) * own] = placed[tile]

    @pl.loop(0, 2)
    def _(part):
        rows_at = pl.ds(pl.multiple_of(part * share, 8), share)
        for a in range(span):
            start = side + (a - reach) * cols
            high, low = split(flat[rows_at, start : start + total])
            l_high[a, part] = high
            l_low[a, part] = low

    @pl.loop(0, peers)
    def _(at):
        n, k = lax.rem(at, 2), at // 2
        first, second = tiles(k)
        tile = jnp.where(n == 0, first, second)
        pltpu.make_async_copy(own_twin_ref, stage.at[tile], sems.at[n, k]).wait()

        @pl.loop(0, rows)
        def _(i):
            to = pl.ds(pl.multiple_of(tile * own + i * cols, cols), cols)
            for b in range(span):
                for h in range(2):
                    start = i * (cols + span - 1) + span - 1 - b
                    high, low = split(stage[tile, h, pl.ds(start, cols), :])
                    s_high[b, to, h * width : (h + 1) * width] = high
                    s_low[b, to, h * width : (h + 1) * width] = low

    half = share // 2
    upper = lax.axis_index("col") % 2 == 1

    @pl.loop(0, span)
    def _(b):
        left = tuple(ref[...].reshape(span * double, total) for ref in (l_high, l_low))
        product = dot3(left, (s_high[b], s_low[b])) * factor
        for a in range(span):
            top = product[a * double : a * double + share]
            bottom = product[a * double + share : (a + 1) * double]
            real = top[:, :width] + bottom[:, width:]
            imag = bottom[:, :width] - top[:, width:]
            for c, value in enumerate((real, imag)):
                mine_ref[a, b, c] = jnp.where(upper, value[half:], value[:half])
                other_ref[a, b, c] = jnp.where(upper, value[:half], value[half:])


def correlate(shares, twin_shares, pieces, twins, rows, cols, span, factor):
    peers = 2 * len(shares)
    reach = span // 2
    double, own = twin_shares.shape[1:]
    share = double // 2
    own_twin = twins[0]
    width = own_twin.shape[-1]
    total = peers * own
    side = round_up(reach * cols, 128)
    vmem = pl.BlockSpec(memory_space=pltpu.VMEM)
    hbm = pl.BlockSpec(memory_space=pltpu.HBM)
    out = jax.ShapeDtypeStruct((span, span, 2, share // 2, width), f32)
    return pl.pallas_call(
        functools.partial(correlate_kernel, (rows, cols, span, peers), factor),
        in_specs=[vmem] * (peers // 2) + [hbm] * (peers // 2) + [vmem, hbm, hbm, hbm],
        out_specs=[vmem, vmem],
        out_shape=[out, out],
        scratch_shapes=[
            pltpu.VMEM((peers, double, own), f32),
            pltpu.VMEM((double, total + 2 * side), f32),
            pltpu.VMEM((span, 2, share, total), bf16),
            pltpu.VMEM((span, 2, share, total), bf16),
            pltpu.VMEM((peers,) + own_twin.shape, f32),
            pltpu.VMEM((span, total, 2 * width), bf16),
            pltpu.VMEM((span, total, 2 * width), bf16),
            pltpu.SemaphoreType.DMA((2, peers // 2)),
        ],
        cost_estimate=pl.CostEstimate(
            flops=6 * span * double * total * span * 2 * width,
            bytes_accessed=4 * (2 * out.size + peers * own_twin.size),
            transcendentals=0,
        ),
        compiler_params=pltpu.CompilerParams(vmem_limit_bytes=28 * 1024 * 1024),
        name="correlate",
    )(*shares, *pieces, twin_shares, *twins)


def swap(value, axis, first):
    pairs = []
    for low in range(first, lax.axis_size(axis) - 1, 2):
        pairs += [(low, low + 1), (low + 1, low)]
    if not pairs:
        return jnp.zeros_like(value)
    return lax.ppermute(value, axis, pairs)


def shifted(value, axis, shift):
    peers = lax.axis_size(axis)
    if shift % peers == 0:
        return value
    return lax.ppermute(value, axis, [(i, (i + shift) % peers) for i in range(peers)])


def edges(initial, last, axis, rider=None, beside=None):
    even = lax.axis_index(axis) % 2 == 0
    shape = initial.shape
    initial, last = (value.reshape(shape[0], -1, shape[-1]) for value in (initial, last))
    inner = jnp.where(even, last, initial)
    outer = swap(jnp.where(even, initial, last), axis, 1)
    count = inner.shape[1]
    if beside is None:
        inner = swap(jnp.concatenate([inner, rider], axis=1), axis, 0)
        inner, rider = inner[:, :count], inner[:, count:]
    else:
        inner, beside = lax.optimization_barrier((inner, beside))
        rider = swap(beside, "row", 0)
        inner, outer, rider = lax.optimization_barrier((inner, outer, rider))
        inner = swap(inner, axis, 0)
    inner = inner.reshape(shape)
    outer = outer.reshape(shape)
    return jnp.where(even, outer, inner), jnp.where(even, inner, outer), rider


def on_device(adjoint_source, saved_currents, lag_blocks, element_inverse):
    rows, cols, parts, width = adjoint_source.shape
    span = lag_blocks.shape[0]
    reach = span // 2
    halo = SWEEPS * reach
    peers = lax.axis_size("row")

    source = adjoint_source.transpose(2, 0, 1, 3)
    saved = saved_currents.transpose(2, 0, 1, 3)
    initial = jnp.concatenate([source[:, :, :halo], saved[:, :, :reach]], axis=2)
    last = jnp.concatenate([source[:, :, cols - halo :], saved[:, :, cols - reach :]], axis=2)
    before, after, twin_own = edges(initial, last, "col", beside=saved)
    source = jnp.concatenate([before[:, :, :halo], source, after[:, :, :halo]], axis=2)
    saved = jnp.concatenate([before[:, :, halo:], saved, after[:, :, halo:]], axis=2)
    sides = jnp.concatenate([saved[:, :, :reach], saved[:, :, cols + reach :]], axis=2)
    twin_sides = sides.reshape(parts, -1, width)
    before, after, arrived = edges(source[:, :halo], source[:, rows - halo :], "row", twin_sides)
    source = jnp.concatenate([before, source, after], axis=1)
    wide = round_up(cols + 2 * halo, 8)
    source = jnp.pad(source, ((0, 0), (0, 0), (0, wide - cols - 2 * halo), (0, 0)))
    twin_sides = arrived.reshape(sides.shape)
    own_twin = jnp.concatenate([twin_sides[:, :, :reach], twin_own, twin_sides[:, :, reach:]], axis=2)
    own_twin = own_twin.reshape(parts, -1, width)

    saved = saved.reshape(parts, -1, width)
    pieces = {0: saved}
    for k in sorted(range(1, peers // 2), key=lambda k: min(k, peers // 2 - k)):
        pieces[k] = shifted(saved, "row", 2 * k)
    pieces = [pieces[k] for k in range(peers // 2)]

    second, own_source, high, low = first_sweep(source, element_inverse, lag_blocks, rows, cols)
    second, own_twin, early = lax.optimization_barrier((second, own_twin, jnp.stack([pieces[1], pieces[-1]])))
    early_twins = swap(early, "row", 0)
    adjoint, sends = second_sweep(second, own_source, element_inverse, high, low, peers)
    *late, sends = lax.optimization_barrier((*pieces[2:-1], sends))
    late_twins = swap(jnp.stack(late), "row", 0)
    shares = [shifted(send, "row", 2 * k) for k, send in enumerate(sends)]
    twin_shares = swap(jnp.stack([received[1] for received in shares]), "row", 0)

    elements = rows * peers * cols * lax.axis_size("col")
    factor = -1.0 / math.sqrt(elements)
    mine, other = correlate(
        shares, twin_shares, pieces, (own_twin, early_twins, late_twins), rows, cols, span, factor
    )
    mine = mine + swap(other, "col", 0)
    total = mine
    for k in range(2, lax.axis_size("col"), 2):
        total = total + shifted(mine, "col", k)
    twin = swap(total, "col", 0)
    even = lax.axis_index("col") % 2 == 0
    lag_grad = jnp.concatenate(
        [jnp.where(even, total, twin), jnp.where(even, twin, total)], axis=3
    )
    return (adjoint.reshape(adjoint_source.shape), lag_grad)


def solution(mesh):
    return jax.shard_map(
        on_device,
        mesh=mesh,
        in_specs=(P("row", "col", None, None), P("row", "col", None, None), P(), P()),
        out_specs=(P("row", "col", None, None), P(None, None, None, "row", None)),
        check_vma=False,
    )
```

```python
import functools
import math

import jax
import jax.numpy as jnp
from jax import lax
from jax.experimental import pallas as pl
from jax.experimental.pallas import tpu as pltpu
from jax.sharding import PartitionSpec as P

SWEEPS = 2

f32 = jnp.float32
bf16 = jnp.bfloat16


def split(value):
    high = value.astype(bf16)
    return high, (value - high.astype(f32)).astype(bf16)


def dot(left, right):
    return jnp.dot(left, right, preferred_element_type=f32)


def dot3(left, right):
    (left_high, left_low), (right_high, right_low) = left, right
    return dot(left_high, right_high) + dot(left_low, right_high) + dot(left_high, right_low)


def round_up(count, unit):
    return (count + unit - 1) // unit * unit


def chip_along_z(z, shift, count):
    return (z + shift + count) % count


def store_block(ref, index, real, imag):
    width = real.shape[0]
    low, high = slice(0, width), slice(width, 2 * width)
    ref[index + (low, low)] = real
    ref[index + (low, high)] = -imag
    ref[index + (high, low)] = imag
    ref[index + (high, high)] = real


def inside(first_row, rows, cols, pitch, margin, tile_rows, tile_cols):
    at = lax.broadcasted_iota(jnp.int32, (rows * pitch, 1), 0)
    i = at // pitch
    j = at - i * pitch
    row = i + (first_row + lax.axis_index("row") * tile_rows - margin)
    col = j + (lax.axis_index("col") * tile_cols - margin)
    row_ok = (row >= 0) & (row < tile_rows * lax.axis_size("row"))
    col_ok = (col >= 0) & (col < tile_cols * lax.axis_size("col"))
    return row_ok & col_ok & (j < cols)


def store_inverse(inverse_ref, high_ref, low_ref):
    real_high, real_low = split(inverse_ref[0])
    imag_high, imag_low = split(inverse_ref[1])
    store_block(high_ref, (), real_high, imag_high)
    store_block(low_ref, (), real_low, imag_low)


def products(high, low, weight_high, weight_low):
    lanes = weight_high.shape[-1]
    weight_high = weight_high.reshape(-1, lanes)
    weight_low = weight_low.reshape(-1, lanes)
    return dot(high, weight_high) + dot(low, weight_high) + dot(high, weight_low)


def first_sweep_kernel(
    sizes,
    source_ref,
    inverse_ref,
    blocks_ref,
    second_ref,
    own_source_ref,
    w_high,
    w_low,
    first,
    x_high,
    x_low,
    acc,
    e_high,
    e_low,
):
    rows, cols, span, pitch, wide = sizes
    reach = span // 2
    mid_rows, mid_cols = rows + 2 * reach, cols + 2 * reach
    full_rows = rows + 4 * reach
    lanes = 2 * source_ref.shape[-1]

    def source_at(i, j):
        return jnp.concatenate([source_ref[0, i, j, :], source_ref[1, i, j, :]], axis=-1)

    store_inverse(inverse_ref, e_high, e_low)

    def invert(value):
        return dot3(split(value), (e_high[...], e_low[...]))

    own_source_ref[...] = source_at(pl.ds(2 * reach, rows), pl.ds(2 * reach, cols))

    step_rows = 4

    @pl.loop(0, full_rows // step_rows)
    def _(s):
        at = pl.ds(s * step_rows, step_rows)
        piece = source_at(at, pl.ds(0, wide)).reshape(step_rows * wide, lanes)
        first[at] = invert(piece).reshape(step_rows, wide, lanes)

    first[full_rows] = jnp.zeros((wide, lanes), f32)

    @pl.loop(0, full_rows // 2)
    def _(s):
        for odd in range(2):
            for b in range(span):
                value = first[pl.ds(2 * s + odd, 2), pl.ds(b, pitch), :]
                high, low = split(value.reshape(2 * pitch, lanes))
                to = pl.ds(pl.multiple_of(s * 2 * pitch, 2 * pitch), 2 * pitch)
                x_high[odd, to, b * lanes : (b + 1) * lanes] = high
                x_low[odd, to, b * lanes : (b + 1) * lanes] = low

    acc[...] = jnp.zeros_like(acc)

    @pl.loop(0, span)
    def _(a):
        for b in range(span):
            real_high, real_low = split(blocks_ref[a, b, 0])
            imag_high, imag_low = split(blocks_ref[a, b, 1])
            store_block(w_high, (a, b), real_high, imag_high)
            store_block(w_low, (a, b), real_low, imag_low)

        at = pl.ds(pl.multiple_of((a // 2) * 2 * pitch, 2 * pitch), mid_rows * pitch)
        acc[...] += products(x_high[a % 2, at, :], x_low[a % 2, at, :], w_high[a], w_low[a])

    step_rows = 3

    @pl.loop(0, mid_rows // step_rows)
    def _(s):
        at = pl.ds(s * step_rows + reach, step_rows)
        count = step_rows * pitch
        flat = pl.ds(pl.multiple_of(s * count, 8), count)
        centre = first[at, pl.ds(reach, pitch), :].reshape(count, lanes)
        source = source_at(at, pl.ds(reach, pitch)).reshape(count, lanes)
        value = centre + invert(source - centre - acc[flat, :])
        mask = inside(s * step_rows, step_rows, mid_cols, pitch, reach, rows, cols)
        value = jnp.where(mask, value, 0.0)
        second_ref[pl.ds(s * step_rows, step_rows)] = value.reshape(step_rows, pitch, lanes)


def first_sweep(source, inverse, lag_blocks, rows, cols):
    span = lag_blocks.shape[0]
    reach = span // 2
    lanes = 2 * source.shape[-1]
    wide = source.shape[2]
    pitch = round_up(cols + 2 * reach, 8)
    full_rows, mid_rows = rows + 4 * reach, rows + 2 * reach
    vmem = pl.BlockSpec(memory_space=pltpu.VMEM)
    weights = (span, span, lanes, lanes)
    return pl.pallas_call(
        functools.partial(first_sweep_kernel, (rows, cols, span, pitch, wide)),
        in_specs=[vmem] * 3,
        out_specs=[vmem] * 4,
        out_shape=[
            jax.ShapeDtypeStruct((mid_rows, pitch, lanes), f32),
            jax.ShapeDtypeStruct((rows, cols, lanes), f32),
            jax.ShapeDtypeStruct(weights, bf16),
            jax.ShapeDtypeStruct(weights, bf16),
        ],
        scratch_shapes=[
            pltpu.VMEM((full_rows + 1, wide, lanes), f32),
            pltpu.VMEM((2, full_rows * pitch, span * lanes), bf16),
            pltpu.VMEM((2, full_rows * pitch, span * lanes), bf16),
            pltpu.VMEM((mid_rows * pitch, lanes), f32),
            pltpu.VMEM((lanes, lanes), bf16),
            pltpu.VMEM((lanes, lanes), bf16),
        ],
        cost_estimate=pl.CostEstimate(
            flops=6 * span * span * lanes * lanes * mid_rows * pitch,
            bytes_accessed=12 * lag_blocks.size,
            transcendentals=0,
        ),
        compiler_params=pltpu.CompilerParams(vmem_limit_bytes=32 * 1024 * 1024),
        name="first_sweep",
    )(source, inverse, lag_blocks)


def second_sweep_kernel(
    sizes,
    second_ref,
    source_ref,
    inverse_ref,
    w_high,
    w_low,
    adjoint_ref,
    *rest,
):
    rows, cols, span, peers = sizes
    sends = rest[: peers // 2]
    x_high, x_low, acc, turned, e_high, e_low = rest[peers // 2 :]
    reach = span // 2
    mid_rows = rows + 2 * reach
    own = rows * cols
    lanes = source_ref.shape[-1]
    width = lanes // 2

    store_inverse(inverse_ref, e_high, e_low)

    @pl.loop(0, mid_rows)
    def _(i):
        for b in range(span):
            high, low = split(second_ref[i, pl.ds(b, cols), :])
            to = pl.ds(pl.multiple_of(i * cols, cols), cols)
            x_high[to, b * lanes : (b + 1) * lanes] = high
            x_low[to, b * lanes : (b + 1) * lanes] = low

    acc[...] = jnp.zeros_like(acc)

    @pl.loop(0, span)
    def _(a):
        at = pl.ds(pl.multiple_of(a * cols, cols), own)
        acc[...] += products(x_high[at, :], x_low[at, :], w_high[a], w_low[a])

    centre = second_ref[reach : reach + rows, pl.ds(reach, cols), :].reshape(own, lanes)
    source = source_ref[...].reshape(own, lanes)
    value = centre + dot3(split(source - centre - acc[...]), (e_high[...], e_low[...]))
    adjoint_ref[...] = value.reshape(adjoint_ref.shape)
    turned[...] = value.T

    share = width // peers
    me = lax.axis_index("row")
    parity = me % 2
    for k in range(peers // 2):
        base = 2 * chip_along_z(me // 2, k, peers // 2)
        for n, peer in enumerate((base + parity, base + 1 - parity)):
            for part in range(2):
                at = pl.multiple_of(part * width + peer * share, share)
                sends[k][n, part * share : (part + 1) * share, :] = turned[pl.ds(at, share), :]


def second_sweep(second, source, inverse, high, low, peers):
    span = high.shape[0]
    rows, cols, lanes = source.shape
    mid_rows = second.shape[0]
    share = lanes // 2 // peers
    vmem = pl.BlockSpec(memory_space=pltpu.VMEM)
    send = jax.ShapeDtypeStruct((2, 2 * share, rows * cols), f32)
    out = pl.pallas_call(
        functools.partial(second_sweep_kernel, (rows, cols, span, peers)),
        in_specs=[vmem] * 5,
        out_specs=[vmem] * (1 + peers // 2),
        out_shape=[jax.ShapeDtypeStruct((rows, cols, lanes), f32)] + [send] * (peers // 2),
        scratch_shapes=[
            pltpu.VMEM((mid_rows * cols, span * lanes), bf16),
            pltpu.VMEM((mid_rows * cols, span * lanes), bf16),
            pltpu.VMEM((rows * cols, lanes), f32),
            pltpu.VMEM((lanes, rows * cols), f32),
            pltpu.VMEM((lanes, lanes), bf16),
            pltpu.VMEM((lanes, lanes), bf16),
        ],
        cost_estimate=pl.CostEstimate(
            flops=6 * span * span * lanes * lanes * rows * cols,
            bytes_accessed=4 * high.size,
            transcendentals=0,
        ),
        compiler_params=pltpu.CompilerParams(vmem_limit_bytes=18 * 1024 * 1024),
        name="second_sweep",
    )(second, source, inverse, high, low)
    return out[0], out[1:]


def spread_kernel(sizes, *refs):
    rows, cols, span, peers = sizes
    half_peers = peers // 2
    piece_refs = refs[:half_peers]
    own_twin_ref, early_ref, late_ref, s_high, s_low, stage, sems = refs[half_peers:]
    own = rows * cols
    width = stage.shape[-1]
    me = lax.axis_index("row")
    parity = me % 2

    def tiles(k):
        base = 2 * chip_along_z(me // 2, -k, half_peers)
        return base + parity, base + 1 - parity

    for k in range(half_peers):
        if k == 0:
            twin = own_twin_ref
        else:
            near = k in (1, half_peers - 1)
            twin = early_ref.at[0 if k == 1 else 1] if near else late_ref.at[k - 2]
        for source, tile in zip((piece_refs[k], twin), tiles(k)):
            pltpu.make_async_copy(source, stage.at[tile], sems.at[tile]).start()

    @pl.loop(0, peers)
    def _(tile):
        pltpu.make_async_copy(own_twin_ref, stage.at[tile], sems.at[tile]).wait()

        @pl.loop(0, rows)
        def _(i):
            to = pl.ds(pl.multiple_of(tile * own + i * cols, cols), cols)
            for b in range(span):
                for h in range(2):
                    start = i * (cols + span - 1) + span - 1 - b
                    high, low = split(stage[tile, h, pl.ds(start, cols), :])
                    s_high[b, to, h * width : (h + 1) * width] = high
                    s_low[b, to, h * width : (h + 1) * width] = low


def spread(pieces, twins, rows, cols, span):
    peers = 2 * len(pieces)
    piece = pieces[0]
    vmem = pl.BlockSpec(memory_space=pltpu.VMEM)
    hbm = pl.BlockSpec(memory_space=pltpu.HBM)
    out = jax.ShapeDtypeStruct((span, peers * rows * cols, 2 * piece.shape[-1]), bf16)
    return pl.pallas_call(
        functools.partial(spread_kernel, (rows, cols, span, peers)),
        in_specs=[hbm] * (len(pieces) + len(twins)),
        out_specs=[vmem, vmem],
        out_shape=[out, out],
        scratch_shapes=[
            pltpu.VMEM((peers,) + piece.shape, f32),
            pltpu.SemaphoreType.DMA((peers,)),
        ],
        cost_estimate=pl.CostEstimate(
            flops=0, bytes_accessed=4 * peers * piece.size, transcendentals=0
        ),
        compiler_params=pltpu.CompilerParams(vmem_limit_bytes=15 * 1024 * 1024),
        name="spread",
    )(*pieces, *twins)


def correlate_kernel(sizes, lags, factor, *refs):
    rows, cols, span, peers = sizes
    half_peers = peers // 2
    shares = refs[:half_peers]
    twin_shares_ref, s_high, s_low, mine_ref, other_ref = refs[half_peers : half_peers + 5]
    placed, flat, l_high, l_low = refs[half_peers + 5 :]
    reach = span // 2
    own = rows * cols
    double = shares[0].shape[1]
    share = double // 2
    width = s_high.shape[-1] // 2
    me = lax.axis_index("row")
    parity = me % 2

    for k in range(half_peers):
        base = 2 * chip_along_z(me // 2, -k, half_peers)
        placed[base + parity] = shares[k][0]
        placed[base + 1 - parity] = twin_shares_ref[k]

    total = peers * own
    side = round_up(reach * cols, 128)
    flat[:, :side] = jnp.zeros((double, side), f32)
    flat[:, side + total :] = jnp.zeros((double, side), f32)
    for tile in range(peers):
        flat[:, side + tile * own : side + (tile + 1) * own] = placed[tile]

    @pl.loop(0, 2)
    def _(part):
        rows_at = pl.ds(pl.multiple_of(part * share, 8), share)
        for a in range(span):
            start = side + (a - reach) * cols
            high, low = split(flat[rows_at, start : start + total])
            l_high[a, part] = high
            l_low[a, part] = low

    half = share // 2
    upper = lax.axis_index("col") % 2 == 1
    first_lag, count = lags

    @pl.loop(0, count)
    def _(n):
        b = first_lag + n
        left = tuple(ref[...].reshape(span * double, total) for ref in (l_high, l_low))
        product = dot3(left, (s_high[b], s_low[b])) * factor
        for a in range(span):
            top = product[a * double : a * double + share]
            bottom = product[a * double + share : (a + 1) * double]
            real = top[:, :width] + bottom[:, width:]
            imag = bottom[:, :width] - top[:, width:]
            for c, value in enumerate((real, imag)):
                mine_ref[a, n, c] = jnp.where(upper, value[half:], value[:half])
                other_ref[a, n, c] = jnp.where(upper, value[:half], value[half:])


def correlate(shares, twin_shares, s_high, s_low, lags, rows, cols, factor):
    peers = 2 * len(shares)
    span, total, lanes = s_high.shape
    reach = span // 2
    double, own = twin_shares.shape[1:]
    share = double // 2
    side = round_up(reach * cols, 128)
    vmem = pl.BlockSpec(memory_space=pltpu.VMEM)
    out = jax.ShapeDtypeStruct((span, lags[1], 2, share // 2, lanes // 2), f32)
    return pl.pallas_call(
        functools.partial(correlate_kernel, (rows, cols, span, peers), lags, factor),
        in_specs=[vmem] * (peers // 2 + 3),
        out_specs=[vmem, vmem],
        out_shape=[out, out],
        scratch_shapes=[
            pltpu.VMEM((peers, double, own), f32),
            pltpu.VMEM((double, total + 2 * side), f32),
            pltpu.VMEM((span, 2, share, total), bf16),
            pltpu.VMEM((span, 2, share, total), bf16),
        ],
        cost_estimate=pl.CostEstimate(
            flops=6 * span * double * total * lags[1] * lanes if lags[0] == 0 else 1,
            bytes_accessed=8 * out.size if lags[0] == 0 else 1,
            transcendentals=0,
        ),
        compiler_params=pltpu.CompilerParams(vmem_limit_bytes=17 * 1024 * 1024),
        name="correlate",
    )(*shares, twin_shares, s_high, s_low)


def swap(value, axis, first):
    pairs = []
    for low in range(first, lax.axis_size(axis) - 1, 2):
        pairs += [(low, low + 1), (low + 1, low)]
    if not pairs:
        return jnp.zeros_like(value)
    return lax.ppermute(value, axis, pairs)


def shifted(value, axis, shift):
    peers = lax.axis_size(axis)
    if shift % peers == 0:
        return value
    return lax.ppermute(value, axis, [(i, (i + shift) % peers) for i in range(peers)])


def edges(initial, last, axis, rider=None, beside=None):
    even = lax.axis_index(axis) % 2 == 0
    shape = initial.shape
    initial, last = (value.reshape(shape[0], -1, shape[-1]) for value in (initial, last))
    inner = jnp.where(even, last, initial)
    outer = swap(jnp.where(even, initial, last), axis, 1)
    count = inner.shape[1]
    if beside is None:
        inner = swap(jnp.concatenate([inner, rider], axis=1), axis, 0)
        inner, rider = inner[:, :count], inner[:, count:]
    else:
        inner, beside = lax.optimization_barrier((inner, beside))
        rider = swap(beside, "row", 0)
        inner, outer, rider = lax.optimization_barrier((inner, outer, rider))
        inner = swap(inner, axis, 0)
    inner = inner.reshape(shape)
    outer = outer.reshape(shape)
    return jnp.where(even, outer, inner), jnp.where(even, inner, outer), rider


def on_device(adjoint_source, saved_currents, lag_blocks, element_inverse):
    rows, cols, parts, width = adjoint_source.shape
    span = lag_blocks.shape[0]
    reach = span // 2
    halo = SWEEPS * reach
    peers = lax.axis_size("row")

    source = adjoint_source.transpose(2, 0, 1, 3)
    saved = saved_currents.transpose(2, 0, 1, 3)
    initial = jnp.concatenate([source[:, :, :halo], saved[:, :, :reach]], axis=2)
    last = jnp.concatenate([source[:, :, cols - halo :], saved[:, :, cols - reach :]], axis=2)
    before, after, twin_own = edges(initial, last, "col", beside=saved)
    source = jnp.concatenate([before[:, :, :halo], source, after[:, :, :halo]], axis=2)
    saved = jnp.concatenate([before[:, :, halo:], saved, after[:, :, halo:]], axis=2)
    sides = jnp.concatenate([saved[:, :, :reach], saved[:, :, cols + reach :]], axis=2)
    twin_sides = sides.reshape(parts, -1, width)
    before, after, arrived = edges(source[:, :halo], source[:, rows - halo :], "row", twin_sides)
    source = jnp.concatenate([before, source, after], axis=1)
    wide = round_up(cols + 2 * halo, 8)
    source = jnp.pad(source, ((0, 0), (0, 0), (0, wide - cols - 2 * halo), (0, 0)))
    twin_sides = arrived.reshape(sides.shape)
    own_twin = jnp.concatenate([twin_sides[:, :, :reach], twin_own, twin_sides[:, :, reach:]], axis=2)
    own_twin = own_twin.reshape(parts, -1, width)

    saved = saved.reshape(parts, -1, width)
    pieces = {0: saved}
    for k in sorted(range(1, peers // 2), key=lambda k: min(k, peers // 2 - k)):
        pieces[k] = shifted(saved, "row", 2 * k)
    pieces = [pieces[k] for k in range(peers // 2)]

    second, own_source, high, low = first_sweep(source, element_inverse, lag_blocks, rows, cols)
    second, own_twin, early = lax.optimization_barrier((second, own_twin, jnp.stack([pieces[1], pieces[-1]])))
    early_twins = swap(early, "row", 0)
    adjoint, sends = second_sweep(second, own_source, element_inverse, high, low, peers)
    *late, sends = lax.optimization_barrier((*pieces[2:-1], sends))
    late_twins = swap(jnp.stack(late), "row", 0)
    shares = [shifted(send, "row", 2 * k) for k, send in enumerate(sends)]
    twin_shares = swap(jnp.stack([received[1] for received in shares]), "row", 0)

    s_high, s_low = spread(pieces, (own_twin, early_twins, late_twins), rows, cols, span)

    elements = rows * peers * cols * lax.axis_size("col")
    factor = -1.0 / math.sqrt(elements)
    even = lax.axis_index("col") % 2 == 0
    totals = []
    for lags in ((0, span),):
        mine, other = correlate(shares, twin_shares, s_high, s_low, lags, rows, cols, factor)
        mine = mine + swap(other, "col", 0)
        twin_shares, mine = lax.optimization_barrier((twin_shares, mine))
        total = mine
        for k in range(2, lax.axis_size("col"), 2):
            total = total + shifted(mine, "col", k)
        totals.append(total)
    total = jnp.concatenate(totals, axis=1)
    twin = swap(total, "col", 0)
    lag_grad = jnp.concatenate(
        [jnp.where(even, total, twin), jnp.where(even, twin, total)], axis=3
    )
    return (adjoint.reshape(adjoint_source.shape), lag_grad)


def solution(mesh):
    return jax.shard_map(
        on_device,
        mesh=mesh,
        in_specs=(P("row", "col", None, None), P("row", "col", None, None), P(), P()),
        out_specs=(P("row", "col", None, None), P(None, None, None, "row", None)),
        check_vma=False,
    )
```

```python
import functools
import math

import jax
import jax.numpy as jnp
from jax import lax
from jax.experimental import pallas as pl
from jax.experimental.pallas import tpu as pltpu
from jax.sharding import PartitionSpec as P

SWEEPS = 2

f32 = jnp.float32
bf16 = jnp.bfloat16


def split(value):
    high = value.astype(bf16)
    return high, (value - high.astype(f32)).astype(bf16)


def dot(left, right):
    return jnp.dot(left, right, preferred_element_type=f32)


def dot3(left, right):
    (left_high, left_low), (right_high, right_low) = left, right
    return dot(left_high, right_high) + dot(left_low, right_high) + dot(left_high, right_low)


def round_up(count, unit):
    return (count + unit - 1) // unit * unit


def chip_along_z(z, shift, count):
    return (z + shift + count) % count


def store_block(ref, index, real, imag):
    width = real.shape[0]
    low, high = slice(0, width), slice(width, 2 * width)
    ref[index + (low, low)] = real
    ref[index + (low, high)] = -imag
    ref[index + (high, low)] = imag
    ref[index + (high, high)] = real


def inside(first_row, rows, cols, pitch, margin, tile_rows, tile_cols):
    at = lax.broadcasted_iota(jnp.int32, (rows * pitch, 1), 0)
    i = at // pitch
    j = at - i * pitch
    row = i + (first_row + lax.axis_index("row") * tile_rows - margin)
    col = j + (lax.axis_index("col") * tile_cols - margin)
    row_ok = (row >= 0) & (row < tile_rows * lax.axis_size("row"))
    col_ok = (col >= 0) & (col < tile_cols * lax.axis_size("col"))
    return row_ok & col_ok & (j < cols)


def store_inverse(inverse_ref, high_ref, low_ref):
    real_high, real_low = split(inverse_ref[0])
    imag_high, imag_low = split(inverse_ref[1])
    store_block(high_ref, (), real_high, imag_high)
    store_block(low_ref, (), real_low, imag_low)


def products(high, low, weight_high, weight_low):
    lanes = weight_high.shape[-1]
    weight_high = weight_high.reshape(-1, lanes)
    weight_low = weight_low.reshape(-1, lanes)
    return dot(high, weight_high) + dot(low, weight_high) + dot(high, weight_low)


def first_sweep_kernel(
    sizes,
    source_ref,
    inverse_ref,
    blocks_ref,
    second_ref,
    own_source_ref,
    w_high,
    w_low,
    first,
    x_high,
    x_low,
    acc,
    e_high,
    e_low,
):
    rows, cols, span, pitch, wide = sizes
    reach = span // 2
    mid_rows, mid_cols = rows + 2 * reach, cols + 2 * reach
    full_rows = rows + 4 * reach
    lanes = 2 * source_ref.shape[-1]

    def source_at(i, j):
        return jnp.concatenate([source_ref[0, i, j, :], source_ref[1, i, j, :]], axis=-1)

    store_inverse(inverse_ref, e_high, e_low)

    def invert(value):
        return dot3(split(value), (e_high[...], e_low[...]))

    own_source_ref[...] = source_at(pl.ds(2 * reach, rows), pl.ds(2 * reach, cols))

    step_rows = 4

    @pl.loop(0, full_rows // step_rows)
    def _(s):
        at = pl.ds(s * step_rows, step_rows)
        piece = source_at(at, pl.ds(0, wide)).reshape(step_rows * wide, lanes)
        first[at] = invert(piece).reshape(step_rows, wide, lanes)

    first[full_rows] = jnp.zeros((wide, lanes), f32)

    @pl.loop(0, full_rows // 2)
    def _(s):
        for odd in range(2):
            for b in range(span):
                value = first[pl.ds(2 * s + odd, 2), pl.ds(b, pitch), :]
                high, low = split(value.reshape(2 * pitch, lanes))
                to = pl.ds(pl.multiple_of(s * 2 * pitch, 2 * pitch), 2 * pitch)
                x_high[odd, to, b * lanes : (b + 1) * lanes] = high
                x_low[odd, to, b * lanes : (b + 1) * lanes] = low

    acc[...] = jnp.zeros_like(acc)

    @pl.loop(0, span)
    def _(a):
        for b in range(span):
            real_high, real_low = split(blocks_ref[a, b, 0])
            imag_high, imag_low = split(blocks_ref[a, b, 1])
            store_block(w_high, (a, b), real_high, imag_high)
            store_block(w_low, (a, b), real_low, imag_low)

        at = pl.ds(pl.multiple_of((a // 2) * 2 * pitch, 2 * pitch), mid_rows * pitch)
        acc[...] += products(x_high[a % 2, at, :], x_low[a % 2, at, :], w_high[a], w_low[a])

    step_rows = 3

    @pl.loop(0, mid_rows // step_rows)
    def _(s):
        at = pl.ds(s * step_rows + reach, step_rows)
        count = step_rows * pitch
        flat = pl.ds(pl.multiple_of(s * count, 8), count)
        centre = first[at, pl.ds(reach, pitch), :].reshape(count, lanes)
        source = source_at(at, pl.ds(reach, pitch)).reshape(count, lanes)
        value = centre + invert(source - centre - acc[flat, :])
        mask = inside(s * step_rows, step_rows, mid_cols, pitch, reach, rows, cols)
        value = jnp.where(mask, value, 0.0)
        second_ref[pl.ds(s * step_rows, step_rows)] = value.reshape(step_rows, pitch, lanes)


def first_sweep(source, inverse, lag_blocks, rows, cols):
    span = lag_blocks.shape[0]
    reach = span // 2
    lanes = 2 * source.shape[-1]
    wide = source.shape[2]
    pitch = round_up(cols + 2 * reach, 8)
    full_rows, mid_rows = rows + 4 * reach, rows + 2 * reach
    vmem = pl.BlockSpec(memory_space=pltpu.VMEM)
    weights = (span, span, lanes, lanes)
    return pl.pallas_call(
        functools.partial(first_sweep_kernel, (rows, cols, span, pitch, wide)),
        in_specs=[vmem] * 3,
        out_specs=[vmem] * 4,
        out_shape=[
            jax.ShapeDtypeStruct((mid_rows, pitch, lanes), f32),
            jax.ShapeDtypeStruct((rows, cols, lanes), f32),
            jax.ShapeDtypeStruct(weights, bf16),
            jax.ShapeDtypeStruct(weights, bf16),
        ],
        scratch_shapes=[
            pltpu.VMEM((full_rows + 1, wide, lanes), f32),
            pltpu.VMEM((2, full_rows * pitch, span * lanes), bf16),
            pltpu.VMEM((2, full_rows * pitch, span * lanes), bf16),
            pltpu.VMEM((mid_rows * pitch, lanes), f32),
            pltpu.VMEM((lanes, lanes), bf16),
            pltpu.VMEM((lanes, lanes), bf16),
        ],
        cost_estimate=pl.CostEstimate(
            flops=6 * span * span * lanes * lanes * mid_rows * pitch,
            bytes_accessed=12 * lag_blocks.size,
            transcendentals=0,
        ),
        compiler_params=pltpu.CompilerParams(vmem_limit_bytes=32 * 1024 * 1024),
        name="first_sweep",
    )(source, inverse, lag_blocks)


def second_sweep_kernel(
    sizes,
    second_ref,
    source_ref,
    inverse_ref,
    w_high,
    w_low,
    adjoint_ref,
    *rest,
):
    rows, cols, span, peers = sizes
    sends = rest[: peers // 2]
    x_high, x_low, acc, turned, e_high, e_low = rest[peers // 2 :]
    reach = span // 2
    mid_rows = rows + 2 * reach
    own = rows * cols
    lanes = source_ref.shape[-1]
    width = lanes // 2

    store_inverse(inverse_ref, e_high, e_low)

    @pl.loop(0, mid_rows)
    def _(i):
        for b in range(span):
            high, low = split(second_ref[i, pl.ds(b, cols), :])
            to = pl.ds(pl.multiple_of(i * cols, cols), cols)
            x_high[to, b * lanes : (b + 1) * lanes] = high
            x_low[to, b * lanes : (b + 1) * lanes] = low

    acc[...] = jnp.zeros_like(acc)

    @pl.loop(0, span)
    def _(a):
        at = pl.ds(pl.multiple_of(a * cols, cols), own)
        acc[...] += products(x_high[at, :], x_low[at, :], w_high[a], w_low[a])

    centre = second_ref[reach : reach + rows, pl.ds(reach, cols), :].reshape(own, lanes)
    source = source_ref[...].reshape(own, lanes)
    value = centre + dot3(split(source - centre - acc[...]), (e_high[...], e_low[...]))
    adjoint_ref[...] = value.reshape(adjoint_ref.shape)
    turned[...] = value.T

    share = width // peers
    me = lax.axis_index("row")
    parity = me % 2
    for k in range(peers // 2):
        base = 2 * chip_along_z(me // 2, k, peers // 2)
        for n, peer in enumerate((base + parity, base + 1 - parity)):
            for part in range(2):
                at = pl.multiple_of(part * width + peer * share, share)
                sends[k][n, part * share : (part + 1) * share, :] = turned[pl.ds(at, share), :]


def second_sweep(second, source, inverse, high, low, peers):
    span = high.shape[0]
    rows, cols, lanes = source.shape
    mid_rows = second.shape[0]
    share = lanes // 2 // peers
    vmem = pl.BlockSpec(memory_space=pltpu.VMEM)
    send = jax.ShapeDtypeStruct((2, 2 * share, rows * cols), f32)
    out = pl.pallas_call(
        functools.partial(second_sweep_kernel, (rows, cols, span, peers)),
        in_specs=[vmem] * 5,
        out_specs=[vmem] * (1 + peers // 2),
        out_shape=[jax.ShapeDtypeStruct((rows, cols, lanes), f32)] + [send] * (peers // 2),
        scratch_shapes=[
            pltpu.VMEM((mid_rows * cols, span * lanes), bf16),
            pltpu.VMEM((mid_rows * cols, span * lanes), bf16),
            pltpu.VMEM((rows * cols, lanes), f32),
            pltpu.VMEM((lanes, rows * cols), f32),
            pltpu.VMEM((lanes, lanes), bf16),
            pltpu.VMEM((lanes, lanes), bf16),
        ],
        cost_estimate=pl.CostEstimate(
            flops=6 * span * span * lanes * lanes * rows * cols,
            bytes_accessed=4 * high.size,
            transcendentals=0,
        ),
        compiler_params=pltpu.CompilerParams(vmem_limit_bytes=18 * 1024 * 1024),
        name="second_sweep",
    )(second, source, inverse, high, low)
    return out[0], out[1:]


def spread_kernel(sizes, *refs):
    rows, cols, span, peers = sizes
    half_peers = peers // 2
    piece_refs = refs[:half_peers]
    own_twin_ref, early_ref, late_ref, s_high, s_low, stage, sems = refs[half_peers:]
    own = rows * cols
    width = stage.shape[-1]
    me = lax.axis_index("row")
    parity = me % 2

    def tiles(k):
        base = 2 * chip_along_z(me // 2, -k, half_peers)
        return base + parity, base + 1 - parity

    for k in range(half_peers):
        if k == 0:
            twin = own_twin_ref
        else:
            near = k in (1, half_peers - 1)
            twin = early_ref.at[0 if k == 1 else 1] if near else late_ref.at[k - 2]
        for source, tile in zip((piece_refs[k], twin), tiles(k)):
            pltpu.make_async_copy(source, stage.at[tile], sems.at[tile]).start()

    @pl.loop(0, peers)
    def _(tile):
        pltpu.make_async_copy(own_twin_ref, stage.at[tile], sems.at[tile]).wait()

        @pl.loop(0, rows)
        def _(i):
            to = pl.ds(pl.multiple_of(tile * own + i * cols, cols), cols)
            for b in range(span):
                for h in range(2):
                    start = i * (cols + span - 1) + span - 1 - b
                    high, low = split(stage[tile, h, pl.ds(start, cols), :])
                    s_high[b, to, h * width : (h + 1) * width] = high
                    s_low[b, to, h * width : (h + 1) * width] = low


def spread(pieces, twins, rows, cols, span):
    peers = 2 * len(pieces)
    piece = pieces[0]
    vmem = pl.BlockSpec(memory_space=pltpu.VMEM)
    hbm = pl.BlockSpec(memory_space=pltpu.HBM)
    out = jax.ShapeDtypeStruct((span, peers * rows * cols, 2 * piece.shape[-1]), bf16)
    return pl.pallas_call(
        functools.partial(spread_kernel, (rows, cols, span, peers)),
        in_specs=[hbm] * (len(pieces) + len(twins)),
        out_specs=[vmem, vmem],
        out_shape=[out, out],
        scratch_shapes=[
            pltpu.VMEM((peers,) + piece.shape, f32),
            pltpu.SemaphoreType.DMA((peers,)),
        ],
        cost_estimate=pl.CostEstimate(
            flops=0, bytes_accessed=4 * peers * piece.size, transcendentals=0
        ),
        compiler_params=pltpu.CompilerParams(vmem_limit_bytes=15 * 1024 * 1024),
        name="spread",
    )(*pieces, *twins)


def correlate_kernel(sizes, lags, factor, *refs):
    rows, cols, span, peers = sizes
    half_peers = peers // 2
    shares = refs[:half_peers]
    twin_shares_ref, s_high, s_low, mine_ref, other_ref = refs[half_peers : half_peers + 5]
    placed, flat, l_high, l_low = refs[half_peers + 5 :]
    reach = span // 2
    own = rows * cols
    double = shares[0].shape[1]
    share = double // 2
    width = s_high.shape[-1] // 2
    me = lax.axis_index("row")
    parity = me % 2

    for k in range(half_peers):
        base = 2 * chip_along_z(me // 2, -k, half_peers)
        placed[base + parity] = shares[k][0]
        placed[base + 1 - parity] = twin_shares_ref[k]

    total = peers * own
    side = round_up(reach * cols, 128)
    flat[:, :side] = jnp.zeros((double, side), f32)
    flat[:, side + total :] = jnp.zeros((double, side), f32)
    for tile in range(peers):
        flat[:, side + tile * own : side + (tile + 1) * own] = placed[tile]

    @pl.loop(0, 2)
    def _(part):
        rows_at = pl.ds(pl.multiple_of(part * share, 8), share)
        for a in range(span):
            start = side + (a - reach) * cols
            high, low = split(flat[rows_at, start : start + total])
            l_high[a, part] = high
            l_low[a, part] = low

    half = share // 2
    upper = lax.axis_index("col") % 2 == 1
    first_lag, count = lags

    @pl.loop(0, count)
    def _(n):
        b = first_lag + n
        left = tuple(ref[...].reshape(span * double, total) for ref in (l_high, l_low))
        product = dot3(left, (s_high[b], s_low[b])) * factor
        for a in range(span):
            top = product[a * double : a * double + share]
            bottom = product[a * double + share : (a + 1) * double]
            real = top[:, :width] + bottom[:, width:]
            imag = bottom[:, :width] - top[:, width:]
            for c, value in enumerate((real, imag)):
                mine_ref[a, n, c] = jnp.where(upper, value[half:], value[:half])
                other_ref[a, n, c] = jnp.where(upper, value[:half], value[half:])


def correlate(shares, twin_shares, s_high, s_low, lags, rows, cols, factor):
    peers = 2 * len(shares)
    span, total, lanes = s_high.shape
    reach = span // 2
    double, own = twin_shares.shape[1:]
    share = double // 2
    side = round_up(reach * cols, 128)
    vmem = pl.BlockSpec(memory_space=pltpu.VMEM)
    out = jax.ShapeDtypeStruct((span, lags[1], 2, share // 2, lanes // 2), f32)
    return pl.pallas_call(
        functools.partial(correlate_kernel, (rows, cols, span, peers), lags, factor),
        in_specs=[vmem] * (peers // 2 + 3),
        out_specs=[vmem, vmem],
        out_shape=[out, out],
        scratch_shapes=[
            pltpu.VMEM((peers, double, own), f32),
            pltpu.VMEM((double, total + 2 * side), f32),
            pltpu.VMEM((span, 2, share, total), bf16),
            pltpu.VMEM((span, 2, share, total), bf16),
        ],
        cost_estimate=pl.CostEstimate(
            flops=6 * span * double * total * lags[1] * lanes if lags[0] == 0 else 1,
            bytes_accessed=8 * out.size if lags[0] == 0 else 1,
            transcendentals=0,
        ),
        compiler_params=pltpu.CompilerParams(vmem_limit_bytes=17 * 1024 * 1024),
        name="correlate",
    )(*shares, twin_shares, s_high, s_low)


def parts_first_kernel(field_ref, out_ref):
    for part in range(2):
        out_ref[part] = field_ref[:, pl.ds(part, out_ref.shape[2], 2), :]


def parts_first(field):
    rows, cols, parts, width = field.shape
    vmem = pl.BlockSpec(memory_space=pltpu.VMEM)
    return pl.pallas_call(
        parts_first_kernel,
        in_specs=[vmem],
        out_specs=vmem,
        out_shape=jax.ShapeDtypeStruct((parts, rows, cols, width), f32),
        cost_estimate=pl.CostEstimate(flops=0, bytes_accessed=8 * field.size, transcendentals=0),
        compiler_params=pltpu.CompilerParams(vmem_limit_bytes=4 * 1024 * 1024),
        name="parts_first",
    )(field.reshape(rows, cols * parts, width))


def swap(value, axis, first):
    pairs = []
    for low in range(first, lax.axis_size(axis) - 1, 2):
        pairs += [(low, low + 1), (low + 1, low)]
    if not pairs:
        return jnp.zeros_like(value)
    return lax.ppermute(value, axis, pairs)


def shifted(value, axis, shift):
    peers = lax.axis_size(axis)
    if shift % peers == 0:
        return value
    return lax.ppermute(value, axis, [(i, (i + shift) % peers) for i in range(peers)])


def edges(initial, last, axis):
    even = lax.axis_index(axis) % 2 == 0
    shape = initial.shape
    initial, last = (value.reshape(shape[0], -1, shape[-1]) for value in (initial, last))
    outer = swap(jnp.where(even, initial, last), axis, 1).reshape(shape)
    inner = swap(jnp.where(even, last, initial), axis, 0).reshape(shape)
    return jnp.where(even, outer, inner), jnp.where(even, inner, outer)


def extended(value, axis, dim, width):
    length = value.shape[dim]
    initial = lax.slice_in_dim(value, 0, width, axis=dim)
    last = lax.slice_in_dim(value, length - width, length, axis=dim)
    before, after = edges(initial, last, axis)
    return jnp.concatenate([before, value, after], axis=dim)


def on_device(adjoint_source, saved_currents, lag_blocks, element_inverse):
    rows, cols, parts, width = adjoint_source.shape
    span = lag_blocks.shape[0]
    reach = span // 2
    halo = SWEEPS * reach
    peers = lax.axis_size("row")

    source = adjoint_source.transpose(2, 0, 1, 3)
    saved = parts_first(saved_currents)
    source = extended(source, "row", 1, halo)
    saved = extended(saved, "col", 2, reach)
    saved = lax.optimization_barrier((saved, source))[0]
    source = extended(source, "col", 2, halo)
    wide = round_up(cols + 2 * halo, 8)
    source = jnp.pad(source, ((0, 0), (0, 0), (0, wide - cols - 2 * halo), (0, 0)))

    saved = saved.reshape(parts, -1, width)
    pieces = {0: saved}
    for k in sorted(range(1, peers // 2), key=lambda k: min(k, peers // 2 - k)):
        pieces[k] = shifted(saved, "row", 2 * k)
    pieces = [pieces[k] for k in range(peers // 2)]
    own_twin = swap(saved, "row", 0)

    second, own_source, high, low = first_sweep(source, element_inverse, lag_blocks, rows, cols)
    second, own_twin, early = lax.optimization_barrier((second, own_twin, jnp.stack([pieces[1], pieces[-1]])))
    early_twins = swap(early, "row", 0)
    adjoint, sends = second_sweep(second, own_source, element_inverse, high, low, peers)
    *late, sends = lax.optimization_barrier((*pieces[2:-1], sends))
    late_twins = swap(jnp.stack(late), "row", 0)
    shares = [shifted(send, "row", 2 * k) for k, send in enumerate(sends)]
    twin_shares = swap(jnp.stack([received[1] for received in shares]), "row", 0)

    s_high, s_low = spread(pieces, (own_twin, early_twins, late_twins), rows, cols, span)

    elements = rows * peers * cols * lax.axis_size("col")
    factor = -1.0 / math.sqrt(elements)
    even = lax.axis_index("col") % 2 == 0
    totals = []
    for lags in ((0, span),):
        mine, other = correlate(shares, twin_shares, s_high, s_low, lags, rows, cols, factor)
        mine = mine + swap(other, "col", 0)
        twin_shares, mine = lax.optimization_barrier((twin_shares, mine))
        total = mine
        for k in range(2, lax.axis_size("col"), 2):
            total = total + shifted(mine, "col", k)
        totals.append(total)
    total = jnp.concatenate(totals, axis=1)
    twin = swap(total, "col", 0)
    lag_grad = jnp.concatenate(
        [jnp.where(even, total, twin), jnp.where(even, twin, total)], axis=3
    )
    return (adjoint.reshape(adjoint_source.shape), lag_grad)


def solution(mesh):
    return jax.shard_map(
        on_device,
        mesh=mesh,
        in_specs=(P("row", "col", None, None), P("row", "col", None, None), P(), P()),
        out_specs=(P("row", "col", None, None), P(None, None, None, "row", None)),
        check_vma=False,
    )
```

```python
import functools
import math

import jax
import jax.numpy as jnp
from jax import lax
from jax.experimental import pallas as pl
from jax.experimental.pallas import tpu as pltpu
from jax.sharding import PartitionSpec as P

SWEEPS = 2

f32 = jnp.float32
bf16 = jnp.bfloat16


def split(value):
    high = value.astype(bf16)
    return high, (value - high.astype(f32)).astype(bf16)


def dot(left, right):
    return jnp.dot(left, right, preferred_element_type=f32)


def dot3(left, right):
    (left_high, left_low), (right_high, right_low) = left, right
    return dot(left_high, right_high) + dot(left_low, right_high) + dot(left_high, right_low)


def round_up(count, unit):
    return (count + unit - 1) // unit * unit


def chip_along_z(z, shift, count):
    return (z + shift + count) % count


def store_block(ref, index, real, imag):
    width = real.shape[0]
    low, high = slice(0, width), slice(width, 2 * width)
    ref[index + (low, low)] = real
    ref[index + (low, high)] = -imag
    ref[index + (high, low)] = imag
    ref[index + (high, high)] = real


def inside(first_row, rows, cols, pitch, margin, tile_rows, tile_cols):
    at = lax.broadcasted_iota(jnp.int32, (rows * pitch, 1), 0)
    i = at // pitch
    j = at - i * pitch
    row = i + (first_row + lax.axis_index("row") * tile_rows - margin)
    col = j + (lax.axis_index("col") * tile_cols - margin)
    row_ok = (row >= 0) & (row < tile_rows * lax.axis_size("row"))
    col_ok = (col >= 0) & (col < tile_cols * lax.axis_size("col"))
    return row_ok & col_ok & (j < cols)


def store_inverse(inverse_ref, high_ref, low_ref):
    real_high, real_low = split(inverse_ref[0])
    imag_high, imag_low = split(inverse_ref[1])
    store_block(high_ref, (), real_high, imag_high)
    store_block(low_ref, (), real_low, imag_low)


def products(high, low, weight_high, weight_low):
    lanes = weight_high.shape[-1]
    weight_high = weight_high.reshape(-1, lanes)
    weight_low = weight_low.reshape(-1, lanes)
    return dot(high, weight_high) + dot(low, weight_high) + dot(high, weight_low)


def first_sweep_kernel(
    sizes,
    source_ref,
    inverse_ref,
    blocks_ref,
    second_ref,
    own_source_ref,
    w_high,
    w_low,
    first,
    x_high,
    x_low,
    acc,
    e_high,
    e_low,
):
    rows, cols, span, pitch, wide = sizes
    reach = span // 2
    mid_rows, mid_cols = rows + 2 * reach, cols + 2 * reach
    full_rows = rows + 4 * reach
    lanes = 2 * source_ref.shape[-1]

    def source_at(i, j):
        return jnp.concatenate([source_ref[0, i, j, :], source_ref[1, i, j, :]], axis=-1)

    store_inverse(inverse_ref, e_high, e_low)

    def invert(value):
        return dot3(split(value), (e_high[...], e_low[...]))

    own_source_ref[...] = source_at(pl.ds(2 * reach, rows), pl.ds(2 * reach, cols))

    step_rows = 4

    @pl.loop(0, full_rows // step_rows)
    def _(s):
        at = pl.ds(s * step_rows, step_rows)
        piece = source_at(at, pl.ds(0, wide)).reshape(step_rows * wide, lanes)
        first[at] = invert(piece).reshape(step_rows, wide, lanes)

    first[full_rows] = jnp.zeros((wide, lanes), f32)

    @pl.loop(0, full_rows // 2)
    def _(s):
        for odd in range(2):
            for b in range(span):
                value = first[pl.ds(2 * s + odd, 2), pl.ds(b, pitch), :]
                high, low = split(value.reshape(2 * pitch, lanes))
                to = pl.ds(pl.multiple_of(s * 2 * pitch, 2 * pitch), 2 * pitch)
                x_high[odd, to, b * lanes : (b + 1) * lanes] = high
                x_low[odd, to, b * lanes : (b + 1) * lanes] = low

    acc[...] = jnp.zeros_like(acc)

    @pl.loop(0, span)
    def _(a):
        for b in range(span):
            real_high, real_low = split(blocks_ref[a, b, 0])
            imag_high, imag_low = split(blocks_ref[a, b, 1])
            store_block(w_high, (a, b), real_high, imag_high)
            store_block(w_low, (a, b), real_low, imag_low)

        at = pl.ds(pl.multiple_of((a // 2) * 2 * pitch, 2 * pitch), mid_rows * pitch)
        acc[...] += products(x_high[a % 2, at, :], x_low[a % 2, at, :], w_high[a], w_low[a])

    step_rows = 3

    @pl.loop(0, mid_rows // step_rows)
    def _(s):
        at = pl.ds(s * step_rows + reach, step_rows)
        count = step_rows * pitch
        flat = pl.ds(pl.multiple_of(s * count, 8), count)
        centre = first[at, pl.ds(reach, pitch), :].reshape(count, lanes)
        source = source_at(at, pl.ds(reach, pitch)).reshape(count, lanes)
        value = centre + invert(source - centre - acc[flat, :])
        mask = inside(s * step_rows, step_rows, mid_cols, pitch, reach, rows, cols)
        value = jnp.where(mask, value, 0.0)
        second_ref[pl.ds(s * step_rows, step_rows)] = value.reshape(step_rows, pitch, lanes)


def first_sweep(source, inverse, lag_blocks, rows, cols):
    span = lag_blocks.shape[0]
    reach = span // 2
    lanes = 2 * source.shape[-1]
    wide = source.shape[2]
    pitch = round_up(cols + 2 * reach, 8)
    full_rows, mid_rows = rows + 4 * reach, rows + 2 * reach
    vmem = pl.BlockSpec(memory_space=pltpu.VMEM)
    weights = (span, span, lanes, lanes)
    return pl.pallas_call(
        functools.partial(first_sweep_kernel, (rows, cols, span, pitch, wide)),
        in_specs=[vmem] * 3,
        out_specs=[vmem] * 4,
        out_shape=[
            jax.ShapeDtypeStruct((mid_rows, pitch, lanes), f32),
            jax.ShapeDtypeStruct((rows, cols, lanes), f32),
            jax.ShapeDtypeStruct(weights, bf16),
            jax.ShapeDtypeStruct(weights, bf16),
        ],
        scratch_shapes=[
            pltpu.VMEM((full_rows + 1, wide, lanes), f32),
            pltpu.VMEM((2, full_rows * pitch, span * lanes), bf16),
            pltpu.VMEM((2, full_rows * pitch, span * lanes), bf16),
            pltpu.VMEM((mid_rows * pitch, lanes), f32),
            pltpu.VMEM((lanes, lanes), bf16),
            pltpu.VMEM((lanes, lanes), bf16),
        ],
        cost_estimate=pl.CostEstimate(
            flops=6 * span * span * lanes * lanes * mid_rows * pitch,
            bytes_accessed=12 * lag_blocks.size,
            transcendentals=0,
        ),
        compiler_params=pltpu.CompilerParams(vmem_limit_bytes=32 * 1024 * 1024),
        name="first_sweep",
    )(source, inverse, lag_blocks)


def second_sweep_kernel(
    sizes,
    second_ref,
    source_ref,
    inverse_ref,
    w_high,
    w_low,
    adjoint_ref,
    *rest,
):
    rows, cols, span, peers = sizes
    sends = rest[: peers // 2]
    x_high, x_low, acc, turned, e_high, e_low = rest[peers // 2 :]
    reach = span // 2
    mid_rows = rows + 2 * reach
    own = rows * cols
    lanes = source_ref.shape[-1]
    width = lanes // 2

    store_inverse(inverse_ref, e_high, e_low)

    @pl.loop(0, mid_rows)
    def _(i):
        for b in range(span):
            high, low = split(second_ref[i, pl.ds(b, cols), :])
            to = pl.ds(pl.multiple_of(i * cols, cols), cols)
            x_high[to, b * lanes : (b + 1) * lanes] = high
            x_low[to, b * lanes : (b + 1) * lanes] = low

    acc[...] = jnp.zeros_like(acc)

    @pl.loop(0, span)
    def _(a):
        at = pl.ds(pl.multiple_of(a * cols, cols), own)
        acc[...] += products(x_high[at, :], x_low[at, :], w_high[a], w_low[a])

    centre = second_ref[reach : reach + rows, pl.ds(reach, cols), :].reshape(own, lanes)
    source = source_ref[...].reshape(own, lanes)
    value = centre + dot3(split(source - centre - acc[...]), (e_high[...], e_low[...]))
    adjoint_ref[...] = value.reshape(adjoint_ref.shape)
    turned[...] = value.T

    share = width // peers
    me = lax.axis_index("row")
    parity = me % 2
    for k in range(peers // 2):
        base = 2 * chip_along_z(me // 2, k, peers // 2)
        for n, peer in enumerate((base + parity, base + 1 - parity)):
            for part in range(2):
                at = pl.multiple_of(part * width + peer * share, share)
                sends[k][n, part * share : (part + 1) * share, :] = turned[pl.ds(at, share), :]


def second_sweep(second, source, inverse, high, low, peers):
    span = high.shape[0]
    rows, cols, lanes = source.shape
    mid_rows = second.shape[0]
    share = lanes // 2 // peers
    vmem = pl.BlockSpec(memory_space=pltpu.VMEM)
    send = jax.ShapeDtypeStruct((2, 2 * share, rows * cols), f32)
    out = pl.pallas_call(
        functools.partial(second_sweep_kernel, (rows, cols, span, peers)),
        in_specs=[vmem] * 5,
        out_specs=[vmem] * (1 + peers // 2),
        out_shape=[jax.ShapeDtypeStruct((rows, cols, lanes), f32)] + [send] * (peers // 2),
        scratch_shapes=[
            pltpu.VMEM((mid_rows * cols, span * lanes), bf16),
            pltpu.VMEM((mid_rows * cols, span * lanes), bf16),
            pltpu.VMEM((rows * cols, lanes), f32),
            pltpu.VMEM((lanes, rows * cols), f32),
            pltpu.VMEM((lanes, lanes), bf16),
            pltpu.VMEM((lanes, lanes), bf16),
        ],
        cost_estimate=pl.CostEstimate(
            flops=6 * span * span * lanes * lanes * rows * cols,
            bytes_accessed=4 * high.size,
            transcendentals=0,
        ),
        compiler_params=pltpu.CompilerParams(vmem_limit_bytes=18 * 1024 * 1024),
        name="second_sweep",
    )(second, source, inverse, high, low)
    return out[0], out[1:]


def tiles_of(k, peers):
    me = lax.axis_index("row")
    parity = me % 2
    base = 2 * chip_along_z(me // 2, -k, peers // 2)
    return base + parity, base + 1 - parity


def spread_kernel(sizes, places, filled, *refs):
    rows, cols, span, peers = sizes
    count = len(places)
    sources = refs[:count]
    s_high, s_low, stage, sems = refs[count + filled :]
    own = rows * cols
    width = stage.shape[-1]
    copies = []
    at = 0
    for source, place in zip(sources, places):
        for n, (k, twin) in enumerate(place):
            piece = source.at[n] if len(source.shape) == 4 else source
            copies.append((pltpu.make_async_copy(piece, stage.at[at], sems.at[at]), tiles_of(k, peers)[twin]))
            copies[-1][0].start()
            at += 1

    for at, (copy, tile) in enumerate(copies):
        copy.wait()

        @pl.loop(0, rows)
        def _(i):
            to = pl.ds(pl.multiple_of(tile * own + i * cols, cols), cols)
            for b in range(span):
                for h in range(2):
                    start = i * (cols + span - 1) + span - 1 - b
                    high, low = split(stage[at, h, pl.ds(start, cols), :])
                    s_high[b, to, h * width : (h + 1) * width] = high
                    s_low[b, to, h * width : (h + 1) * width] = low


def spread(placed, rows, cols, span, peers, filled=()):
    sources, places = zip(*placed)
    piece = sources[0].shape[-3:]
    vmem = pl.BlockSpec(memory_space=pltpu.VMEM)
    hbm = pl.BlockSpec(memory_space=pltpu.HBM)
    out = jax.ShapeDtypeStruct((span, peers * rows * cols, 2 * piece[-1]), bf16)
    count = sum(len(place) for place in places)
    return pl.pallas_call(
        functools.partial(spread_kernel, (rows, cols, span, peers), places, len(filled)),
        in_specs=[hbm] * len(sources) + [vmem] * len(filled),
        out_specs=[vmem, vmem],
        out_shape=[out, out],
        input_output_aliases={len(sources) + n: n for n in range(len(filled))},
        scratch_shapes=[
            pltpu.VMEM((count,) + piece, f32),
            pltpu.SemaphoreType.DMA((count,)),
        ],
        cost_estimate=pl.CostEstimate(
            flops=0, bytes_accessed=4 * count * math.prod(piece), transcendentals=0
        ),
        compiler_params=pltpu.CompilerParams(vmem_limit_bytes=30 * 1024 * 1024),
        name="spread",
    )(*sources, *filled)


def correlate_kernel(sizes, lags, factor, *refs):
    rows, cols, span, peers = sizes
    half_peers = peers // 2
    shares = refs[:half_peers]
    twin_shares_ref, s_high, s_low, mine_ref, other_ref = refs[half_peers : half_peers + 5]
    placed, flat, l_high, l_low = refs[half_peers + 5 :]
    reach = span // 2
    own = rows * cols
    double = shares[0].shape[1]
    share = double // 2
    width = s_high.shape[-1] // 2

    for k in range(half_peers):
        tile, twin = tiles_of(k, peers)
        placed[tile] = shares[k][0]
        placed[twin] = twin_shares_ref[k]

    total = peers * own
    side = round_up(reach * cols, 128)
    flat[:, :side] = jnp.zeros((double, side), f32)
    flat[:, side + total :] = jnp.zeros((double, side), f32)
    for tile in range(peers):
        flat[:, side + tile * own : side + (tile + 1) * own] = placed[tile]

    @pl.loop(0, 2)
    def _(part):
        rows_at = pl.ds(pl.multiple_of(part * share, 8), share)
        for a in range(span):
            start = side + (a - reach) * cols
            high, low = split(flat[rows_at, start : start + total])
            l_high[a, part] = high
            l_low[a, part] = low

    half = share // 2
    upper = lax.axis_index("col") % 2 == 1
    first_lag, count = lags

    @pl.loop(0, count)
    def _(n):
        b = first_lag + n
        left = tuple(ref[...].reshape(span * double, total) for ref in (l_high, l_low))
        product = dot3(left, (s_high[b], s_low[b])) * factor
        for a in range(span):
            top = product[a * double : a * double + share]
            bottom = product[a * double + share : (a + 1) * double]
            real = top[:, :width] + bottom[:, width:]
            imag = bottom[:, :width] - top[:, width:]
            for c, value in enumerate((real, imag)):
                mine_ref[a, n, c] = jnp.where(upper, value[half:], value[:half])
                other_ref[a, n, c] = jnp.where(upper, value[:half], value[half:])


def correlate(shares, twin_shares, s_high, s_low, lags, rows, cols, factor):
    peers = 2 * len(shares)
    span, total, lanes = s_high.shape
    reach = span // 2
    double, own = twin_shares.shape[1:]
    share = double // 2
    side = round_up(reach * cols, 128)
    vmem = pl.BlockSpec(memory_space=pltpu.VMEM)
    out = jax.ShapeDtypeStruct((span, lags[1], 2, share // 2, lanes // 2), f32)
    return pl.pallas_call(
        functools.partial(correlate_kernel, (rows, cols, span, peers), lags, factor),
        in_specs=[vmem] * (peers // 2 + 3),
        out_specs=[vmem, vmem],
        out_shape=[out, out],
        scratch_shapes=[
            pltpu.VMEM((peers, double, own), f32),
            pltpu.VMEM((double, total + 2 * side), f32),
            pltpu.VMEM((span, 2, share, total), bf16),
            pltpu.VMEM((span, 2, share, total), bf16),
        ],
        cost_estimate=pl.CostEstimate(
            flops=6 * span * double * total * lags[1] * lanes if lags[0] == 0 else 1,
            bytes_accessed=8 * out.size if lags[0] == 0 else 1,
            transcendentals=0,
        ),
        compiler_params=pltpu.CompilerParams(vmem_limit_bytes=17 * 1024 * 1024),
        name="correlate",
    )(*shares, twin_shares, s_high, s_low)


def parts_first_kernel(field_ref, out_ref):
    for part in range(2):
        out_ref[part] = field_ref[:, pl.ds(part, out_ref.shape[2], 2), :]


def parts_first(field):
    rows, cols, parts, width = field.shape
    vmem = pl.BlockSpec(memory_space=pltpu.VMEM)
    return pl.pallas_call(
        parts_first_kernel,
        in_specs=[vmem],
        out_specs=vmem,
        out_shape=jax.ShapeDtypeStruct((parts, rows, cols, width), f32),
        cost_estimate=pl.CostEstimate(flops=0, bytes_accessed=8 * field.size, transcendentals=0),
        compiler_params=pltpu.CompilerParams(vmem_limit_bytes=4 * 1024 * 1024),
        name="parts_first",
    )(field.reshape(rows, cols * parts, width))


def swap(value, axis, first):
    pairs = []
    for low in range(first, lax.axis_size(axis) - 1, 2):
        pairs += [(low, low + 1), (low + 1, low)]
    if not pairs:
        return jnp.zeros_like(value)
    return lax.ppermute(value, axis, pairs)


def shifted(value, axis, shift):
    peers = lax.axis_size(axis)
    if shift % peers == 0:
        return value
    return lax.ppermute(value, axis, [(i, (i + shift) % peers) for i in range(peers)])


def edges(initial, last, axis):
    even = lax.axis_index(axis) % 2 == 0
    shape = initial.shape
    initial, last = (value.reshape(shape[0], -1, shape[-1]) for value in (initial, last))
    outer = swap(jnp.where(even, initial, last), axis, 1).reshape(shape)
    inner = swap(jnp.where(even, last, initial), axis, 0).reshape(shape)
    return jnp.where(even, outer, inner), jnp.where(even, inner, outer), inner


def extended(value, axis, dim, width):
    length = value.shape[dim]
    initial = lax.slice_in_dim(value, 0, width, axis=dim)
    last = lax.slice_in_dim(value, length - width, length, axis=dim)
    before, after, inner = edges(initial, last, axis)
    return jnp.concatenate([before, value, after], axis=dim), inner


def on_device(adjoint_source, saved_currents, lag_blocks, element_inverse):
    rows, cols, parts, width = adjoint_source.shape
    span = lag_blocks.shape[0]
    reach = span // 2
    halo = SWEEPS * reach
    peers = lax.axis_size("row")

    source = adjoint_source.transpose(2, 0, 1, 3)
    saved = parts_first(saved_currents)
    source, _ = extended(source, "row", 1, halo)
    saved, _ = extended(saved, "col", 2, reach)
    saved = lax.optimization_barrier((saved, source))[0]
    source, inner = extended(source, "col", 2, halo)
    wide = round_up(cols + 2 * halo, 8)
    source = jnp.pad(source, ((0, 0), (0, 0), (0, wide - cols - 2 * halo), (0, 0)))

    saved = saved.reshape(parts, -1, width)
    pieces = {0: saved}
    behind = lax.optimization_barrier((saved, inner))[0]
    for k in sorted(range(1, peers // 2), key=lambda k: min(k, peers // 2 - k)):
        near = k in (1, peers // 2 - 1)
        pieces[k] = shifted(saved if near else behind, "row", 2 * k)
    pieces = [pieces[k] for k in range(peers // 2)]
    own_twin = swap(lax.optimization_barrier((saved, source))[0], "row", 0)

    second, own_source, high, low = first_sweep(source, element_inverse, lag_blocks, rows, cols)
    second, own_twin, early = lax.optimization_barrier((second, own_twin, jnp.stack([pieces[1], pieces[-1]])))
    early_twins = swap(early, "row", 0)
    adjoint, sends = second_sweep(second, own_source, element_inverse, high, low, peers)
    *late, sends = lax.optimization_barrier((*pieces[2:-1], sends))
    late_twins = swap(jnp.stack(late), "row", 0)
    shares = [shifted(send, "row", 2 * k) for k, send in enumerate(sends)]
    twin_shares = swap(jnp.stack([received[1] for received in shares]), "row", 0)

    last = peers // 2 - 1
    arrived = [(piece, ((k, 0),)) for k, piece in enumerate(pieces)]
    arrived += [(own_twin, ((0, 1),)), (early_twins, ((1, 1), (last, 1)))]
    spreads = spread(arrived, rows, cols, span, peers)
    late = [(late_twins, tuple((k, 1) for k in range(2, last)))]
    s_high, s_low = spread(late, rows, cols, span, peers, tuple(spreads))

    elements = rows * peers * cols * lax.axis_size("col")
    factor = -1.0 / math.sqrt(elements)
    even = lax.axis_index("col") % 2 == 0
    totals = []
    for lags in ((0, span),):
        mine, other = correlate(shares, twin_shares, s_high, s_low, lags, rows, cols, factor)
        mine = mine + swap(other, "col", 0)
        twin_shares, mine = lax.optimization_barrier((twin_shares, mine))
        for piece in (mine[: span // 2 + 1], mine[span // 2 + 1 :]):
            total = piece
            for k in range(2, lax.axis_size("col"), 2):
                total = total + shifted(piece, "col", k)
            totals.append(total)
    twins = [swap(total, "col", 0) for total in totals]
    total, twin = jnp.concatenate(totals, axis=0), jnp.concatenate(twins, axis=0)
    lag_grad = jnp.concatenate(
        [jnp.where(even, total, twin), jnp.where(even, twin, total)], axis=3
    )
    return (adjoint.reshape(adjoint_source.shape), lag_grad)


def solution(mesh):
    return jax.shard_map(
        on_device,
        mesh=mesh,
        in_specs=(P("row", "col", None, None), P("row", "col", None, None), P(), P()),
        out_specs=(P("row", "col", None, None), P(None, None, None, "row", None)),
        check_vma=False,
    )
```

```python
import functools
import math

import jax
import jax.numpy as jnp
from jax import lax
from jax.experimental import pallas as pl
from jax.experimental.pallas import tpu as pltpu
from jax.sharding import PartitionSpec as P

SWEEPS = 2

f32 = jnp.float32
bf16 = jnp.bfloat16


def split(value):
    high = value.astype(bf16)
    return high, (value - high.astype(f32)).astype(bf16)


def dot(left, right):
    return jnp.dot(left, right, preferred_element_type=f32)


def dot3(left, right):
    (left_high, left_low), (right_high, right_low) = left, right
    return dot(left_high, right_high) + dot(left_low, right_high) + dot(left_high, right_low)


def largest_divisor(count, most):
    return max(n for n in range(1, most + 1) if count % n == 0)


def round_up(count, unit):
    return (count + unit - 1) // unit * unit


def chip_along_z(z, shift, count):
    return (z + shift + count) % count


def store_block(ref, index, real, imag):
    width = real.shape[0]
    low, high = slice(0, width), slice(width, 2 * width)
    ref[index + (low, low)] = real
    ref[index + (low, high)] = -imag
    ref[index + (high, low)] = imag
    ref[index + (high, high)] = real


def inside(first_row, rows, cols, pitch, margin, tile_rows, tile_cols):
    at = lax.broadcasted_iota(jnp.int32, (rows * pitch, 1), 0)
    i = at // pitch
    j = at - i * pitch
    row = i + (first_row + lax.axis_index("row") * tile_rows - margin)
    col = j + (lax.axis_index("col") * tile_cols - margin)
    row_ok = (row >= 0) & (row < tile_rows * lax.axis_size("row"))
    col_ok = (col >= 0) & (col < tile_cols * lax.axis_size("col"))
    return row_ok & col_ok & (j < cols)


def store_inverse(inverse_ref, high_ref, low_ref):
    real_high, real_low = split(inverse_ref[0])
    imag_high, imag_low = split(inverse_ref[1])
    store_block(high_ref, (), real_high, imag_high)
    store_block(low_ref, (), real_low, imag_low)


def products(high, low, weight_high, weight_low):
    lanes = weight_high.shape[-1]
    weight_high = weight_high.reshape(-1, lanes)
    weight_low = weight_low.reshape(-1, lanes)
    return dot(high, weight_high) + dot(low, weight_high) + dot(high, weight_low)


def first_sweep_kernel(
    sizes,
    source_ref,
    inverse_ref,
    blocks_ref,
    second_ref,
    own_source_ref,
    w_high,
    w_low,
    first,
    x_high,
    x_low,
    acc,
    e_high,
    e_low,
):
    rows, cols, span, pitch, wide = sizes
    reach = span // 2
    mid_rows, mid_cols = rows + 2 * reach, cols + 2 * reach
    full_rows = rows + 4 * reach
    lanes = 2 * source_ref.shape[-1]

    def source_at(i, j):
        return jnp.concatenate([source_ref[0, i, j, :], source_ref[1, i, j, :]], axis=-1)

    store_inverse(inverse_ref, e_high, e_low)

    def invert(value):
        return dot3(split(value), (e_high[...], e_low[...]))

    own_source_ref[...] = source_at(pl.ds(2 * reach, rows), pl.ds(2 * reach, cols))

    step_rows = largest_divisor(full_rows, 12)

    @pl.loop(0, full_rows // step_rows)
    def _(s):
        at = pl.ds(s * step_rows, step_rows)
        piece = source_at(at, pl.ds(0, wide)).reshape(step_rows * wide, lanes)
        first[at] = invert(piece).reshape(step_rows, wide, lanes)

    first[full_rows] = jnp.zeros((wide, lanes), f32)

    @pl.loop(0, full_rows // 2)
    def _(s):
        for odd in range(2):
            for b in range(span):
                value = first[pl.ds(2 * s + odd, 2), pl.ds(b, pitch), :]
                high, low = split(value.reshape(2 * pitch, lanes))
                to = pl.ds(pl.multiple_of(s * 2 * pitch, 2 * pitch), 2 * pitch)
                x_high[odd, to, b * lanes : (b + 1) * lanes] = high
                x_low[odd, to, b * lanes : (b + 1) * lanes] = low

    acc[...] = jnp.zeros_like(acc)

    @pl.loop(0, span)
    def _(a):
        for b in range(span):
            real_high, real_low = split(blocks_ref[a, b, 0])
            imag_high, imag_low = split(blocks_ref[a, b, 1])
            store_block(w_high, (a, b), real_high, imag_high)
            store_block(w_low, (a, b), real_low, imag_low)

        at = pl.ds(pl.multiple_of((a // 2) * 2 * pitch, 2 * pitch), mid_rows * pitch)
        acc[...] += products(x_high[a % 2, at, :], x_low[a % 2, at, :], w_high[a], w_low[a])

    step_rows = largest_divisor(mid_rows, 18)

    @pl.loop(0, mid_rows // step_rows)
    def _(s):
        at = pl.ds(s * step_rows + reach, step_rows)
        count = step_rows * pitch
        flat = pl.ds(pl.multiple_of(s * count, 8), count)
        centre = first[at, pl.ds(reach, pitch), :].reshape(count, lanes)
        source = source_at(at, pl.ds(reach, pitch)).reshape(count, lanes)
        value = centre + invert(source - centre - acc[flat, :])
        mask = inside(s * step_rows, step_rows, mid_cols, pitch, reach, rows, cols)
        value = jnp.where(mask, value, 0.0)
        second_ref[pl.ds(s * step_rows, step_rows)] = value.reshape(step_rows, pitch, lanes)


def first_sweep(source, inverse, lag_blocks, rows, cols):
    span = lag_blocks.shape[0]
    reach = span // 2
    lanes = 2 * source.shape[-1]
    wide = source.shape[2]
    pitch = round_up(cols + 2 * reach, 8)
    full_rows, mid_rows = rows + 4 * reach, rows + 2 * reach
    vmem = pl.BlockSpec(memory_space=pltpu.VMEM)
    weights = (span, span, lanes, lanes)
    return pl.pallas_call(
        functools.partial(first_sweep_kernel, (rows, cols, span, pitch, wide)),
        in_specs=[vmem] * 3,
        out_specs=[vmem] * 4,
        out_shape=[
            jax.ShapeDtypeStruct((mid_rows, pitch, lanes), f32),
            jax.ShapeDtypeStruct((rows, cols, lanes), f32),
            jax.ShapeDtypeStruct(weights, bf16),
            jax.ShapeDtypeStruct(weights, bf16),
        ],
        scratch_shapes=[
            pltpu.VMEM((full_rows + 1, wide, lanes), f32),
            pltpu.VMEM((2, full_rows * pitch, span * lanes), bf16),
            pltpu.VMEM((2, full_rows * pitch, span * lanes), bf16),
            pltpu.VMEM((mid_rows * pitch, lanes), f32),
            pltpu.VMEM((lanes, lanes), bf16),
            pltpu.VMEM((lanes, lanes), bf16),
        ],
        cost_estimate=pl.CostEstimate(
            flops=6 * span * span * lanes * lanes * mid_rows * pitch,
            bytes_accessed=12 * lag_blocks.size,
            transcendentals=0,
        ),
        compiler_params=pltpu.CompilerParams(vmem_limit_bytes=32 * 1024 * 1024),
        name="first_sweep",
    )(source, inverse, lag_blocks)


def second_sweep_kernel(
    sizes,
    second_ref,
    source_ref,
    inverse_ref,
    w_high,
    w_low,
    adjoint_ref,
    *rest,
):
    rows, cols, span, peers = sizes
    sends = rest[: peers // 2]
    x_high, x_low, acc, turned, e_high, e_low = rest[peers // 2 :]
    reach = span // 2
    mid_rows = rows + 2 * reach
    own = rows * cols
    lanes = source_ref.shape[-1]
    width = lanes // 2

    store_inverse(inverse_ref, e_high, e_low)

    step_rows = largest_divisor(mid_rows, 3)

    @pl.loop(0, mid_rows // step_rows)
    def _(s):
        for b in range(span):
            at = pl.ds(s * step_rows, step_rows)
            value = second_ref[at, pl.ds(b, cols), :].reshape(step_rows * cols, lanes)
            high, low = split(value)
            to = pl.ds(pl.multiple_of(s * step_rows * cols, cols), step_rows * cols)
            x_high[to, b * lanes : (b + 1) * lanes] = high
            x_low[to, b * lanes : (b + 1) * lanes] = low

    acc[...] = jnp.zeros_like(acc)

    @pl.loop(0, span)
    def _(a):
        at = pl.ds(pl.multiple_of(a * cols, cols), own)
        acc[...] += products(x_high[at, :], x_low[at, :], w_high[a], w_low[a])

    centre = second_ref[reach : reach + rows, pl.ds(reach, cols), :].reshape(own, lanes)
    source = source_ref[...].reshape(own, lanes)
    value = centre + dot3(split(source - centre - acc[...]), (e_high[...], e_low[...]))
    adjoint_ref[...] = value.reshape(adjoint_ref.shape)
    turned[...] = value.T

    share = width // peers
    me = lax.axis_index("row")
    parity = me % 2
    for k in range(peers // 2):
        base = 2 * chip_along_z(me // 2, k, peers // 2)
        for n, peer in enumerate((base + parity, base + 1 - parity)):
            for part in range(2):
                at = pl.multiple_of(part * width + peer * share, share)
                sends[k][n, part * share : (part + 1) * share, :] = turned[pl.ds(at, share), :]


def second_sweep(second, source, inverse, high, low, peers):
    span = high.shape[0]
    rows, cols, lanes = source.shape
    mid_rows = second.shape[0]
    share = lanes // 2 // peers
    vmem = pl.BlockSpec(memory_space=pltpu.VMEM)
    send = jax.ShapeDtypeStruct((2, 2 * share, rows * cols), f32)
    out = pl.pallas_call(
        functools.partial(second_sweep_kernel, (rows, cols, span, peers)),
        in_specs=[vmem] * 5,
        out_specs=[vmem] * (1 + peers // 2),
        out_shape=[jax.ShapeDtypeStruct((rows, cols, lanes), f32)] + [send] * (peers // 2),
        scratch_shapes=[
            pltpu.VMEM((mid_rows * cols, span * lanes), bf16),
            pltpu.VMEM((mid_rows * cols, span * lanes), bf16),
            pltpu.VMEM((rows * cols, lanes), f32),
            pltpu.VMEM((lanes, rows * cols), f32),
            pltpu.VMEM((lanes, lanes), bf16),
            pltpu.VMEM((lanes, lanes), bf16),
        ],
        cost_estimate=pl.CostEstimate(
            flops=6 * span * span * lanes * lanes * rows * cols,
            bytes_accessed=4 * high.size,
            transcendentals=0,
        ),
        compiler_params=pltpu.CompilerParams(vmem_limit_bytes=18 * 1024 * 1024),
        name="second_sweep",
    )(second, source, inverse, high, low)
    return out[0], out[1:]


def tiles_of(k, peers):
    me = lax.axis_index("row")
    parity = me % 2
    base = 2 * chip_along_z(me // 2, -k, peers // 2)
    return base + parity, base + 1 - parity


def spread_kernel(sizes, places, filled, *refs):
    rows, cols, span, peers = sizes
    count = len(places)
    sources = refs[:count]
    s_high, s_low, stage, sems = refs[count + filled :]
    own = rows * cols
    width = stage.shape[-1]
    copies = []
    at = 0
    for source, place in zip(sources, places):
        for n, (k, twin) in enumerate(place):
            piece = source.at[n] if len(source.shape) == 4 else source
            copies.append((pltpu.make_async_copy(piece, stage.at[at], sems.at[at]), tiles_of(k, peers)[twin]))
            copies[-1][0].start()
            at += 1

    for at, (copy, tile) in enumerate(copies):
        copy.wait()

        @pl.loop(0, rows)
        def _(i):
            to = pl.ds(pl.multiple_of(tile * own + i * cols, cols), cols)
            for b in range(span):
                for h in range(2):
                    start = i * (cols + span - 1) + span - 1 - b
                    high, low = split(stage[at, h, pl.ds(start, cols), :])
                    s_high[b, to, h * width : (h + 1) * width] = high
                    s_low[b, to, h * width : (h + 1) * width] = low


def spread(placed, rows, cols, span, peers, filled=()):
    sources, places = zip(*placed)
    piece = sources[0].shape[-3:]
    vmem = pl.BlockSpec(memory_space=pltpu.VMEM)
    hbm = pl.BlockSpec(memory_space=pltpu.HBM)
    out = jax.ShapeDtypeStruct((span, peers * rows * cols, 2 * piece[-1]), bf16)
    count = sum(len(place) for place in places)
    return pl.pallas_call(
        functools.partial(spread_kernel, (rows, cols, span, peers), places, len(filled)),
        in_specs=[hbm] * len(sources) + [vmem] * len(filled),
        out_specs=[vmem, vmem],
        out_shape=[out, out],
        input_output_aliases={len(sources) + n: n for n in range(len(filled))},
        scratch_shapes=[
            pltpu.VMEM((count,) + piece, f32),
            pltpu.SemaphoreType.DMA((count,)),
        ],
        cost_estimate=pl.CostEstimate(
            flops=0, bytes_accessed=4 * count * math.prod(piece), transcendentals=0
        ),
        compiler_params=pltpu.CompilerParams(vmem_limit_bytes=30 * 1024 * 1024),
        name="spread",
    )(*sources, *filled)


def correlate_kernel(sizes, lags, factor, *refs):
    rows, cols, span, peers = sizes
    half_peers = peers // 2
    shares = refs[:half_peers]
    twin_shares_ref, s_high, s_low, mine_ref, other_ref = refs[half_peers : half_peers + 5]
    placed, flat, l_high, l_low = refs[half_peers + 5 :]
    reach = span // 2
    own = rows * cols
    double = shares[0].shape[1]
    share = double // 2
    width = s_high.shape[-1] // 2

    for k in range(half_peers):
        tile, twin = tiles_of(k, peers)
        placed[tile] = shares[k][0]
        placed[twin] = twin_shares_ref[k]

    total = peers * own
    side = round_up(reach * cols, 128)
    flat[:, :side] = jnp.zeros((double, side), f32)
    flat[:, side + total :] = jnp.zeros((double, side), f32)
    for tile in range(peers):
        flat[:, side + tile * own : side + (tile + 1) * own] = placed[tile]

    @pl.loop(0, 2)
    def _(part):
        rows_at = pl.ds(pl.multiple_of(part * share, 8), share)
        for a in range(span):
            start = side + (a - reach) * cols
            high, low = split(flat[rows_at, start : start + total])
            l_high[a, part] = high
            l_low[a, part] = low

    half = share // 2
    upper = lax.axis_index("col") % 2 == 1
    first_lag, count = lags

    @pl.loop(0, count)
    def _(n):
        b = first_lag + n
        left = tuple(ref[...].reshape(span * double, total) for ref in (l_high, l_low))
        product = dot3(left, (s_high[b], s_low[b])) * factor
        for a in range(span):
            top = product[a * double : a * double + share]
            bottom = product[a * double + share : (a + 1) * double]
            real = top[:, :width] + bottom[:, width:]
            imag = bottom[:, :width] - top[:, width:]
            for c, value in enumerate((real, imag)):
                mine_ref[a, n, c] = jnp.where(upper, value[half:], value[:half])
                other_ref[a, n, c] = jnp.where(upper, value[:half], value[half:])


def correlate(shares, twin_shares, s_high, s_low, lags, rows, cols, factor):
    peers = 2 * len(shares)
    span, total, lanes = s_high.shape
    reach = span // 2
    double, own = twin_shares.shape[1:]
    share = double // 2
    side = round_up(reach * cols, 128)
    vmem = pl.BlockSpec(memory_space=pltpu.VMEM)
    out = jax.ShapeDtypeStruct((span, lags[1], 2, share // 2, lanes // 2), f32)
    return pl.pallas_call(
        functools.partial(correlate_kernel, (rows, cols, span, peers), lags, factor),
        in_specs=[vmem] * (peers // 2 + 3),
        out_specs=[vmem, vmem],
        out_shape=[out, out],
        scratch_shapes=[
            pltpu.VMEM((peers, double, own), f32),
            pltpu.VMEM((double, total + 2 * side), f32),
            pltpu.VMEM((span, 2, share, total), bf16),
            pltpu.VMEM((span, 2, share, total), bf16),
        ],
        cost_estimate=pl.CostEstimate(
            flops=6 * span * double * total * lags[1] * lanes if lags[0] == 0 else 1,
            bytes_accessed=8 * out.size if lags[0] == 0 else 1,
            transcendentals=0,
        ),
        compiler_params=pltpu.CompilerParams(vmem_limit_bytes=17 * 1024 * 1024),
        name="correlate",
    )(*shares, twin_shares, s_high, s_low)


def parts_first_kernel(field_ref, out_ref):
    for part in range(2):
        out_ref[part] = field_ref[:, pl.ds(part, out_ref.shape[2], 2), :]


def parts_first(field):
    rows, cols, parts, width = field.shape
    vmem = pl.BlockSpec(memory_space=pltpu.VMEM)
    return pl.pallas_call(
        parts_first_kernel,
        in_specs=[vmem],
        out_specs=vmem,
        out_shape=jax.ShapeDtypeStruct((parts, rows, cols, width), f32),
        cost_estimate=pl.CostEstimate(flops=0, bytes_accessed=8 * field.size, transcendentals=0),
        compiler_params=pltpu.CompilerParams(vmem_limit_bytes=4 * 1024 * 1024),
        name="parts_first",
    )(field.reshape(rows, cols * parts, width))


def swap(value, axis, first):
    pairs = []
    for low in range(first, lax.axis_size(axis) - 1, 2):
        pairs += [(low, low + 1), (low + 1, low)]
    if not pairs:
        return jnp.zeros_like(value)
    return lax.ppermute(value, axis, pairs)


def shifted(value, axis, shift):
    peers = lax.axis_size(axis)
    if shift % peers == 0:
        return value
    return lax.ppermute(value, axis, [(i, (i + shift) % peers) for i in range(peers)])


def edges(initial, last, axis):
    even = lax.axis_index(axis) % 2 == 0
    shape = initial.shape
    initial, last = (value.reshape(shape[0], -1, shape[-1]) for value in (initial, last))
    outer = swap(jnp.where(even, initial, last), axis, 1).reshape(shape)
    inner = swap(jnp.where(even, last, initial), axis, 0).reshape(shape)
    return jnp.where(even, outer, inner), jnp.where(even, inner, outer), inner


def extended(value, axis, dim, width):
    length = value.shape[dim]
    initial = lax.slice_in_dim(value, 0, width, axis=dim)
    last = lax.slice_in_dim(value, length - width, length, axis=dim)
    before, after, inner = edges(initial, last, axis)
    return jnp.concatenate([before, value, after], axis=dim), inner


def on_device(adjoint_source, saved_currents, lag_blocks, element_inverse):
    rows, cols, parts, width = adjoint_source.shape
    span = lag_blocks.shape[0]
    reach = span // 2
    halo = SWEEPS * reach
    peers = lax.axis_size("row")

    source = adjoint_source.transpose(2, 0, 1, 3)
    saved = parts_first(saved_currents)
    source, _ = extended(source, "row", 1, halo)
    saved, _ = extended(saved, "col", 2, reach)
    saved = lax.optimization_barrier((saved, source))[0]
    source, inner = extended(source, "col", 2, halo)
    wide = round_up(cols + 2 * halo, 8)
    source = jnp.pad(source, ((0, 0), (0, 0), (0, wide - cols - 2 * halo), (0, 0)))

    saved = saved.reshape(parts, -1, width)
    pieces = {0: saved}
    behind = lax.optimization_barrier((saved, inner))[0]
    for k in sorted(range(1, peers // 2), key=lambda k: min(k, peers // 2 - k)):
        near = k in (1, peers // 2 - 1)
        pieces[k] = shifted(saved if near else behind, "row", 2 * k)
    pieces = [pieces[k] for k in range(peers // 2)]
    own_twin = swap(saved, "row", 0)

    second, own_source, high, low = first_sweep(source, element_inverse, lag_blocks, rows, cols)
    second, own_twin, early = lax.optimization_barrier((second, own_twin, jnp.stack([pieces[1], pieces[-1]])))
    early_twins = swap(early, "row", 0)
    adjoint, sends = second_sweep(second, own_source, element_inverse, high, low, peers)
    *late, sends = lax.optimization_barrier((*pieces[2:-1], sends))
    late_twins = swap(jnp.stack(late), "row", 0)
    shares = [shifted(send, "row", 2 * k) for k, send in enumerate(sends)]
    twin_shares = swap(jnp.stack([received[1] for received in shares]), "row", 0)

    last = peers // 2 - 1
    arrived = [(piece, ((k, 0),)) for k, piece in enumerate(pieces)]
    arrived += [(own_twin, ((0, 1),)), (early_twins, ((1, 1), (last, 1)))]
    spreads = spread(arrived, rows, cols, span, peers)
    late = [(late_twins, tuple((k, 1) for k in range(2, last)))]
    s_high, s_low = spread(late, rows, cols, span, peers, tuple(spreads))

    elements = rows * peers * cols * lax.axis_size("col")
    factor = -1.0 / math.sqrt(elements)
    even = lax.axis_index("col") % 2 == 0
    totals = []
    for lags in ((0, span),):
        mine, other = correlate(shares, twin_shares, s_high, s_low, lags, rows, cols, factor)
        mine = mine + swap(other, "col", 0)
        twin_shares, mine = lax.optimization_barrier((twin_shares, mine))
        for piece in (mine[: span // 2 + 1], mine[span // 2 + 1 :]):
            total = piece
            for k in range(2, lax.axis_size("col"), 2):
                total = total + shifted(piece, "col", k)
            totals.append(total)
    twins = [swap(total, "col", 0) for total in totals]
    total, twin = jnp.concatenate(totals, axis=0), jnp.concatenate(twins, axis=0)
    lag_grad = jnp.concatenate(
        [jnp.where(even, total, twin), jnp.where(even, twin, total)], axis=3
    )
    return (adjoint.reshape(adjoint_source.shape), lag_grad)


def solution(mesh):
    return jax.shard_map(
        on_device,
        mesh=mesh,
        in_specs=(P("row", "col", None, None), P("row", "col", None, None), P(), P()),
        out_specs=(P("row", "col", None, None), P(None, None, None, "row", None)),
        check_vma=False,
    )
```

```python
import functools
import math

import jax
import jax.numpy as jnp
from jax import lax
from jax.experimental import pallas as pl
from jax.experimental.pallas import tpu as pltpu
from jax.sharding import PartitionSpec as P

SWEEPS = 2

f32 = jnp.float32
bf16 = jnp.bfloat16


def split(value):
    high = value.astype(bf16)
    return high, (value - high.astype(f32)).astype(bf16)


def dot(left, right):
    return jnp.dot(left, right, preferred_element_type=f32)


def dot3(left, right):
    (left_high, left_low), (right_high, right_low) = left, right
    return dot(left_high, right_high) + dot(left_low, right_high) + dot(left_high, right_low)


def largest_divisor(count, most):
    return max(n for n in range(1, most + 1) if count % n == 0)


def round_up(count, unit):
    return (count + unit - 1) // unit * unit


def chip_along_z(z, shift, count):
    return (z + shift + count) % count


def store_block(ref, index, real, imag):
    width = real.shape[0]
    low, high = slice(0, width), slice(width, 2 * width)
    ref[index + (low, low)] = real
    ref[index + (low, high)] = -imag
    ref[index + (high, low)] = imag
    ref[index + (high, high)] = real


def inside(first_row, rows, cols, pitch, margin, tile_rows, tile_cols):
    at = lax.broadcasted_iota(jnp.int32, (rows * pitch, 1), 0)
    i = at // pitch
    j = at - i * pitch
    row = i + (first_row + lax.axis_index("row") * tile_rows - margin)
    col = j + (lax.axis_index("col") * tile_cols - margin)
    row_ok = (row >= 0) & (row < tile_rows * lax.axis_size("row"))
    col_ok = (col >= 0) & (col < tile_cols * lax.axis_size("col"))
    return row_ok & col_ok & (j < cols)


def store_inverse(inverse_ref, high_ref, low_ref):
    real_high, real_low = split(inverse_ref[0])
    imag_high, imag_low = split(inverse_ref[1])
    store_block(high_ref, (), real_high, imag_high)
    store_block(low_ref, (), real_low, imag_low)


def products(high, low, weight_high, weight_low):
    lanes = weight_high.shape[-1]
    weight_high = weight_high.reshape(-1, lanes)
    weight_low = weight_low.reshape(-1, lanes)
    return dot(high, weight_high) + dot(low, weight_high) + dot(high, weight_low)


def first_sweep_kernel(
    sizes,
    source_ref,
    inverse_ref,
    blocks_ref,
    second_ref,
    own_source_ref,
    w_high,
    w_low,
    first,
    x_high,
    x_low,
    acc,
    e_high,
    e_low,
):
    rows, cols, span, pitch, wide = sizes
    reach = span // 2
    mid_rows, mid_cols = rows + 2 * reach, cols + 2 * reach
    full_rows = rows + 4 * reach
    lanes = 2 * source_ref.shape[-1]

    def source_at(i, j):
        return jnp.concatenate([source_ref[0, i, j, :], source_ref[1, i, j, :]], axis=-1)

    store_inverse(inverse_ref, e_high, e_low)

    def invert(value):
        return dot3(split(value), (e_high[...], e_low[...]))

    own_source_ref[...] = source_at(pl.ds(2 * reach, rows), pl.ds(2 * reach, cols))

    step_rows = largest_divisor(full_rows, 12)

    @pl.loop(0, full_rows // step_rows)
    def _(s):
        at = pl.ds(s * step_rows, step_rows)
        piece = source_at(at, pl.ds(0, wide)).reshape(step_rows * wide, lanes)
        first[at] = invert(piece).reshape(step_rows, wide, lanes)

    first[full_rows] = jnp.zeros((wide, lanes), f32)

    @pl.loop(0, full_rows // 2)
    def _(s):
        for odd in range(2):
            for b in range(span):
                value = first[pl.ds(2 * s + odd, 2), pl.ds(b, pitch), :]
                high, low = split(value.reshape(2 * pitch, lanes))
                to = pl.ds(pl.multiple_of(s * 2 * pitch, 2 * pitch), 2 * pitch)
                x_high[odd, to, b * lanes : (b + 1) * lanes] = high
                x_low[odd, to, b * lanes : (b + 1) * lanes] = low

    acc[...] = jnp.zeros_like(acc)

    @pl.loop(0, span)
    def _(a):
        for b in range(span):
            real_high, real_low = split(blocks_ref[a, b, 0])
            imag_high, imag_low = split(blocks_ref[a, b, 1])
            store_block(w_high, (a, b), real_high, imag_high)
            store_block(w_low, (a, b), real_low, imag_low)

        at = pl.ds(pl.multiple_of((a // 2) * 2 * pitch, 2 * pitch), mid_rows * pitch)
        acc[...] += products(x_high[a % 2, at, :], x_low[a % 2, at, :], w_high[a], w_low[a])

    step_rows = largest_divisor(mid_rows, 18)

    @pl.loop(0, mid_rows // step_rows)
    def _(s):
        at = pl.ds(s * step_rows + reach, step_rows)
        count = step_rows * pitch
        flat = pl.ds(pl.multiple_of(s * count, 8), count)
        centre = first[at, pl.ds(reach, pitch), :].reshape(count, lanes)
        source = source_at(at, pl.ds(reach, pitch)).reshape(count, lanes)
        value = centre + invert(source - centre - acc[flat, :])
        mask = inside(s * step_rows, step_rows, mid_cols, pitch, reach, rows, cols)
        value = jnp.where(mask, value, 0.0)
        second_ref[pl.ds(s * step_rows, step_rows)] = value.reshape(step_rows, pitch, lanes)


def first_sweep(source, inverse, lag_blocks, rows, cols):
    span = lag_blocks.shape[0]
    reach = span // 2
    lanes = 2 * source.shape[-1]
    wide = source.shape[2]
    pitch = round_up(cols + 2 * reach, 8)
    full_rows, mid_rows = rows + 4 * reach, rows + 2 * reach
    vmem = pl.BlockSpec(memory_space=pltpu.VMEM)
    weights = (span, span, lanes, lanes)
    return pl.pallas_call(
        functools.partial(first_sweep_kernel, (rows, cols, span, pitch, wide)),
        in_specs=[vmem] * 3,
        out_specs=[vmem] * 4,
        out_shape=[
            jax.ShapeDtypeStruct((mid_rows, pitch, lanes), f32),
            jax.ShapeDtypeStruct((rows, cols, lanes), f32),
            jax.ShapeDtypeStruct(weights, bf16),
            jax.ShapeDtypeStruct(weights, bf16),
        ],
        scratch_shapes=[
            pltpu.VMEM((full_rows + 1, wide, lanes), f32),
            pltpu.VMEM((2, full_rows * pitch, span * lanes), bf16),
            pltpu.VMEM((2, full_rows * pitch, span * lanes), bf16),
            pltpu.VMEM((mid_rows * pitch, lanes), f32),
            pltpu.VMEM((lanes, lanes), bf16),
            pltpu.VMEM((lanes, lanes), bf16),
        ],
        cost_estimate=pl.CostEstimate(
            flops=6 * span * span * lanes * lanes * mid_rows * pitch,
            bytes_accessed=12 * lag_blocks.size,
            transcendentals=0,
        ),
        compiler_params=pltpu.CompilerParams(vmem_limit_bytes=32 * 1024 * 1024),
        name="first_sweep",
    )(source, inverse, lag_blocks)


def second_sweep_kernel(
    sizes,
    second_ref,
    source_ref,
    inverse_ref,
    w_high,
    w_low,
    adjoint_ref,
    *rest,
):
    rows, cols, span, peers = sizes
    sends = rest[: peers // 2]
    x_high, x_low, acc, turned, e_high, e_low = rest[peers // 2 :]
    reach = span // 2
    mid_rows = rows + 2 * reach
    own = rows * cols
    lanes = source_ref.shape[-1]
    width = lanes // 2

    store_inverse(inverse_ref, e_high, e_low)

    step_rows = largest_divisor(mid_rows, 3)

    @pl.loop(0, mid_rows // step_rows)
    def _(s):
        for b in range(span):
            at = pl.ds(s * step_rows, step_rows)
            value = second_ref[at, pl.ds(b, cols), :].reshape(step_rows * cols, lanes)
            high, low = split(value)
            to = pl.ds(pl.multiple_of(s * step_rows * cols, cols), step_rows * cols)
            x_high[to, b * lanes : (b + 1) * lanes] = high
            x_low[to, b * lanes : (b + 1) * lanes] = low

    acc[...] = jnp.zeros_like(acc)

    def one_lag(a):
        at = pl.ds(pl.multiple_of(a * cols, cols), own)
        return products(x_high[at, :], x_low[at, :], w_high[a], w_low[a])

    @pl.loop(0, span // 2)
    def _(pair):
        acc[...] += one_lag(2 * pair) + one_lag(2 * pair + 1)

    if span % 2:
        acc[...] += one_lag(span - 1)

    centre = second_ref[reach : reach + rows, pl.ds(reach, cols), :].reshape(own, lanes)
    source = source_ref[...].reshape(own, lanes)
    value = centre + dot3(split(source - centre - acc[...]), (e_high[...], e_low[...]))
    adjoint_ref[...] = value.reshape(adjoint_ref.shape)
    turned[...] = value.T

    share = width // peers
    me = lax.axis_index("row")
    parity = me % 2
    for k in range(peers // 2):
        base = 2 * chip_along_z(me // 2, k, peers // 2)
        for n, peer in enumerate((base + parity, base + 1 - parity)):
            for part in range(2):
                at = pl.multiple_of(part * width + peer * share, share)
                sends[k][n, part * share : (part + 1) * share, :] = turned[pl.ds(at, share), :]


def second_sweep(second, source, inverse, high, low, peers):
    span = high.shape[0]
    rows, cols, lanes = source.shape
    mid_rows = second.shape[0]
    share = lanes // 2 // peers
    vmem = pl.BlockSpec(memory_space=pltpu.VMEM)
    send = jax.ShapeDtypeStruct((2, 2 * share, rows * cols), f32)
    out = pl.pallas_call(
        functools.partial(second_sweep_kernel, (rows, cols, span, peers)),
        in_specs=[vmem] * 5,
        out_specs=[vmem] * (1 + peers // 2),
        out_shape=[jax.ShapeDtypeStruct((rows, cols, lanes), f32)] + [send] * (peers // 2),
        scratch_shapes=[
            pltpu.VMEM((mid_rows * cols, span * lanes), bf16),
            pltpu.VMEM((mid_rows * cols, span * lanes), bf16),
            pltpu.VMEM((rows * cols, lanes), f32),
            pltpu.VMEM((lanes, rows * cols), f32),
            pltpu.VMEM((lanes, lanes), bf16),
            pltpu.VMEM((lanes, lanes), bf16),
        ],
        cost_estimate=pl.CostEstimate(
            flops=6 * span * span * lanes * lanes * rows * cols,
            bytes_accessed=4 * high.size,
            transcendentals=0,
        ),
        compiler_params=pltpu.CompilerParams(vmem_limit_bytes=18 * 1024 * 1024),
        name="second_sweep",
    )(second, source, inverse, high, low)
    return out[0], out[1:]


def tiles_of(k, peers):
    me = lax.axis_index("row")
    parity = me % 2
    base = 2 * chip_along_z(me // 2, -k, peers // 2)
    return base + parity, base + 1 - parity


def spread_kernel(sizes, places, filled, *refs):
    rows, cols, span, peers = sizes
    count = len(places)
    sources = refs[:count]
    s_high, s_low, stage, sems = refs[count + filled :]
    own = rows * cols
    width = stage.shape[-1]
    copies = []
    at = 0
    for source, place in zip(sources, places):
        for n, (k, twin) in enumerate(place):
            piece = source.at[n] if len(source.shape) == 4 else source
            copies.append((pltpu.make_async_copy(piece, stage.at[at], sems.at[at]), tiles_of(k, peers)[twin]))
            copies[-1][0].start()
            at += 1

    for at, (copy, tile) in enumerate(copies):
        copy.wait()

        @pl.loop(0, rows)
        def _(i):
            to = pl.ds(pl.multiple_of(tile * own + i * cols, cols), cols)
            for b in range(span):
                for h in range(2):
                    start = i * (cols + span - 1) + span - 1 - b
                    high, low = split(stage[at, h, pl.ds(start, cols), :])
                    s_high[b, to, h * width : (h + 1) * width] = high
                    s_low[b, to, h * width : (h + 1) * width] = low


def spread(placed, rows, cols, span, peers, filled=()):
    sources, places = zip(*placed)
    piece = sources[0].shape[-3:]
    vmem = pl.BlockSpec(memory_space=pltpu.VMEM)
    hbm = pl.BlockSpec(memory_space=pltpu.HBM)
    out = jax.ShapeDtypeStruct((span, peers * rows * cols, 2 * piece[-1]), bf16)
    count = sum(len(place) for place in places)
    return pl.pallas_call(
        functools.partial(spread_kernel, (rows, cols, span, peers), places, len(filled)),
        in_specs=[hbm] * len(sources) + [vmem] * len(filled),
        out_specs=[vmem, vmem],
        out_shape=[out, out],
        input_output_aliases={len(sources) + n: n for n in range(len(filled))},
        scratch_shapes=[
            pltpu.VMEM((count,) + piece, f32),
            pltpu.SemaphoreType.DMA((count,)),
        ],
        cost_estimate=pl.CostEstimate(
            flops=0, bytes_accessed=4 * count * math.prod(piece), transcendentals=0
        ),
        compiler_params=pltpu.CompilerParams(vmem_limit_bytes=30 * 1024 * 1024),
        name="spread",
    )(*sources, *filled)


def correlate_kernel(sizes, lags, factor, *refs):
    rows, cols, span, peers = sizes
    half_peers = peers // 2
    shares = refs[:half_peers]
    twin_shares_ref, s_high, s_low, mine_ref, other_ref = refs[half_peers : half_peers + 5]
    placed, flat, l_high, l_low = refs[half_peers + 5 :]
    reach = span // 2
    own = rows * cols
    double = shares[0].shape[1]
    share = double // 2
    width = s_high.shape[-1] // 2

    for k in range(half_peers):
        tile, twin = tiles_of(k, peers)
        placed[tile] = shares[k][0]
        placed[twin] = twin_shares_ref[k]

    total = peers * own
    side = round_up(reach * cols, 128)
    flat[:, :side] = jnp.zeros((double, side), f32)
    flat[:, side + total :] = jnp.zeros((double, side), f32)
    for tile in range(peers):
        flat[:, side + tile * own : side + (tile + 1) * own] = placed[tile]

    @pl.loop(0, 2)
    def _(part):
        rows_at = pl.ds(pl.multiple_of(part * share, 8), share)
        for a in range(span):
            start = side + (a - reach) * cols
            high, low = split(flat[rows_at, start : start + total])
            l_high[a, part] = high
            l_low[a, part] = low

    half = share // 2
    upper = lax.axis_index("col") % 2 == 1
    first_lag, count = lags

    def one_lag(n):
        b = first_lag + n
        left = tuple(ref[...].reshape(span * double, total) for ref in (l_high, l_low))
        product = dot3(left, (s_high[b], s_low[b])) * factor
        for a in range(span):
            top = product[a * double : a * double + share]
            bottom = product[a * double + share : (a + 1) * double]
            real = top[:, :width] + bottom[:, width:]
            imag = bottom[:, :width] - top[:, width:]
            for c, value in enumerate((real, imag)):
                mine_ref[a, n, c] = jnp.where(upper, value[half:], value[:half])
                other_ref[a, n, c] = jnp.where(upper, value[:half], value[half:])

    for n in range(count):
        one_lag(n)


def correlate(shares, twin_shares, s_high, s_low, lags, rows, cols, factor):
    peers = 2 * len(shares)
    span, total, lanes = s_high.shape
    reach = span // 2
    double, own = twin_shares.shape[1:]
    share = double // 2
    side = round_up(reach * cols, 128)
    vmem = pl.BlockSpec(memory_space=pltpu.VMEM)
    out = jax.ShapeDtypeStruct((span, lags[1], 2, share // 2, lanes // 2), f32)
    return pl.pallas_call(
        functools.partial(correlate_kernel, (rows, cols, span, peers), lags, factor),
        in_specs=[vmem] * (peers // 2 + 3),
        out_specs=[vmem, vmem],
        out_shape=[out, out],
        scratch_shapes=[
            pltpu.VMEM((peers, double, own), f32),
            pltpu.VMEM((double, total + 2 * side), f32),
            pltpu.VMEM((span, 2, share, total), bf16),
            pltpu.VMEM((span, 2, share, total), bf16),
        ],
        cost_estimate=pl.CostEstimate(
            flops=6 * span * double * total * lags[1] * lanes if lags[0] == 0 else 1,
            bytes_accessed=8 * out.size if lags[0] == 0 else 1,
            transcendentals=0,
        ),
        compiler_params=pltpu.CompilerParams(vmem_limit_bytes=17 * 1024 * 1024),
        name="correlate",
    )(*shares, twin_shares, s_high, s_low)


def parts_first_kernel(field_ref, out_ref):
    for part in range(2):
        out_ref[part] = field_ref[:, pl.ds(part, out_ref.shape[2], 2), :]


def parts_first(field):
    rows, cols, parts, width = field.shape
    vmem = pl.BlockSpec(memory_space=pltpu.VMEM)
    return pl.pallas_call(
        parts_first_kernel,
        in_specs=[vmem],
        out_specs=vmem,
        out_shape=jax.ShapeDtypeStruct((parts, rows, cols, width), f32),
        cost_estimate=pl.CostEstimate(flops=0, bytes_accessed=8 * field.size, transcendentals=0),
        compiler_params=pltpu.CompilerParams(vmem_limit_bytes=4 * 1024 * 1024),
        name="parts_first",
    )(field.reshape(rows, cols * parts, width))


def swap(value, axis, first):
    pairs = []
    for low in range(first, lax.axis_size(axis) - 1, 2):
        pairs += [(low, low + 1), (low + 1, low)]
    if not pairs:
        return jnp.zeros_like(value)
    return lax.ppermute(value, axis, pairs)


def shifted(value, axis, shift):
    peers = lax.axis_size(axis)
    if shift % peers == 0:
        return value
    return lax.ppermute(value, axis, [(i, (i + shift) % peers) for i in range(peers)])


def edges(initial, last, axis):
    even = lax.axis_index(axis) % 2 == 0
    shape = initial.shape
    initial, last = (value.reshape(shape[0], -1, shape[-1]) for value in (initial, last))
    outer = swap(jnp.where(even, initial, last), axis, 1).reshape(shape)
    inner = swap(jnp.where(even, last, initial), axis, 0).reshape(shape)
    return jnp.where(even, outer, inner), jnp.where(even, inner, outer), inner


def extended(value, axis, dim, width):
    length = value.shape[dim]
    initial = lax.slice_in_dim(value, 0, width, axis=dim)
    last = lax.slice_in_dim(value, length - width, length, axis=dim)
    before, after, inner = edges(initial, last, axis)
    return jnp.concatenate([before, value, after], axis=dim), inner


def on_device(adjoint_source, saved_currents, lag_blocks, element_inverse):
    rows, cols, parts, width = adjoint_source.shape
    span = lag_blocks.shape[0]
    reach = span // 2
    halo = SWEEPS * reach
    peers = lax.axis_size("row")

    source = adjoint_source.transpose(2, 0, 1, 3)
    saved = parts_first(saved_currents)
    source, _ = extended(source, "row", 1, halo)
    saved, _ = extended(saved, "col", 2, reach)
    saved = lax.optimization_barrier((saved, source))[0]
    source, inner = extended(source, "col", 2, halo)
    wide = round_up(cols + 2 * halo, 8)
    source = jnp.pad(source, ((0, 0), (0, 0), (0, wide - cols - 2 * halo), (0, 0)))

    saved = saved.reshape(parts, -1, width)
    pieces = {0: saved}
    behind = lax.optimization_barrier((saved, inner))[0]
    for k in sorted(range(1, peers // 2), key=lambda k: min(k, peers // 2 - k)):
        near = k in (1, peers // 2 - 1)
        pieces[k] = shifted(saved if near else behind, "row", 2 * k)
    pieces = [pieces[k] for k in range(peers // 2)]
    own_twin = swap(saved, "row", 0)

    second, own_source, high, low = first_sweep(source, element_inverse, lag_blocks, rows, cols)
    second, own_twin, early = lax.optimization_barrier((second, own_twin, jnp.stack([pieces[1], pieces[-1]])))
    early_twins = swap(early, "row", 0)
    adjoint, sends = second_sweep(second, own_source, element_inverse, high, low, peers)
    adjoint = adjoint.reshape(adjoint_source.shape)
    *late, sends = lax.optimization_barrier((*pieces[2:-1], sends))
    late_twins = swap(jnp.stack(late), "row", 0)
    shares = [shifted(send, "row", 2 * k) for k, send in enumerate(sends)]
    twin_shares = swap(jnp.stack([received[1] for received in shares]), "row", 0)

    last = peers // 2 - 1
    arrived = [(piece, ((k, 0),)) for k, piece in enumerate(pieces)]
    arrived += [(own_twin, ((0, 1),)), (early_twins, ((1, 1), (last, 1)))]
    spreads = spread(arrived, rows, cols, span, peers)
    late = [(late_twins, tuple((k, 1) for k in range(2, last)))]
    s_high, s_low = spread(late, rows, cols, span, peers, tuple(spreads))

    elements = rows * peers * cols * lax.axis_size("col")
    factor = -1.0 / math.sqrt(elements)
    even = lax.axis_index("col") % 2 == 0
    totals = []
    for lags in ((0, span),):
        mine, other = correlate(shares, twin_shares, s_high, s_low, lags, rows, cols, factor)
        mine = mine + swap(other, "col", 0)
        mine, adjoint = lax.optimization_barrier((mine, adjoint))
        for piece in (mine[: span // 2 + 1], mine[span // 2 + 1 :]):
            total = piece
            for k in range(2, lax.axis_size("col"), 2):
                total = total + shifted(piece, "col", k)
            totals.append(total)
    twins = [swap(total, "col", 0) for total in totals]
    total, twin = jnp.concatenate(totals, axis=0), jnp.concatenate(twins, axis=0)
    lag_grad = jnp.concatenate(
        [jnp.where(even, total, twin), jnp.where(even, twin, total)], axis=3
    )
    return (adjoint, lag_grad)


def solution(mesh):
    return jax.shard_map(
        on_device,
        mesh=mesh,
        in_specs=(P("row", "col", None, None), P("row", "col", None, None), P(), P()),
        out_specs=(P("row", "col", None, None), P(None, None, None, "row", None)),
        check_vma=False,
    )
```

```python
import functools
import math

import jax
import jax.numpy as jnp
from jax import lax
from jax.experimental import pallas as pl
from jax.experimental.pallas import tpu as pltpu
from jax.sharding import PartitionSpec as P

SWEEPS = 2

f32 = jnp.float32
bf16 = jnp.bfloat16


def split(value):
    high = value.astype(bf16)
    return high, (value - high.astype(f32)).astype(bf16)


def dot(left, right):
    return jnp.dot(left, right, preferred_element_type=f32)


def dot3(left, right):
    (left_high, left_low), (right_high, right_low) = left, right
    return dot(left_high, right_high) + dot(left_low, right_high) + dot(left_high, right_low)


def largest_divisor(count, most):
    return max(n for n in range(1, most + 1) if count % n == 0)


def round_up(count, unit):
    return (count + unit - 1) // unit * unit


def chip_along_z(z, shift, count):
    return (z + shift + count) % count


def store_block(ref, index, real, imag):
    width = real.shape[0]
    low, high = slice(0, width), slice(width, 2 * width)
    ref[index + (low, low)] = real
    ref[index + (low, high)] = -imag
    ref[index + (high, low)] = imag
    ref[index + (high, high)] = real


def inside(first_row, rows, cols, pitch, margin, tile_rows, tile_cols):
    at = lax.broadcasted_iota(jnp.int32, (rows * pitch, 1), 0)
    i = at // pitch
    j = at - i * pitch
    row = i + (first_row + lax.axis_index("row") * tile_rows - margin)
    col = j + (lax.axis_index("col") * tile_cols - margin)
    row_ok = (row >= 0) & (row < tile_rows * lax.axis_size("row"))
    col_ok = (col >= 0) & (col < tile_cols * lax.axis_size("col"))
    return row_ok & col_ok & (j < cols)


def store_inverse(inverse_ref, high_ref, low_ref):
    real_high, real_low = split(inverse_ref[0])
    imag_high, imag_low = split(inverse_ref[1])
    store_block(high_ref, (), real_high, imag_high)
    store_block(low_ref, (), real_low, imag_low)


def products(high, low, weight_high, weight_low):
    lanes = weight_high.shape[-1]
    weight_high = weight_high.reshape(-1, lanes)
    weight_low = weight_low.reshape(-1, lanes)
    return dot(high, weight_high) + dot(low, weight_high) + dot(high, weight_low)


def first_sweep_kernel(
    sizes,
    source_ref,
    inverse_ref,
    blocks_ref,
    second_ref,
    own_source_ref,
    w_high,
    w_low,
    first,
    x_high,
    x_low,
    acc,
    e_high,
    e_low,
):
    rows, cols, span, pitch, wide = sizes
    reach = span // 2
    mid_rows, mid_cols = rows + 2 * reach, cols + 2 * reach
    full_rows = rows + 4 * reach
    lanes = 2 * source_ref.shape[-1]

    def source_at(i, j):
        return jnp.concatenate([source_ref[0, i, j, :], source_ref[1, i, j, :]], axis=-1)

    store_inverse(inverse_ref, e_high, e_low)

    def invert(value):
        return dot3(split(value), (e_high[...], e_low[...]))

    own_source_ref[...] = source_at(pl.ds(2 * reach, rows), pl.ds(2 * reach, cols))

    step_rows = largest_divisor(full_rows, 12)

    @pl.loop(0, full_rows // step_rows)
    def _(s):
        at = pl.ds(s * step_rows, step_rows)
        piece = source_at(at, pl.ds(0, wide)).reshape(step_rows * wide, lanes)
        first[at] = invert(piece).reshape(step_rows, wide, lanes)

    first[full_rows] = jnp.zeros((wide, lanes), f32)

    @pl.loop(0, full_rows // 2)
    def _(s):
        for odd in range(2):
            for b in range(span):
                value = first[pl.ds(2 * s + odd, 2), pl.ds(b, pitch), :]
                high, low = split(value.reshape(2 * pitch, lanes))
                to = pl.ds(pl.multiple_of(s * 2 * pitch, 2 * pitch), 2 * pitch)
                x_high[odd, to, b * lanes : (b + 1) * lanes] = high
                x_low[odd, to, b * lanes : (b + 1) * lanes] = low

    acc[...] = jnp.zeros_like(acc)

    def one_lag(a):
        for b in range(span):
            real_high, real_low = split(blocks_ref[a, b, 0])
            imag_high, imag_low = split(blocks_ref[a, b, 1])
            store_block(w_high, (a, b), real_high, imag_high)
            store_block(w_low, (a, b), real_low, imag_low)

        at = pl.ds(pl.multiple_of((a // 2) * 2 * pitch, 2 * pitch), mid_rows * pitch)
        return products(x_high[a % 2, at, :], x_low[a % 2, at, :], w_high[a], w_low[a])

    @pl.loop(0, span // 2)
    def _(pair):
        acc[...] += one_lag(2 * pair) + one_lag(2 * pair + 1)

    if span % 2:
        acc[...] += one_lag(span - 1)

    step_rows = largest_divisor(mid_rows, 18)

    @pl.loop(0, mid_rows // step_rows)
    def _(s):
        at = pl.ds(s * step_rows + reach, step_rows)
        count = step_rows * pitch
        flat = pl.ds(pl.multiple_of(s * count, 8), count)
        centre = first[at, pl.ds(reach, pitch), :].reshape(count, lanes)
        source = source_at(at, pl.ds(reach, pitch)).reshape(count, lanes)
        value = centre + invert(source - centre - acc[flat, :])
        mask = inside(s * step_rows, step_rows, mid_cols, pitch, reach, rows, cols)
        value = jnp.where(mask, value, 0.0)
        second_ref[pl.ds(s * step_rows, step_rows)] = value.reshape(step_rows, pitch, lanes)


def first_sweep(source, inverse, lag_blocks, rows, cols):
    span = lag_blocks.shape[0]
    reach = span // 2
    lanes = 2 * source.shape[-1]
    wide = source.shape[2]
    pitch = round_up(cols + 2 * reach, 8)
    full_rows, mid_rows = rows + 4 * reach, rows + 2 * reach
    vmem = pl.BlockSpec(memory_space=pltpu.VMEM)
    weights = (span, span, lanes, lanes)
    return pl.pallas_call(
        functools.partial(first_sweep_kernel, (rows, cols, span, pitch, wide)),
        in_specs=[vmem] * 3,
        out_specs=[vmem] * 4,
        out_shape=[
            jax.ShapeDtypeStruct((mid_rows, pitch, lanes), f32),
            jax.ShapeDtypeStruct((rows, cols, lanes), f32),
            jax.ShapeDtypeStruct(weights, bf16),
            jax.ShapeDtypeStruct(weights, bf16),
        ],
        scratch_shapes=[
            pltpu.VMEM((full_rows + 1, wide, lanes), f32),
            pltpu.VMEM((2, full_rows * pitch, span * lanes), bf16),
            pltpu.VMEM((2, full_rows * pitch, span * lanes), bf16),
            pltpu.VMEM((mid_rows * pitch, lanes), f32),
            pltpu.VMEM((lanes, lanes), bf16),
            pltpu.VMEM((lanes, lanes), bf16),
        ],
        cost_estimate=pl.CostEstimate(
            flops=6 * span * span * lanes * lanes * mid_rows * pitch,
            bytes_accessed=12 * lag_blocks.size,
            transcendentals=0,
        ),
        compiler_params=pltpu.CompilerParams(vmem_limit_bytes=32 * 1024 * 1024),
        name="first_sweep",
    )(source, inverse, lag_blocks)


def second_sweep_kernel(
    sizes,
    second_ref,
    source_ref,
    inverse_ref,
    w_high,
    w_low,
    adjoint_ref,
    *rest,
):
    rows, cols, span, peers = sizes
    sends = rest[: peers // 2]
    x_high, x_low, acc, turned, e_high, e_low = rest[peers // 2 :]
    reach = span // 2
    mid_rows = rows + 2 * reach
    own = rows * cols
    lanes = source_ref.shape[-1]
    width = lanes // 2

    store_inverse(inverse_ref, e_high, e_low)

    step_rows = largest_divisor(mid_rows, 3)

    @pl.loop(0, mid_rows // step_rows)
    def _(s):
        for b in range(span):
            at = pl.ds(s * step_rows, step_rows)
            value = second_ref[at, pl.ds(b, cols), :].reshape(step_rows * cols, lanes)
            high, low = split(value)
            to = pl.ds(pl.multiple_of(s * step_rows * cols, cols), step_rows * cols)
            x_high[to, b * lanes : (b + 1) * lanes] = high
            x_low[to, b * lanes : (b + 1) * lanes] = low

    acc[...] = jnp.zeros_like(acc)

    def one_lag(a):
        at = pl.ds(pl.multiple_of(a * cols, cols), own)
        return products(x_high[at, :], x_low[at, :], w_high[a], w_low[a])

    @pl.loop(0, span // 2)
    def _(pair):
        acc[...] += one_lag(2 * pair) + one_lag(2 * pair + 1)

    if span % 2:
        acc[...] += one_lag(span - 1)

    centre = second_ref[reach : reach + rows, pl.ds(reach, cols), :].reshape(own, lanes)
    source = source_ref[...].reshape(own, lanes)
    value = centre + dot3(split(source - centre - acc[...]), (e_high[...], e_low[...]))
    adjoint_ref[...] = value.reshape(adjoint_ref.shape)
    turned[...] = value.T

    share = width // peers
    me = lax.axis_index("row")
    parity = me % 2
    for k in range(peers // 2):
        base = 2 * chip_along_z(me // 2, k, peers // 2)
        for n, peer in enumerate((base + parity, base + 1 - parity)):
            for part in range(2):
                at = pl.multiple_of(part * width + peer * share, share)
                sends[k][n, part * share : (part + 1) * share, :] = turned[pl.ds(at, share), :]


def second_sweep(second, source, inverse, high, low, peers):
    span = high.shape[0]
    rows, cols, lanes = source.shape
    mid_rows = second.shape[0]
    share = lanes // 2 // peers
    vmem = pl.BlockSpec(memory_space=pltpu.VMEM)
    send = jax.ShapeDtypeStruct((2, 2 * share, rows * cols), f32)
    out = pl.pallas_call(
        functools.partial(second_sweep_kernel, (rows, cols, span, peers)),
        in_specs=[vmem] * 5,
        out_specs=[vmem] * (1 + peers // 2),
        out_shape=[jax.ShapeDtypeStruct((rows, cols, lanes), f32)] + [send] * (peers // 2),
        scratch_shapes=[
            pltpu.VMEM((mid_rows * cols, span * lanes), bf16),
            pltpu.VMEM((mid_rows * cols, span * lanes), bf16),
            pltpu.VMEM((rows * cols, lanes), f32),
            pltpu.VMEM((lanes, rows * cols), f32),
            pltpu.VMEM((lanes, lanes), bf16),
            pltpu.VMEM((lanes, lanes), bf16),
        ],
        cost_estimate=pl.CostEstimate(
            flops=6 * span * span * lanes * lanes * rows * cols,
            bytes_accessed=4 * high.size,
            transcendentals=0,
        ),
        compiler_params=pltpu.CompilerParams(vmem_limit_bytes=18 * 1024 * 1024),
        name="second_sweep",
    )(second, source, inverse, high, low)
    return out[0], out[1:]


def tiles_of(k, peers):
    me = lax.axis_index("row")
    parity = me % 2
    base = 2 * chip_along_z(me // 2, -k, peers // 2)
    return base + parity, base + 1 - parity


def spread_kernel(sizes, places, filled, *refs):
    rows, cols, span, peers = sizes
    count = len(places)
    sources = refs[:count]
    s_high, s_low, stage, sems = refs[count + filled :]
    own = rows * cols
    width = stage.shape[-1]
    copies = []
    at = 0
    for source, place in zip(sources, places):
        for n, (k, twin) in enumerate(place):
            piece = source.at[n] if len(source.shape) == 4 else source
            copies.append((pltpu.make_async_copy(piece, stage.at[at], sems.at[at]), tiles_of(k, peers)[twin]))
            copies[-1][0].start()
            at += 1

    for at, (copy, tile) in enumerate(copies):
        copy.wait()

        @pl.loop(0, rows)
        def _(i):
            to = pl.ds(pl.multiple_of(tile * own + i * cols, cols), cols)
            for b in range(span):
                for h in range(2):
                    start = i * (cols + span - 1) + span - 1 - b
                    high, low = split(stage[at, h, pl.ds(start, cols), :])
                    s_high[b, to, h * width : (h + 1) * width] = high
                    s_low[b, to, h * width : (h + 1) * width] = low


def spread(placed, rows, cols, span, peers, filled=()):
    sources, places = zip(*placed)
    piece = sources[0].shape[-3:]
    vmem = pl.BlockSpec(memory_space=pltpu.VMEM)
    hbm = pl.BlockSpec(memory_space=pltpu.HBM)
    out = jax.ShapeDtypeStruct((span, peers * rows * cols, 2 * piece[-1]), bf16)
    count = sum(len(place) for place in places)
    return pl.pallas_call(
        functools.partial(spread_kernel, (rows, cols, span, peers), places, len(filled)),
        in_specs=[hbm] * len(sources) + [vmem] * len(filled),
        out_specs=[vmem, vmem],
        out_shape=[out, out],
        input_output_aliases={len(sources) + n: n for n in range(len(filled))},
        scratch_shapes=[
            pltpu.VMEM((count,) + piece, f32),
            pltpu.SemaphoreType.DMA((count,)),
        ],
        cost_estimate=pl.CostEstimate(
            flops=0, bytes_accessed=4 * count * math.prod(piece), transcendentals=0
        ),
        compiler_params=pltpu.CompilerParams(vmem_limit_bytes=30 * 1024 * 1024),
        name="spread",
    )(*sources, *filled)


def correlate_kernel(sizes, lags, factor, *refs):
    rows, cols, span, peers = sizes
    half_peers = peers // 2
    shares = refs[:half_peers]
    twin_shares_ref, s_high, s_low, mine_ref, other_ref = refs[half_peers : half_peers + 5]
    placed, flat, l_high, l_low = refs[half_peers + 5 :]
    reach = span // 2
    own = rows * cols
    double = shares[0].shape[1]
    share = double // 2
    width = s_high.shape[-1] // 2

    for k in range(half_peers):
        tile, twin = tiles_of(k, peers)
        placed[tile] = shares[k][0]
        placed[twin] = twin_shares_ref[k]

    total = peers * own
    side = round_up(reach * cols, 128)
    flat[:, :side] = jnp.zeros((double, side), f32)
    flat[:, side + total :] = jnp.zeros((double, side), f32)
    for tile in range(peers):
        flat[:, side + tile * own : side + (tile + 1) * own] = placed[tile]

    @pl.loop(0, 2)
    def _(part):
        rows_at = pl.ds(pl.multiple_of(part * share, 8), share)
        for a in range(span):
            start = side + (a - reach) * cols
            high, low = split(flat[rows_at, start : start + total])
            l_high[a, part] = high
            l_low[a, part] = low

    half = share // 2
    upper = lax.axis_index("col") % 2 == 1
    first_lag, count = lags

    def one_lag(n):
        b = first_lag + n
        left = tuple(ref[...].reshape(span * double, total) for ref in (l_high, l_low))
        product = dot3(left, (s_high[b], s_low[b])) * factor
        for a in range(span):
            top = product[a * double : a * double + share]
            bottom = product[a * double + share : (a + 1) * double]
            real = top[:, :width] + bottom[:, width:]
            imag = bottom[:, :width] - top[:, width:]
            for c, value in enumerate((real, imag)):
                mine_ref[a, n, c] = jnp.where(upper, value[half:], value[:half])
                other_ref[a, n, c] = jnp.where(upper, value[:half], value[half:])

    for n in range(count):
        one_lag(n)


def correlate(shares, twin_shares, s_high, s_low, lags, rows, cols, factor):
    peers = 2 * len(shares)
    span, total, lanes = s_high.shape
    reach = span // 2
    double, own = twin_shares.shape[1:]
    share = double // 2
    side = round_up(reach * cols, 128)
    vmem = pl.BlockSpec(memory_space=pltpu.VMEM)
    out = jax.ShapeDtypeStruct((span, lags[1], 2, share // 2, lanes // 2), f32)
    return pl.pallas_call(
        functools.partial(correlate_kernel, (rows, cols, span, peers), lags, factor),
        in_specs=[vmem] * (peers // 2 + 3),
        out_specs=[vmem, vmem],
        out_shape=[out, out],
        scratch_shapes=[
            pltpu.VMEM((peers, double, own), f32),
            pltpu.VMEM((double, total + 2 * side), f32),
            pltpu.VMEM((span, 2, share, total), bf16),
            pltpu.VMEM((span, 2, share, total), bf16),
        ],
        cost_estimate=pl.CostEstimate(
            flops=6 * span * double * total * lags[1] * lanes if lags[0] == 0 else 1,
            bytes_accessed=8 * out.size if lags[0] == 0 else 1,
            transcendentals=0,
        ),
        compiler_params=pltpu.CompilerParams(vmem_limit_bytes=17 * 1024 * 1024),
        name="correlate",
    )(*shares, twin_shares, s_high, s_low)


def parts_first_kernel(field_ref, out_ref):
    for part in range(2):
        out_ref[part] = field_ref[:, pl.ds(part, out_ref.shape[2], 2), :]


def parts_first(field):
    rows, cols, parts, width = field.shape
    vmem = pl.BlockSpec(memory_space=pltpu.VMEM)
    return pl.pallas_call(
        parts_first_kernel,
        in_specs=[vmem],
        out_specs=vmem,
        out_shape=jax.ShapeDtypeStruct((parts, rows, cols, width), f32),
        cost_estimate=pl.CostEstimate(flops=0, bytes_accessed=8 * field.size, transcendentals=0),
        compiler_params=pltpu.CompilerParams(vmem_limit_bytes=4 * 1024 * 1024),
        name="parts_first",
    )(field.reshape(rows, cols * parts, width))


def swap(value, axis, first):
    pairs = []
    for low in range(first, lax.axis_size(axis) - 1, 2):
        pairs += [(low, low + 1), (low + 1, low)]
    if not pairs:
        return jnp.zeros_like(value)
    return lax.ppermute(value, axis, pairs)


def shifted(value, axis, shift):
    peers = lax.axis_size(axis)
    if shift % peers == 0:
        return value
    return lax.ppermute(value, axis, [(i, (i + shift) % peers) for i in range(peers)])


def edges(initial, last, axis):
    even = lax.axis_index(axis) % 2 == 0
    shape = initial.shape
    initial, last = (value.reshape(shape[0], -1, shape[-1]) for value in (initial, last))
    outer = swap(jnp.where(even, initial, last), axis, 1).reshape(shape)
    inner = swap(jnp.where(even, last, initial), axis, 0).reshape(shape)
    return jnp.where(even, outer, inner), jnp.where(even, inner, outer), inner


def extended(value, axis, dim, width):
    length = value.shape[dim]
    initial = lax.slice_in_dim(value, 0, width, axis=dim)
    last = lax.slice_in_dim(value, length - width, length, axis=dim)
    before, after, inner = edges(initial, last, axis)
    return jnp.concatenate([before, value, after], axis=dim), inner


def on_device(adjoint_source, saved_currents, lag_blocks, element_inverse):
    rows, cols, parts, width = adjoint_source.shape
    span = lag_blocks.shape[0]
    reach = span // 2
    halo = SWEEPS * reach
    peers = lax.axis_size("row")

    source = adjoint_source.transpose(2, 0, 1, 3)
    saved = parts_first(saved_currents)
    source, _ = extended(source, "row", 1, halo)
    saved, _ = extended(saved, "col", 2, reach)
    saved = lax.optimization_barrier((saved, source))[0]
    source, inner = extended(source, "col", 2, halo)
    wide = round_up(cols + 2 * halo, 8)
    source = jnp.pad(source, ((0, 0), (0, 0), (0, wide - cols - 2 * halo), (0, 0)))

    saved = saved.reshape(parts, -1, width)
    pieces = {0: saved}
    behind = lax.optimization_barrier((saved, inner))[0]
    for k in sorted(range(1, peers // 2), key=lambda k: min(k, peers // 2 - k)):
        near = k in (1, peers // 2 - 1)
        pieces[k] = shifted(saved if near else behind, "row", 2 * k)
    pieces = [pieces[k] for k in range(peers // 2)]
    own_twin = swap(saved, "row", 0)

    second, own_source, high, low = first_sweep(source, element_inverse, lag_blocks, rows, cols)
    second, own_twin, early = lax.optimization_barrier((second, own_twin, jnp.stack([pieces[1], pieces[-1]])))
    early_twins = swap(early, "row", 0)
    adjoint, sends = second_sweep(second, own_source, element_inverse, high, low, peers)
    adjoint = adjoint.reshape(adjoint_source.shape)
    *late, sends = lax.optimization_barrier((*pieces[2:-1], sends))
    late_twins = swap(jnp.stack(late), "row", 0)
    shares = [shifted(send, "row", 2 * k) for k, send in enumerate(sends)]
    twin_shares = swap(jnp.stack([received[1] for received in shares]), "row", 0)

    last = peers // 2 - 1
    arrived = [(piece, ((k, 0),)) for k, piece in enumerate(pieces)]
    arrived += [(own_twin, ((0, 1),)), (early_twins, ((1, 1), (last, 1)))]
    spreads = spread(arrived, rows, cols, span, peers)
    late = [(late_twins, tuple((k, 1) for k in range(2, last)))]
    s_high, s_low = spread(late, rows, cols, span, peers, tuple(spreads))

    elements = rows * peers * cols * lax.axis_size("col")
    factor = -1.0 / math.sqrt(elements)
    even = lax.axis_index("col") % 2 == 0
    totals = []
    for lags in ((0, span),):
        mine, other = correlate(shares, twin_shares, s_high, s_low, lags, rows, cols, factor)
        mine = mine + swap(other, "col", 0)
        mine, adjoint = lax.optimization_barrier((mine, adjoint))
        for piece in (mine[: span // 2 + 1], mine[span // 2 + 1 :]):
            total = piece
            for k in range(2, lax.axis_size("col"), 2):
                total = total + shifted(piece, "col", k)
            totals.append(total)
    twins = [swap(total, "col", 0) for total in totals]
    total, twin = jnp.concatenate(totals, axis=0), jnp.concatenate(twins, axis=0)
    lag_grad = jnp.concatenate(
        [jnp.where(even, total, twin), jnp.where(even, twin, total)], axis=3
    )
    return (adjoint, lag_grad)


def solution(mesh):
    return jax.shard_map(
        on_device,
        mesh=mesh,
        in_specs=(P("row", "col", None, None), P("row", "col", None, None), P(), P()),
        out_specs=(P("row", "col", None, None), P(None, None, None, "row", None)),
        check_vma=False,
    )
```

```python
import functools
import math

import jax
import jax.numpy as jnp
from jax import lax
from jax.experimental import pallas as pl
from jax.experimental.pallas import tpu as pltpu
from jax.sharding import PartitionSpec as P

SWEEPS = 2

f32 = jnp.float32
bf16 = jnp.bfloat16


def split(value):
    high = value.astype(bf16)
    return high, (value - high.astype(f32)).astype(bf16)


def dot(left, right):
    return jnp.dot(left, right, preferred_element_type=f32)


def dot3(left, right):
    (left_high, left_low), (right_high, right_low) = left, right
    return dot(left_high, right_high) + dot(left_low, right_high) + dot(left_high, right_low)


def largest_divisor(count, most):
    return max(n for n in range(1, most + 1) if count % n == 0)


def round_up(count, unit):
    return (count + unit - 1) // unit * unit


def chip_along_z(z, shift, count):
    return (z + shift + count) % count


def store_block(ref, index, real, imag):
    width = real.shape[0]
    low, high = slice(0, width), slice(width, 2 * width)
    ref[index + (low, low)] = real
    ref[index + (low, high)] = -imag
    ref[index + (high, low)] = imag
    ref[index + (high, high)] = real


def inside(first_row, rows, cols, pitch, margin, tile_rows, tile_cols):
    at = lax.broadcasted_iota(jnp.int32, (rows * pitch, 1), 0)
    i = at // pitch
    j = at - i * pitch
    row = i + (first_row + lax.axis_index("row") * tile_rows - margin)
    col = j + (lax.axis_index("col") * tile_cols - margin)
    row_ok = (row >= 0) & (row < tile_rows * lax.axis_size("row"))
    col_ok = (col >= 0) & (col < tile_cols * lax.axis_size("col"))
    return row_ok & col_ok & (j < cols)


def store_inverse(inverse_ref, high_ref, low_ref):
    real_high, real_low = split(inverse_ref[0])
    imag_high, imag_low = split(inverse_ref[1])
    store_block(high_ref, (), real_high, imag_high)
    store_block(low_ref, (), real_low, imag_low)


def products(high, low, weight_high, weight_low):
    lanes = weight_high.shape[-1]
    weight_high = weight_high.reshape(-1, lanes)
    weight_low = weight_low.reshape(-1, lanes)
    return dot(high, weight_high) + dot(low, weight_high) + dot(high, weight_low)


def first_sweep_kernel(
    sizes,
    source_ref,
    inverse_ref,
    blocks_ref,
    second_ref,
    own_source_ref,
    w_high,
    w_low,
    first,
    x_high,
    x_low,
    acc,
    e_high,
    e_low,
):
    rows, cols, span, pitch, wide = sizes
    reach = span // 2
    mid_rows, mid_cols = rows + 2 * reach, cols + 2 * reach
    full_rows = rows + 4 * reach
    lanes = 2 * source_ref.shape[-1]

    def source_at(i, j):
        return jnp.concatenate([source_ref[0, i, j, :], source_ref[1, i, j, :]], axis=-1)

    store_inverse(inverse_ref, e_high, e_low)

    def invert(value):
        return dot3(split(value), (e_high[...], e_low[...]))

    own_source_ref[...] = source_at(pl.ds(2 * reach, rows), pl.ds(2 * reach, cols))

    step_rows = largest_divisor(full_rows, 12)

    @pl.loop(0, full_rows // step_rows)
    def _(s):
        at = pl.ds(s * step_rows, step_rows)
        piece = source_at(at, pl.ds(0, wide)).reshape(step_rows * wide, lanes)
        first[at] = invert(piece).reshape(step_rows, wide, lanes)

    first[full_rows] = jnp.zeros((wide, lanes), f32)

    step_rows = 2 * largest_divisor(full_rows // 2, 3)

    @pl.loop(0, full_rows // step_rows)
    def _(s):
        for odd in range(2):
            for b in range(span):
                value = first[pl.ds(s * step_rows + odd, step_rows), pl.ds(b, pitch), :]
                count = step_rows * pitch
                high, low = split(value.reshape(count, lanes))
                to = pl.ds(pl.multiple_of(s * count, 2 * pitch), count)
                x_high[odd, to, b * lanes : (b + 1) * lanes] = high
                x_low[odd, to, b * lanes : (b + 1) * lanes] = low

    acc[...] = jnp.zeros_like(acc)

    def one_lag(a):
        for b in range(span):
            real_high, real_low = split(blocks_ref[a, b, 0])
            imag_high, imag_low = split(blocks_ref[a, b, 1])
            store_block(w_high, (a, b), real_high, imag_high)
            store_block(w_low, (a, b), real_low, imag_low)

        at = pl.ds(pl.multiple_of((a // 2) * 2 * pitch, 2 * pitch), mid_rows * pitch)
        return products(x_high[a % 2, at, :], x_low[a % 2, at, :], w_high[a], w_low[a])

    @pl.loop(0, span // 2)
    def _(pair):
        acc[...] += one_lag(2 * pair) + one_lag(2 * pair + 1)

    if span % 2:
        acc[...] += one_lag(span - 1)

    step_rows = largest_divisor(mid_rows, 18)

    @pl.loop(0, mid_rows // step_rows)
    def _(s):
        at = pl.ds(s * step_rows + reach, step_rows)
        count = step_rows * pitch
        flat = pl.ds(pl.multiple_of(s * count, 8), count)
        centre = first[at, pl.ds(reach, pitch), :].reshape(count, lanes)
        source = source_at(at, pl.ds(reach, pitch)).reshape(count, lanes)
        value = centre + invert(source - centre - acc[flat, :])
        mask = inside(s * step_rows, step_rows, mid_cols, pitch, reach, rows, cols)
        value = jnp.where(mask, value, 0.0)
        second_ref[pl.ds(s * step_rows, step_rows)] = value.reshape(step_rows, pitch, lanes)


def first_sweep(source, inverse, lag_blocks, rows, cols):
    span = lag_blocks.shape[0]
    reach = span // 2
    lanes = 2 * source.shape[-1]
    wide = source.shape[2]
    pitch = round_up(cols + 2 * reach, 8)
    full_rows, mid_rows = rows + 4 * reach, rows + 2 * reach
    vmem = pl.BlockSpec(memory_space=pltpu.VMEM)
    weights = (span, span, lanes, lanes)
    return pl.pallas_call(
        functools.partial(first_sweep_kernel, (rows, cols, span, pitch, wide)),
        in_specs=[vmem] * 3,
        out_specs=[vmem] * 4,
        out_shape=[
            jax.ShapeDtypeStruct((mid_rows, pitch, lanes), f32),
            jax.ShapeDtypeStruct((rows, cols, lanes), f32),
            jax.ShapeDtypeStruct(weights, bf16),
            jax.ShapeDtypeStruct(weights, bf16),
        ],
        scratch_shapes=[
            pltpu.VMEM((full_rows + 1, wide, lanes), f32),
            pltpu.VMEM((2, full_rows * pitch, span * lanes), bf16),
            pltpu.VMEM((2, full_rows * pitch, span * lanes), bf16),
            pltpu.VMEM((mid_rows * pitch, lanes), f32),
            pltpu.VMEM((lanes, lanes), bf16),
            pltpu.VMEM((lanes, lanes), bf16),
        ],
        cost_estimate=pl.CostEstimate(
            flops=6 * span * span * lanes * lanes * mid_rows * pitch,
            bytes_accessed=12 * lag_blocks.size,
            transcendentals=0,
        ),
        compiler_params=pltpu.CompilerParams(vmem_limit_bytes=32 * 1024 * 1024),
        name="first_sweep",
    )(source, inverse, lag_blocks)


def second_sweep_kernel(
    sizes,
    second_ref,
    source_ref,
    inverse_ref,
    w_high,
    w_low,
    adjoint_ref,
    *rest,
):
    rows, cols, span, peers = sizes
    sends = rest[: peers // 2]
    x_high, x_low, acc, turned, e_high, e_low = rest[peers // 2 :]
    reach = span // 2
    mid_rows = rows + 2 * reach
    own = rows * cols
    lanes = source_ref.shape[-1]
    width = lanes // 2

    store_inverse(inverse_ref, e_high, e_low)

    step_rows = largest_divisor(mid_rows, 3)

    @pl.loop(0, mid_rows // step_rows)
    def _(s):
        for b in range(span):
            at = pl.ds(s * step_rows, step_rows)
            value = second_ref[at, pl.ds(b, cols), :].reshape(step_rows * cols, lanes)
            high, low = split(value)
            to = pl.ds(pl.multiple_of(s * step_rows * cols, cols), step_rows * cols)
            x_high[to, b * lanes : (b + 1) * lanes] = high
            x_low[to, b * lanes : (b + 1) * lanes] = low

    acc[...] = jnp.zeros_like(acc)

    def one_lag(a):
        at = pl.ds(pl.multiple_of(a * cols, cols), own)
        return products(x_high[at, :], x_low[at, :], w_high[a], w_low[a])

    acc[...] = functools.reduce(lambda left, right: left + right, map(one_lag, range(span)))

    centre = second_ref[reach : reach + rows, pl.ds(reach, cols), :].reshape(own, lanes)
    source = source_ref[...].reshape(own, lanes)
    value = centre + dot3(split(source - centre - acc[...]), (e_high[...], e_low[...]))
    adjoint_ref[...] = value.reshape(adjoint_ref.shape)
    turned[...] = value.T

    share = width // peers
    me = lax.axis_index("row")
    parity = me % 2
    for k in range(peers // 2):
        base = 2 * chip_along_z(me // 2, k, peers // 2)
        for n, peer in enumerate((base + parity, base + 1 - parity)):
            for part in range(2):
                at = pl.multiple_of(part * width + peer * share, share)
                sends[k][n, part * share : (part + 1) * share, :] = turned[pl.ds(at, share), :]


def second_sweep(second, source, inverse, high, low, peers):
    span = high.shape[0]
    rows, cols, lanes = source.shape
    mid_rows = second.shape[0]
    share = lanes // 2 // peers
    vmem = pl.BlockSpec(memory_space=pltpu.VMEM)
    send = jax.ShapeDtypeStruct((2, 2 * share, rows * cols), f32)
    out = pl.pallas_call(
        functools.partial(second_sweep_kernel, (rows, cols, span, peers)),
        in_specs=[vmem] * 5,
        out_specs=[vmem] * (1 + peers // 2),
        out_shape=[jax.ShapeDtypeStruct((rows, cols, lanes), f32)] + [send] * (peers // 2),
        scratch_shapes=[
            pltpu.VMEM((mid_rows * cols, span * lanes), bf16),
            pltpu.VMEM((mid_rows * cols, span * lanes), bf16),
            pltpu.VMEM((rows * cols, lanes), f32),
            pltpu.VMEM((lanes, rows * cols), f32),
            pltpu.VMEM((lanes, lanes), bf16),
            pltpu.VMEM((lanes, lanes), bf16),
        ],
        cost_estimate=pl.CostEstimate(
            flops=6 * span * span * lanes * lanes * rows * cols,
            bytes_accessed=4 * high.size,
            transcendentals=0,
        ),
        compiler_params=pltpu.CompilerParams(vmem_limit_bytes=18 * 1024 * 1024),
        name="second_sweep",
    )(second, source, inverse, high, low)
    return out[0], out[1:]


def tiles_of(k, peers):
    me = lax.axis_index("row")
    parity = me % 2
    base = 2 * chip_along_z(me // 2, -k, peers // 2)
    return base + parity, base + 1 - parity


def spread_kernel(sizes, places, filled, *refs):
    rows, cols, span, peers = sizes
    count = len(places)
    sources = refs[:count]
    s_high, s_low, stage, sems = refs[count + filled :]
    own = rows * cols
    width = stage.shape[-1]
    copies = []
    at = 0
    for source, place in zip(sources, places):
        for n, (k, twin) in enumerate(place):
            piece = source.at[n] if len(source.shape) == 4 else source
            copies.append((pltpu.make_async_copy(piece, stage.at[at], sems.at[at]), tiles_of(k, peers)[twin]))
            copies[-1][0].start()
            at += 1

    for at, (copy, tile) in enumerate(copies):
        copy.wait()

        @pl.loop(0, rows)
        def _(i):
            to = pl.ds(pl.multiple_of(tile * own + i * cols, cols), cols)
            for b in range(span):
                for h in range(2):
                    start = i * (cols + span - 1) + span - 1 - b
                    high, low = split(stage[at, h, pl.ds(start, cols), :])
                    s_high[b, to, h * width : (h + 1) * width] = high
                    s_low[b, to, h * width : (h + 1) * width] = low


def spread(placed, rows, cols, span, peers, filled=()):
    sources, places = zip(*placed)
    piece = sources[0].shape[-3:]
    vmem = pl.BlockSpec(memory_space=pltpu.VMEM)
    hbm = pl.BlockSpec(memory_space=pltpu.HBM)
    out = jax.ShapeDtypeStruct((span, peers * rows * cols, 2 * piece[-1]), bf16)
    count = sum(len(place) for place in places)
    return pl.pallas_call(
        functools.partial(spread_kernel, (rows, cols, span, peers), places, len(filled)),
        in_specs=[hbm] * len(sources) + [vmem] * len(filled),
        out_specs=[vmem, vmem],
        out_shape=[out, out],
        input_output_aliases={len(sources) + n: n for n in range(len(filled))},
        scratch_shapes=[
            pltpu.VMEM((count,) + piece, f32),
            pltpu.SemaphoreType.DMA((count,)),
        ],
        cost_estimate=pl.CostEstimate(
            flops=0, bytes_accessed=4 * count * math.prod(piece), transcendentals=0
        ),
        compiler_params=pltpu.CompilerParams(vmem_limit_bytes=30 * 1024 * 1024),
        name="spread",
    )(*sources, *filled)


def correlate_kernel(sizes, lags, factor, *refs):
    rows, cols, span, peers = sizes
    half_peers = peers // 2
    shares = refs[:half_peers]
    twin_shares_ref, s_high, s_low, mine_ref, other_ref = refs[half_peers : half_peers + 5]
    placed, flat, l_high, l_low = refs[half_peers + 5 :]
    reach = span // 2
    own = rows * cols
    double = shares[0].shape[1]
    share = double // 2
    width = s_high.shape[-1] // 2

    for k in range(half_peers):
        tile, twin = tiles_of(k, peers)
        placed[tile] = shares[k][0]
        placed[twin] = twin_shares_ref[k]

    total = peers * own
    side = round_up(reach * cols, 128)
    flat[:, :side] = jnp.zeros((double, side), f32)
    flat[:, side + total :] = jnp.zeros((double, side), f32)
    for tile in range(peers):
        flat[:, side + tile * own : side + (tile + 1) * own] = placed[tile]

    @pl.loop(0, 2)
    def _(part):
        rows_at = pl.ds(pl.multiple_of(part * share, 8), share)
        for a in range(span):
            start = side + (a - reach) * cols
            high, low = split(flat[rows_at, start : start + total])
            l_high[a, part] = high
            l_low[a, part] = low

    half = share // 2
    upper = lax.axis_index("col") % 2 == 1
    first_lag, count = lags

    def one_lag(n):
        b = first_lag + n
        left = tuple(ref[...].reshape(span * double, total) for ref in (l_high, l_low))
        product = dot3(left, (s_high[b], s_low[b])) * factor
        for a in range(span):
            top = product[a * double : a * double + share]
            bottom = product[a * double + share : (a + 1) * double]
            real = top[:, :width] + bottom[:, width:]
            imag = bottom[:, :width] - top[:, width:]
            for c, value in enumerate((real, imag)):
                mine_ref[a, n, c] = jnp.where(upper, value[half:], value[:half])
                other_ref[a, n, c] = jnp.where(upper, value[:half], value[half:])

    for n in range(count):
        one_lag(n)


def correlate(shares, twin_shares, s_high, s_low, lags, rows, cols, factor):
    peers = 2 * len(shares)
    span, total, lanes = s_high.shape
    reach = span // 2
    double, own = twin_shares.shape[1:]
    share = double // 2
    side = round_up(reach * cols, 128)
    vmem = pl.BlockSpec(memory_space=pltpu.VMEM)
    out = jax.ShapeDtypeStruct((span, lags[1], 2, share // 2, lanes // 2), f32)
    return pl.pallas_call(
        functools.partial(correlate_kernel, (rows, cols, span, peers), lags, factor),
        in_specs=[vmem] * (peers // 2 + 3),
        out_specs=[vmem, vmem],
        out_shape=[out, out],
        scratch_shapes=[
            pltpu.VMEM((peers, double, own), f32),
            pltpu.VMEM((double, total + 2 * side), f32),
            pltpu.VMEM((span, 2, share, total), bf16),
            pltpu.VMEM((span, 2, share, total), bf16),
        ],
        cost_estimate=pl.CostEstimate(
            flops=6 * span * double * total * lags[1] * lanes if lags[0] == 0 else 1,
            bytes_accessed=8 * out.size if lags[0] == 0 else 1,
            transcendentals=0,
        ),
        compiler_params=pltpu.CompilerParams(vmem_limit_bytes=17 * 1024 * 1024),
        name="correlate",
    )(*shares, twin_shares, s_high, s_low)


def parts_first_kernel(field_ref, out_ref):
    for part in range(2):
        out_ref[part] = field_ref[:, pl.ds(part, out_ref.shape[2], 2), :]


def parts_first(field):
    rows, cols, parts, width = field.shape
    vmem = pl.BlockSpec(memory_space=pltpu.VMEM)
    return pl.pallas_call(
        parts_first_kernel,
        in_specs=[vmem],
        out_specs=vmem,
        out_shape=jax.ShapeDtypeStruct((parts, rows, cols, width), f32),
        cost_estimate=pl.CostEstimate(flops=0, bytes_accessed=8 * field.size, transcendentals=0),
        compiler_params=pltpu.CompilerParams(vmem_limit_bytes=4 * 1024 * 1024),
        name="parts_first",
    )(field.reshape(rows, cols * parts, width))


def swap(value, axis, first):
    pairs = []
    for low in range(first, lax.axis_size(axis) - 1, 2):
        pairs += [(low, low + 1), (low + 1, low)]
    if not pairs:
        return jnp.zeros_like(value)
    return lax.ppermute(value, axis, pairs)


def shifted(value, axis, shift):
    peers = lax.axis_size(axis)
    if shift % peers == 0:
        return value
    return lax.ppermute(value, axis, [(i, (i + shift) % peers) for i in range(peers)])


def edges(initial, last, axis):
    even = lax.axis_index(axis) % 2 == 0
    shape = initial.shape
    initial, last = (value.reshape(shape[0], -1, shape[-1]) for value in (initial, last))
    outer = swap(jnp.where(even, initial, last), axis, 1).reshape(shape)
    inner = swap(jnp.where(even, last, initial), axis, 0).reshape(shape)
    return jnp.where(even, outer, inner), jnp.where(even, inner, outer), inner


def extended(value, axis, dim, width):
    length = value.shape[dim]
    initial = lax.slice_in_dim(value, 0, width, axis=dim)
    last = lax.slice_in_dim(value, length - width, length, axis=dim)
    before, after, inner = edges(initial, last, axis)
    return jnp.concatenate([before, value, after], axis=dim), inner


def on_device(adjoint_source, saved_currents, lag_blocks, element_inverse):
    rows, cols, parts, width = adjoint_source.shape
    span = lag_blocks.shape[0]
    reach = span // 2
    halo = SWEEPS * reach
    peers = lax.axis_size("row")

    source = adjoint_source.transpose(2, 0, 1, 3)
    saved = parts_first(saved_currents)
    source, _ = extended(source, "row", 1, halo)
    saved, _ = extended(saved, "col", 2, reach)
    saved = lax.optimization_barrier((saved, source))[0]
    source, inner = extended(source, "col", 2, halo)
    wide = round_up(cols + 2 * halo, 8)
    source = jnp.pad(source, ((0, 0), (0, 0), (0, wide - cols - 2 * halo), (0, 0)))

    saved = saved.reshape(parts, -1, width)
    pieces = {0: saved}
    behind = lax.optimization_barrier((saved, inner))[0]
    for k in sorted(range(1, peers // 2), key=lambda k: min(k, peers // 2 - k)):
        near = k in (1, peers // 2 - 1)
        pieces[k] = shifted(saved if near else behind, "row", 2 * k)
    pieces = [pieces[k] for k in range(peers // 2)]
    own_twin = swap(saved, "row", 0)

    second, own_source, high, low = first_sweep(source, element_inverse, lag_blocks, rows, cols)
    second, own_twin, early = lax.optimization_barrier((second, own_twin, jnp.stack([pieces[1], pieces[-1]])))
    early_twins = swap(early, "row", 0)
    adjoint, sends = second_sweep(second, own_source, element_inverse, high, low, peers)
    adjoint = adjoint.reshape(adjoint_source.shape)
    *late, sends = lax.optimization_barrier((*pieces[2:-1], sends))
    late_twins = swap(jnp.stack(late), "row", 0)
    shares = [shifted(send, "row", 2 * k) for k, send in enumerate(sends)]
    twin_shares = swap(jnp.stack([received[1] for received in shares]), "row", 0)

    last = peers // 2 - 1
    arrived = [(piece, ((k, 0),)) for k, piece in enumerate(pieces)]
    arrived += [(own_twin, ((0, 1),)), (early_twins, ((1, 1), (last, 1)))]
    spreads = spread(arrived, rows, cols, span, peers)
    late = [(late_twins, tuple((k, 1) for k in range(2, last)))]
    s_high, s_low = spread(late, rows, cols, span, peers, tuple(spreads))

    elements = rows * peers * cols * lax.axis_size("col")
    factor = -1.0 / math.sqrt(elements)
    even = lax.axis_index("col") % 2 == 0
    totals = []
    for lags in ((0, span),):
        mine, other = correlate(shares, twin_shares, s_high, s_low, lags, rows, cols, factor)
        mine = mine + swap(other, "col", 0)
        mine, adjoint = lax.optimization_barrier((mine, adjoint))
        for piece in (mine[: span // 2 + 1], mine[span // 2 + 1 :]):
            total = piece
            for k in range(2, lax.axis_size("col"), 2):
                total = total + shifted(piece, "col", k)
            totals.append(total)
    twins = [swap(total, "col", 0) for total in totals]
    total, twin = jnp.concatenate(totals, axis=0), jnp.concatenate(twins, axis=0)
    lag_grad = jnp.concatenate(
        [jnp.where(even, total, twin), jnp.where(even, twin, total)], axis=3
    )
    return (adjoint, lag_grad)


def solution(mesh):
    return jax.shard_map(
        on_device,
        mesh=mesh,
        in_specs=(P("row", "col", None, None), P("row", "col", None, None), P(), P()),
        out_specs=(P("row", "col", None, None), P(None, None, None, "row", None)),
        check_vma=False,
    )
```

```python
import functools
import math

import jax
import jax.numpy as jnp
from jax import lax
from jax.experimental import pallas as pl
from jax.experimental.pallas import tpu as pltpu
from jax.sharding import PartitionSpec as P

SWEEPS = 2

f32 = jnp.float32
bf16 = jnp.bfloat16


def split(value):
    high = value.astype(bf16)
    return high, (value - high.astype(f32)).astype(bf16)


def dot(left, right):
    return jnp.dot(left, right, preferred_element_type=f32)


def dot3(left, right):
    (left_high, left_low), (right_high, right_low) = left, right
    return dot(left_high, right_high) + dot(left_low, right_high) + dot(left_high, right_low)


def largest_divisor(count, most):
    return max(n for n in range(1, most + 1) if count % n == 0)


def round_up(count, unit):
    return (count + unit - 1) // unit * unit


def chip_along_z(z, shift, count):
    return (z + shift + count) % count


def store_block(ref, index, real, imag):
    width = real.shape[0]
    low, high = slice(0, width), slice(width, 2 * width)
    ref[index + (low, low)] = real
    ref[index + (low, high)] = -imag
    ref[index + (high, low)] = imag
    ref[index + (high, high)] = real


def inside(first_row, rows, cols, pitch, margin, tile_rows, tile_cols):
    at = lax.broadcasted_iota(jnp.int32, (rows * pitch, 1), 0)
    i = at // pitch
    j = at - i * pitch
    row = i + (first_row + lax.axis_index("row") * tile_rows - margin)
    col = j + (lax.axis_index("col") * tile_cols - margin)
    row_ok = (row >= 0) & (row < tile_rows * lax.axis_size("row"))
    col_ok = (col >= 0) & (col < tile_cols * lax.axis_size("col"))
    return row_ok & col_ok & (j < cols)


def store_inverse(inverse_ref, high_ref, low_ref):
    real_high, real_low = split(inverse_ref[0])
    imag_high, imag_low = split(inverse_ref[1])
    store_block(high_ref, (), real_high, imag_high)
    store_block(low_ref, (), real_low, imag_low)


def products(high, low, weight_high, weight_low):
    lanes = weight_high.shape[-1]
    weight_high = weight_high.reshape(-1, lanes)
    weight_low = weight_low.reshape(-1, lanes)
    return dot(high, weight_high) + dot(low, weight_high) + dot(high, weight_low)


def first_sweep_kernel(
    sizes,
    source_ref,
    inverse_ref,
    blocks_ref,
    second_ref,
    own_source_ref,
    w_high,
    w_low,
    first,
    x_high,
    x_low,
    acc,
    e_high,
    e_low,
):
    rows, cols, span, pitch, wide = sizes
    reach = span // 2
    mid_rows, mid_cols = rows + 2 * reach, cols + 2 * reach
    full_rows = rows + 4 * reach
    lanes = 2 * source_ref.shape[-1]

    def source_at(i, j):
        return jnp.concatenate([source_ref[0, i, j, :], source_ref[1, i, j, :]], axis=-1)

    store_inverse(inverse_ref, e_high, e_low)

    def invert(value):
        return dot3(split(value), (e_high[...], e_low[...]))

    own_source_ref[...] = source_at(pl.ds(2 * reach, rows), pl.ds(2 * reach, cols))

    step_rows = largest_divisor(full_rows, 12)

    @pl.loop(0, full_rows // step_rows)
    def _(s):
        at = pl.ds(s * step_rows, step_rows)
        piece = source_at(at, pl.ds(0, wide)).reshape(step_rows * wide, lanes)
        first[at] = invert(piece).reshape(step_rows, wide, lanes)

    first[full_rows] = jnp.zeros((wide, lanes), f32)

    step_rows = 2 * largest_divisor(full_rows // 2, 3)

    @pl.loop(0, full_rows // step_rows)
    def _(s):
        for odd in range(2):
            for b in range(span):
                value = first[pl.ds(s * step_rows + odd, step_rows), pl.ds(b, pitch), :]
                count = step_rows * pitch
                high, low = split(value.reshape(count, lanes))
                to = pl.ds(pl.multiple_of(s * count, 2 * pitch), count)
                x_high[odd, to, b * lanes : (b + 1) * lanes] = high
                x_low[odd, to, b * lanes : (b + 1) * lanes] = low

    acc[...] = jnp.zeros_like(acc)

    def one_lag(a):
        for b in range(span):
            real_high, real_low = split(blocks_ref[a, b, 0])
            imag_high, imag_low = split(blocks_ref[a, b, 1])
            store_block(w_high, (a, b), real_high, imag_high)
            store_block(w_low, (a, b), real_low, imag_low)

        at = pl.ds(pl.multiple_of((a // 2) * 2 * pitch, 2 * pitch), mid_rows * pitch)
        return products(x_high[a % 2, at, :], x_low[a % 2, at, :], w_high[a], w_low[a])

    @pl.loop(0, span // 2)
    def _(pair):
        acc[...] += one_lag(2 * pair) + one_lag(2 * pair + 1)

    if span % 2:
        acc[...] += one_lag(span - 1)

    step_rows = largest_divisor(mid_rows, 18)

    @pl.loop(0, mid_rows // step_rows)
    def _(s):
        at = pl.ds(s * step_rows + reach, step_rows)
        count = step_rows * pitch
        flat = pl.ds(pl.multiple_of(s * count, 8), count)
        centre = first[at, pl.ds(reach, pitch), :].reshape(count, lanes)
        source = source_at(at, pl.ds(reach, pitch)).reshape(count, lanes)
        value = centre + invert(source - centre - acc[flat, :])
        mask = inside(s * step_rows, step_rows, mid_cols, pitch, reach, rows, cols)
        value = jnp.where(mask, value, 0.0)
        second_ref[pl.ds(s * step_rows, step_rows)] = value.reshape(step_rows, pitch, lanes)


def first_sweep(source, inverse, lag_blocks, rows, cols):
    span = lag_blocks.shape[0]
    reach = span // 2
    lanes = 2 * source.shape[-1]
    wide = source.shape[2]
    pitch = round_up(cols + 2 * reach, 8)
    full_rows, mid_rows = rows + 4 * reach, rows + 2 * reach
    vmem = pl.BlockSpec(memory_space=pltpu.VMEM)
    weights = (span, span, lanes, lanes)
    return pl.pallas_call(
        functools.partial(first_sweep_kernel, (rows, cols, span, pitch, wide)),
        in_specs=[vmem] * 3,
        out_specs=[vmem] * 4,
        out_shape=[
            jax.ShapeDtypeStruct((mid_rows, pitch, lanes), f32),
            jax.ShapeDtypeStruct((rows, cols, lanes), f32),
            jax.ShapeDtypeStruct(weights, bf16),
            jax.ShapeDtypeStruct(weights, bf16),
        ],
        scratch_shapes=[
            pltpu.VMEM((full_rows + 1, wide, lanes), f32),
            pltpu.VMEM((2, full_rows * pitch, span * lanes), bf16),
            pltpu.VMEM((2, full_rows * pitch, span * lanes), bf16),
            pltpu.VMEM((mid_rows * pitch, lanes), f32),
            pltpu.VMEM((lanes, lanes), bf16),
            pltpu.VMEM((lanes, lanes), bf16),
        ],
        cost_estimate=pl.CostEstimate(
            flops=6 * span * span * lanes * lanes * mid_rows * pitch,
            bytes_accessed=12 * lag_blocks.size,
            transcendentals=0,
        ),
        compiler_params=pltpu.CompilerParams(vmem_limit_bytes=32 * 1024 * 1024),
        name="first_sweep",
    )(source, inverse, lag_blocks)


def second_sweep_kernel(
    sizes,
    second_ref,
    source_ref,
    inverse_ref,
    w_high,
    w_low,
    adjoint_ref,
    *rest,
):
    rows, cols, span, peers = sizes
    sends = rest[: peers // 2]
    x_high, x_low, acc, turned, e_high, e_low = rest[peers // 2 :]
    reach = span // 2
    mid_rows = rows + 2 * reach
    own = rows * cols
    lanes = source_ref.shape[-1]
    width = lanes // 2

    store_inverse(inverse_ref, e_high, e_low)

    step_rows = largest_divisor(mid_rows, 3)

    @pl.loop(0, mid_rows // step_rows)
    def _(s):
        for b in range(span):
            at = pl.ds(s * step_rows, step_rows)
            value = second_ref[at, pl.ds(b, cols), :].reshape(step_rows * cols, lanes)
            high, low = split(value)
            to = pl.ds(pl.multiple_of(s * step_rows * cols, cols), step_rows * cols)
            x_high[to, b * lanes : (b + 1) * lanes] = high
            x_low[to, b * lanes : (b + 1) * lanes] = low

    acc[...] = jnp.zeros_like(acc)

    def one_lag(a):
        at = pl.ds(pl.multiple_of(a * cols, cols), own)
        return products(x_high[at, :], x_low[at, :], w_high[a], w_low[a])

    acc[...] = functools.reduce(lambda left, right: left + right, map(one_lag, range(span)))

    centre = second_ref[reach : reach + rows, pl.ds(reach, cols), :].reshape(own, lanes)
    source = source_ref[...].reshape(own, lanes)
    value = centre + dot3(split(source - centre - acc[...]), (e_high[...], e_low[...]))
    adjoint_ref[...] = value.reshape(adjoint_ref.shape)
    turned[...] = value.T

    share = width // peers
    me = lax.axis_index("row")
    parity = me % 2
    for k in range(peers // 2):
        base = 2 * chip_along_z(me // 2, k, peers // 2)
        for n, peer in enumerate((base + parity, base + 1 - parity)):
            for part in range(2):
                at = pl.multiple_of(part * width + peer * share, share)
                sends[k][n, part * share : (part + 1) * share, :] = turned[pl.ds(at, share), :]


def second_sweep(second, source, inverse, high, low, peers):
    span = high.shape[0]
    rows, cols, lanes = source.shape
    mid_rows = second.shape[0]
    share = lanes // 2 // peers
    vmem = pl.BlockSpec(memory_space=pltpu.VMEM)
    send = jax.ShapeDtypeStruct((2, 2 * share, rows * cols), f32)
    out = pl.pallas_call(
        functools.partial(second_sweep_kernel, (rows, cols, span, peers)),
        in_specs=[vmem] * 5,
        out_specs=[vmem] * (1 + peers // 2),
        out_shape=[jax.ShapeDtypeStruct((rows, cols, lanes), f32)] + [send] * (peers // 2),
        scratch_shapes=[
            pltpu.VMEM((mid_rows * cols, span * lanes), bf16),
            pltpu.VMEM((mid_rows * cols, span * lanes), bf16),
            pltpu.VMEM((rows * cols, lanes), f32),
            pltpu.VMEM((lanes, rows * cols), f32),
            pltpu.VMEM((lanes, lanes), bf16),
            pltpu.VMEM((lanes, lanes), bf16),
        ],
        cost_estimate=pl.CostEstimate(
            flops=6 * span * span * lanes * lanes * rows * cols,
            bytes_accessed=4 * high.size,
            transcendentals=0,
        ),
        compiler_params=pltpu.CompilerParams(vmem_limit_bytes=18 * 1024 * 1024),
        name="second_sweep",
    )(second, source, inverse, high, low)
    return out[0], out[1:]


def tiles_of(k, peers):
    me = lax.axis_index("row")
    parity = me % 2
    base = 2 * chip_along_z(me // 2, -k, peers // 2)
    return base + parity, base + 1 - parity


def spread_kernel(sizes, places, filled, *refs):
    rows, cols, span, peers = sizes
    count = len(places)
    sources = refs[:count]
    s_high, s_low, stage, sems = refs[count + filled :]
    own = rows * cols
    width = stage.shape[-1]
    copies = []
    at = 0
    for source, place in zip(sources, places):
        for n, (k, twin) in enumerate(place):
            piece = source.at[n] if len(source.shape) == 4 else source
            copies.append((pltpu.make_async_copy(piece, stage.at[at], sems.at[at]), tiles_of(k, peers)[twin]))
            copies[-1][0].start()
            at += 1

    for at, (copy, tile) in enumerate(copies):
        copy.wait()

        @pl.loop(0, rows)
        def _(i):
            to = pl.ds(pl.multiple_of(tile * own + i * cols, cols), cols)
            for b in range(span):
                for h in range(2):
                    start = i * (cols + span - 1) + span - 1 - b
                    high, low = split(stage[at, h, pl.ds(start, cols), :])
                    s_high[b, to, h * width : (h + 1) * width] = high
                    s_low[b, to, h * width : (h + 1) * width] = low


def spread(placed, rows, cols, span, peers, filled=()):
    sources, places = zip(*placed)
    piece = sources[0].shape[-3:]
    vmem = pl.BlockSpec(memory_space=pltpu.VMEM)
    hbm = pl.BlockSpec(memory_space=pltpu.HBM)
    out = jax.ShapeDtypeStruct((span, peers * rows * cols, 2 * piece[-1]), bf16)
    count = sum(len(place) for place in places)
    return pl.pallas_call(
        functools.partial(spread_kernel, (rows, cols, span, peers), places, len(filled)),
        in_specs=[hbm] * len(sources) + [vmem] * len(filled),
        out_specs=[vmem, vmem],
        out_shape=[out, out],
        input_output_aliases={len(sources) + n: n for n in range(len(filled))},
        scratch_shapes=[
            pltpu.VMEM((count,) + piece, f32),
            pltpu.SemaphoreType.DMA((count,)),
        ],
        cost_estimate=pl.CostEstimate(
            flops=0, bytes_accessed=4 * count * math.prod(piece), transcendentals=0
        ),
        compiler_params=pltpu.CompilerParams(vmem_limit_bytes=30 * 1024 * 1024),
        name="spread",
    )(*sources, *filled)


def correlate_kernel(sizes, lags, factor, *refs):
    rows, cols, span, peers = sizes
    half_peers = peers // 2
    shares = refs[:half_peers]
    twin_shares_ref, s_high, s_low, mine_ref, other_ref = refs[half_peers : half_peers + 5]
    placed, flat, l_high, l_low = refs[half_peers + 5 :]
    reach = span // 2
    own = rows * cols
    double = shares[0].shape[1]
    share = double // 2
    width = s_high.shape[-1] // 2

    for k in range(half_peers):
        tile, twin = tiles_of(k, peers)
        placed[tile] = shares[k][0]
        placed[twin] = twin_shares_ref[k]

    total = peers * own
    side = round_up(reach * cols, 128)
    flat[:, :side] = jnp.zeros((double, side), f32)
    flat[:, side + total :] = jnp.zeros((double, side), f32)
    for tile in range(peers):
        flat[:, side + tile * own : side + (tile + 1) * own] = placed[tile]

    @pl.loop(0, 2)
    def _(part):
        rows_at = pl.ds(pl.multiple_of(part * share, 8), share)
        for a in range(span):
            start = side + (a - reach) * cols
            high, low = split(flat[rows_at, start : start + total])
            l_high[a, part] = high
            l_low[a, part] = low

    half = share // 2
    upper = lax.axis_index("col") % 2 == 1
    first_lag, count = lags

    def one_lag(n):
        b = first_lag + n
        left = tuple(ref[...].reshape(span * double, total) for ref in (l_high, l_low))
        product = dot3(left, (s_high[b], s_low[b])) * factor
        for a in range(span):
            top = product[a * double : a * double + share]
            bottom = product[a * double + share : (a + 1) * double]
            real = top[:, :width] + bottom[:, width:]
            imag = bottom[:, :width] - top[:, width:]
            for c, value in enumerate((real, imag)):
                mine_ref[a, n, c] = jnp.where(upper, value[half:], value[:half])
                other_ref[a, n, c] = jnp.where(upper, value[:half], value[half:])

    for n in range(count):
        one_lag(n)


def correlate(shares, twin_shares, s_high, s_low, lags, rows, cols, factor):
    peers = 2 * len(shares)
    span, total, lanes = s_high.shape
    reach = span // 2
    double, own = twin_shares.shape[1:]
    share = double // 2
    side = round_up(reach * cols, 128)
    vmem = pl.BlockSpec(memory_space=pltpu.VMEM)
    out = jax.ShapeDtypeStruct((span, lags[1], 2, share // 2, lanes // 2), f32)
    return pl.pallas_call(
        functools.partial(correlate_kernel, (rows, cols, span, peers), lags, factor),
        in_specs=[vmem] * (peers // 2 + 3),
        out_specs=[vmem, vmem],
        out_shape=[out, out],
        scratch_shapes=[
            pltpu.VMEM((peers, double, own), f32),
            pltpu.VMEM((double, total + 2 * side), f32),
            pltpu.VMEM((span, 2, share, total), bf16),
            pltpu.VMEM((span, 2, share, total), bf16),
        ],
        cost_estimate=pl.CostEstimate(
            flops=6 * span * double * total * lags[1] * lanes if lags[0] == 0 else 1,
            bytes_accessed=8 * out.size if lags[0] == 0 else 1,
            transcendentals=0,
        ),
        compiler_params=pltpu.CompilerParams(vmem_limit_bytes=17 * 1024 * 1024),
        name="correlate",
    )(*shares, twin_shares, s_high, s_low)


def parts_first_kernel(field_ref, out_ref):
    for part in range(2):
        out_ref[part] = field_ref[:, pl.ds(part, out_ref.shape[2], 2), :]


def parts_first(field):
    rows, cols, parts, width = field.shape
    vmem = pl.BlockSpec(memory_space=pltpu.VMEM)
    return pl.pallas_call(
        parts_first_kernel,
        in_specs=[vmem],
        out_specs=vmem,
        out_shape=jax.ShapeDtypeStruct((parts, rows, cols, width), f32),
        cost_estimate=pl.CostEstimate(flops=0, bytes_accessed=8 * field.size, transcendentals=0),
        compiler_params=pltpu.CompilerParams(vmem_limit_bytes=4 * 1024 * 1024),
        name="parts_first",
    )(field.reshape(rows, cols * parts, width))


def swap(value, axis, first):
    pairs = []
    for low in range(first, lax.axis_size(axis) - 1, 2):
        pairs += [(low, low + 1), (low + 1, low)]
    if not pairs:
        return jnp.zeros_like(value)
    return lax.ppermute(value, axis, pairs)


def shifted(value, axis, shift):
    peers = lax.axis_size(axis)
    if shift % peers == 0:
        return value
    return lax.ppermute(value, axis, [(i, (i + shift) % peers) for i in range(peers)])


def edges(initial, last, axis):
    even = lax.axis_index(axis) % 2 == 0
    shape = initial.shape
    initial, last = (value.reshape(shape[0], -1, shape[-1]) for value in (initial, last))
    outer = swap(jnp.where(even, initial, last), axis, 1).reshape(shape)
    inner = swap(jnp.where(even, last, initial), axis, 0).reshape(shape)
    return jnp.where(even, outer, inner), jnp.where(even, inner, outer), inner


def extended(value, axis, dim, width):
    length = value.shape[dim]
    initial = lax.slice_in_dim(value, 0, width, axis=dim)
    last = lax.slice_in_dim(value, length - width, length, axis=dim)
    before, after, inner = edges(initial, last, axis)
    return jnp.concatenate([before, value, after], axis=dim), inner


def on_device(adjoint_source, saved_currents, lag_blocks, element_inverse):
    rows, cols, parts, width = adjoint_source.shape
    span = lag_blocks.shape[0]
    reach = span // 2
    halo = SWEEPS * reach
    peers = lax.axis_size("row")

    source = adjoint_source.transpose(2, 0, 1, 3)
    saved = parts_first(saved_currents)
    source, _ = extended(source, "row", 1, halo)
    saved, _ = extended(saved, "col", 2, reach)
    saved = lax.optimization_barrier((saved, source))[0]
    source, inner = extended(source, "col", 2, halo)
    wide = round_up(cols + 2 * halo, 8)
    source = jnp.pad(source, ((0, 0), (0, 0), (0, wide - cols - 2 * halo), (0, 0)))

    saved = saved.reshape(parts, -1, width)
    pieces = {0: saved}
    behind = lax.optimization_barrier((saved, inner))[0]
    for k in sorted(range(1, peers // 2), key=lambda k: min(k, peers // 2 - k)):
        near = k in (1, peers // 2 - 1)
        pieces[k] = shifted(saved if near else behind, "row", 2 * k)
    pieces = [pieces[k] for k in range(peers // 2)]
    own_twin = swap(saved, "row", 0)

    second, own_source, high, low = first_sweep(source, element_inverse, lag_blocks, rows, cols)
    second, own_twin, early = lax.optimization_barrier((second, own_twin, jnp.stack([pieces[1], pieces[-1]])))
    early_twins = swap(early, "row", 0)
    adjoint, sends = second_sweep(second, own_source, element_inverse, high, low, peers)
    adjoint = adjoint.reshape(adjoint_source.shape)
    *late, sends = lax.optimization_barrier((*pieces[2:-1], sends))
    late_twins = swap(jnp.stack(late), "row", 0)
    shares = [shifted(send, "row", 2 * k) for k, send in enumerate(sends)]
    twin_shares = swap(jnp.stack([received[1] for received in shares]), "row", 0)

    last = peers // 2 - 1
    arrived = [(piece, ((k, 0),)) for k, piece in enumerate(pieces)]
    arrived += [(own_twin, ((0, 1),)), (early_twins, ((1, 1), (last, 1)))]
    spreads = spread(arrived, rows, cols, span, peers)
    late = [(late_twins, tuple((k, 1) for k in range(2, last)))]
    s_high, s_low = spread(late, rows, cols, span, peers, tuple(spreads))

    elements = rows * peers * cols * lax.axis_size("col")
    factor = -1.0 / math.sqrt(elements)
    even = lax.axis_index("col") % 2 == 0
    totals = []
    for lags in ((0, span),):
        mine, other = correlate(shares, twin_shares, s_high, s_low, lags, rows, cols, factor)
        mine = mine + swap(other, "col", 0)
        mine, adjoint = lax.optimization_barrier((mine, adjoint))
        for piece in (mine[: span - 2], mine[span - 2 :]):
            total = piece
            for k in range(2, lax.axis_size("col"), 2):
                total = total + shifted(piece, "col", k)
            totals.append(total)
    twins = [swap(total, "col", 0) for total in totals]
    total, twin = jnp.concatenate(totals, axis=0), jnp.concatenate(twins, axis=0)
    lag_grad = jnp.concatenate(
        [jnp.where(even, total, twin), jnp.where(even, twin, total)], axis=3
    )
    return (adjoint, lag_grad)


def solution(mesh):
    return jax.shard_map(
        on_device,
        mesh=mesh,
        in_specs=(P("row", "col", None, None), P("row", "col", None, None), P(), P()),
        out_specs=(P("row", "col", None, None), P(None, None, None, "row", None)),
        check_vma=False,
    )
```
